32 devices in a mesh: section: 2 (over x), tensor: 4 (over z), replica: 4 (over y, core).
Axes of the slice: x: 2, y: 2, z: 4, core: 2. Of those that a mesh axis runs over, the one named last changes fastest.
Arguments:
- state: bfloat16 [2, 4, 8192], P('section', None, 'replica'), may hold values from -6 to 6
- next_embed: bfloat16 [2, 4, 8192], P(None, None, 'replica'), may hold values from -6 to 6
- tenant: int32 [2, 4], replicated, may hold values from 0 to 399
- lengths: int32 [2, 4], P(None, 'replica'), may hold values from 1 to 64, 160 in all within a row
- gain: bfloat16 [2, 400, 8192], P('section', 'tensor', 'replica'), may hold values from 0.099609375 to 1.8984375
- bias: bfloat16 [2, 400, 8192], P('section', 'tensor', 'replica'), may hold values from -3 to 3
- wq: bfloat16 [2, 8192, 8192], P('section', 'replica', 'tensor'), may hold values from -0.0625 to 0.0625
- wo: bfloat16 [2, 8192, 8192], P('section', 'tensor', 'replica'), may hold values from -0.0625 to 0.0625
- keys: bfloat16 [2, 2, 4, 8, 64, 128], P('section', None, 'replica', None, 'tensor'), may hold values from -300 to 300
- values: bfloat16 [2, 2, 4, 8, 64, 128], P('section', None, 'replica', None, 'tensor'), may hold values from -6 to 6
Outputs:
- state_out: bfloat16 [2, 4, 8192], P('section', None, 'replica')
- emitted: bfloat16 [2, 4, 8192], P('section', None, 'replica')
The draws below stay inside these ranges and needn't reach their ends.
Inputs may be any that keep to these rules, and one draw needn't show every extreme that they name: Each entry lengths[m, r] is the length of one row's cache, between 1 and 64. The total is not per row: the 4 entries of one micro-batch m (the row lengths[m] of the array) add up to 160, and one row of every micro-batch has all 64 positions.
All inputs are finite; a program needn't handle non-finite values. No bound on the sum of `lengths` on one device may be relied on, other than what follows from the above.
Results may differ from the reference program's by a relative error of at most 0.02.
Values may be sent and summed in bfloat16 or wider, within the bound.
No kernel may reach another device: no remote copies, remote signals or barrier semaphores. Data moves between devices by JAX's collectives and lax.ppermute only.
A program may use at most 64 MiB of HBM per device.

```python
import math
import jax
import jax.numpy as jnp
import numpy as np
from jax import lax

D = 8192
HEADS = 64
KVH = 8
HD = 128
TENANTS = 400
LAYERS = 2
MBS = 2
ROWS_MB = 4
CTX = 64
HQ = 8192


def feature_scale(lowest, highest):
    place = jnp.arange(D).astype(jnp.float32) / (D - 1)
    return lowest * jnp.exp(place * jnp.log(highest / lowest))


def rising_rows(key, lowest, highest):
    shape = (MBS, ROWS_MB, D)
    base = jax.random.normal(key, shape, jnp.float32)
    return jnp.clip(base * feature_scale(lowest, highest)[None, None, :], -6.0, 6.0)


def draw_state(key, part):
    key = jax.random.fold_in(key, 21)
    return rising_rows(key, 0.3, 3.0).astype(jnp.bfloat16)


def draw_next_embed(key, part):
    key = jax.random.fold_in(key, 23)
    return rising_rows(key, 0.3, 3.0).astype(jnp.bfloat16)


def draw_keys(key, part):
    key = jax.random.fold_in(key, 11)
    shape = (LAYERS, MBS, ROWS_MB, KVH, CTX, HD)
    base = jnp.clip(jax.random.normal(key, shape, jnp.float32), -6.0, 6.0)
    return base.astype(jnp.bfloat16)


def place_ends(result, own_key, least, largest):
    extent = result.shape
    index_at = [jax.random.randint(jax.random.fold_in(own_key, axis), (), 0, extent[axis]) for axis in range(len(extent))]
    result = result.at[tuple(index_at)].set(least)
    longest = extent.index(max(extent))
    index_at[longest] = (index_at[longest] + 1) % extent[longest]
    return result.at[tuple(index_at)].set(largest)


def block_levels(key, extent, split, least, largest):
    level, own = 1.0, jax.random.fold_in(key, 6)
    for axis_at, blocks in split:
        steps = jnp.exp(jax.random.uniform(jax.random.fold_in(own, axis_at), (blocks,), jnp.float32, least / len(split), largest / len(split)))
        level = level * jnp.repeat(steps, extent[axis_at] // blocks).reshape([-1 if axis == axis_at else 1 for axis in range(len(extent))])
    return level


def rank_bounds(number_of, skew):
    weights = [(1 << 20) // math.isqrt(grade ** skew) + 1 for grade in range(1, number_of + 1)]
    deviation = 1 + sum(weights) // (1 << 30)
    return np.cumsum(np.array([max(1, weight // deviation) for weight in weights]))


def ranked(own_key, extent, number_of, slope):
    table = rank_bounds(number_of, slope)
    ticket = jax.random.randint(jax.random.fold_in(own_key, 1), extent, 0, int(table[number_of - 1]))
    standing = jnp.searchsorted(jnp.asarray(table, jnp.int32), ticket, side="right")
    return jax.random.permutation(jax.random.fold_in(own_key, 2), number_of)[standing].astype(jnp.int32)


def split_up(count, total, limit, skew):
    loads = [(1 << 20) // math.isqrt(standing ** skew) + 1 for standing in range(2, count + 1)]
    rest, given = total - limit - (count - 1), [1] * (count - 1)
    while rest > 0:
        candidates = [i for i in range(count - 1) if given[i] < limit]
        whole, left = sum([loads[i] for i in candidates]), rest
        for i in candidates:
            extra = min(limit - given[i], max(1, left * loads[i] // whole), rest)
            given[i] = given[i] + extra
            rest = rest - extra
    return np.array([limit] + given)


def ragged_sizes(key, count, total, limit, slope):
    if count == 2:
        one = jax.random.randint(key, (), max(1, total - limit), min(limit, total - 1) + 1)
        return jnp.stack([one, total - one])
    sizes = jnp.asarray(split_up(count, total, limit, slope), jnp.int32)
    couples = (count - 1) // 2
    source_of, receiver = sizes[1:1 + 2 * couples:2], sizes[2:2 + 2 * couples:2]
    margin = jnp.minimum(source_of - 1, limit - receiver)
    passed = jax.random.randint(jax.random.fold_in(key, 1), (couples,), 0, 1 << 20) % (margin + 1)
    sizes = sizes.at[1:1 + 2 * couples:2].set(source_of - passed).at[2:2 + 2 * couples:2].set(receiver + passed)
    return sizes[jax.random.permutation(jax.random.fold_in(key, 2), count)]


def scatter_about(stream_key, shape, deviation, reach, cuts=(), dtype=jnp.bfloat16):
    drawn = jax.random.normal(stream_key, shape, jnp.float32) * deviation
    if len(cuts) > 0:
        drawn = block_levels(stream_key, shape, cuts, -0.22, 0.18) * drawn
    return jnp.clip(drawn, min=-reach, max=reach).astype(dtype)


def setup_inputs(seed: int = 0) -> dict:
    splits = jax.random.split(jax.random.key(seed), 11)
    state = draw_state(jax.random.fold_in(splits[10], 71), 0)
    next_embed = draw_next_embed(jax.random.fold_in(splits[10], 71), 0)
    tenant = place_ends(ranked(splits[2], (MBS, ROWS_MB), TENANTS, 2), jax.random.fold_in(splits[2], 3), 0, TENANTS - 1).astype(jnp.int32)
    lengths = jax.vmap(lambda own: ragged_sizes(own, ROWS_MB, CTX + (ROWS_MB - 1) * (CTX // 2), CTX, 2))(jax.random.split(splits[3], MBS)).reshape((MBS, ROWS_MB)).astype(jnp.int32)
    gain = jnp.clip(1.0 + 0.18 * jax.random.normal(splits[4], (LAYERS, TENANTS, D), jnp.float32), 0.099609375, 1.8984375).astype(jnp.bfloat16)
    bias = scatter_about(splits[5], (LAYERS, TENANTS, D), 0.5, 3.0, ((0, 2), (1, 4), (2, 4)))
    wq = scatter_about(splits[6], (LAYERS, D, HQ), D ** -0.5, 0.0625, ((0, 2), (1, 4), (2, 4)))
    wo = scatter_about(splits[7], (LAYERS, HQ, D), HQ ** -0.5, 0.0625, ((0, 2), (1, 4), (2, 4)))
    keys = draw_keys(jax.random.fold_in(splits[10], 71), 0)
    values = scatter_about(splits[9], (LAYERS, MBS, ROWS_MB, KVH, CTX, HD), 1.0, 6.0, ((0, 2), (2, 4), (4, 4)))
    return {"state": state, "next_embed": next_embed, "tenant": tenant, "lengths": lengths, "gain": gain, "bias": bias, "wq": wq, "wo": wo, "keys": keys, "values": values}


def one_layer(h, gain_row, bias_row, wq_layer, wo_layer, keys_mb, values_mb, lengths_mb):
    hf = h.astype(jnp.float32)
    mean = lax.optimization_barrier(jnp.mean(hf, axis=-1, keepdims=True))
    var = lax.optimization_barrier(jnp.mean(hf * hf, axis=-1, keepdims=True)) - mean * mean
    normed = (hf - mean) * jax.lax.rsqrt(var + 1e-05) * gain_row.astype(jnp.float32) + bias_row.astype(jnp.float32)
    normed = normed.astype(jnp.bfloat16)
    query = jnp.dot(normed, wq_layer, preferred_element_type=jnp.float32).astype(jnp.bfloat16)
    rows = h.shape[0]
    grouped = query.reshape(rows, KVH, HEADS // KVH, HD).astype(jnp.float32)
    scores = jnp.einsum('rgjd,rgpd->rgjp', grouped, keys_mb.astype(jnp.float32)) / jnp.sqrt(jnp.float32(HD))
    valid = jnp.arange(CTX)[None, None, None, :] < lengths_mb[:, None, None, None]
    scores = jnp.where(valid, scores, -1e+30)
    top = lax.optimization_barrier(jnp.max(scores, axis=-1, keepdims=True))
    probs = jnp.exp(scores - top) * valid.astype(jnp.float32)
    weight = probs / lax.optimization_barrier(jnp.sum(probs, axis=-1, keepdims=True))
    att = jnp.einsum('rgjp,rgpd->rgjd', weight, values_mb.astype(jnp.float32))
    att = att.reshape(rows, HEADS * HD).astype(jnp.bfloat16)
    out = jnp.dot(att, wo_layer, preferred_element_type=jnp.float32)
    return (hf + out).astype(jnp.bfloat16)

def reference(state, next_embed, tenant, lengths, gain, bias, wq, wo, keys, values):
    finals = []
    emitted = []
    for batch in range(MBS):
        ids = tenant[batch]
        h = state[batch]
        for layer in range(batch, LAYERS):
            h = one_layer(h, gain[layer][ids], bias[layer][ids], wq[layer], wo[layer], keys[layer, batch], values[layer, batch], lengths[batch])
        emitted.append(h)
        h = next_embed[batch]
        for layer in range(batch):
            h = one_layer(h, gain[layer][ids], bias[layer][ids], wq[layer], wo[layer], keys[layer, batch], values[layer, batch], lengths[batch])
        finals.append(h)
    return (jnp.stack(finals), jnp.stack(emitted))
```

```python
import jax
import jax.numpy as jnp
from jax import lax
from jax.sharding import PartitionSpec as P

HD = 128
BF = jnp.bfloat16
F32 = jnp.float32


def swapped(block, axis, bits):
    route = [(i, i ^ bits) for i in range(lax.axis_size(axis))]
    return lax.ppermute(block, axis, route)


def peers(block, axis):
    return [block] + [swapped(block, axis, d) for d in range(1, lax.axis_size(axis))]


def tree_sum(pieces):
    pieces = [piece.astype(F32) for piece in pieces]
    while len(pieces) > 1:
        pieces = [pieces[i] + pieces[i + 1] for i in range(0, len(pieces), 2)]
    return pieces[0]


def unswap(rows, place):
    count = rows.shape[0]
    bit = 1
    while bit < count:
        flipped = rows.reshape((count // (2 * bit), 2, bit) + rows.shape[1:])[:, ::-1].reshape(rows.shape)
        rows = jnp.where((place & bit) > 0, flipped, rows)
        bit *= 2
    return rows


def on_device(state, next_embed, tenant, lengths, gain, bias, wq, wo, keys, values):
    sections = lax.axis_size("section")
    tensors = lax.axis_size("tensor")
    section_at = lax.axis_index("section")
    tensor_at = lax.axis_index("tensor")
    replica_at = lax.axis_index("replica")
    rows_mb = state.shape[1]
    width_part = state.shape[2]
    width_all = width_part * lax.axis_size("replica")
    query_part = wq.shape[2]
    heads_dev = query_part // HD
    key_heads = keys.shape[3]
    group = heads_dev * tensors // key_heads
    kv_dev = max(1, heads_dev // group)
    per_kv = heads_dev // kv_dev
    pos_dev = keys.shape[4]
    batches = tenant.shape[0]
    order = jnp.stack([(section_at - tick) % sections for tick in range(sections)])

    ids = tenant[order].reshape(-1)
    local = ids - tensor_at * gain.shape[1]
    onehot = (local[:, None] == jnp.arange(gain.shape[1])[None, :]).astype(BF)
    gain_mine = jnp.dot(onehot, gain[0], preferred_element_type=F32).astype(BF)
    bias_mine = jnp.dot(onehot, bias[0], preferred_element_type=F32).astype(BF)
    affine = jnp.stack([gain_mine, bias_mine], 0).reshape(2, sections, rows_mb, width_part)
    affine = tree_sum(peers(affine, "tensor"))

    kv = jnp.stack([keys[0, :, 0], values[0, :, 0]], 0)

    def heads_of(place):
        start = place * heads_dev // group
        return lax.dynamic_slice_in_dim(kv, start, kv_dev, 2)

    parts = [heads_of(tensor_at)]
    spots = [tensor_at * pos_dev + jnp.arange(pos_dev)]
    for d in range(1, tensors):
        parts.append(swapped(heads_of(tensor_at ^ d), "tensor", d))
        spots.append((tensor_at ^ d) * pos_dev + jnp.arange(pos_dev))
    kv = jnp.concatenate(parts, 3)
    spots = jnp.concatenate(spots)
    kv_rows = unswap(jnp.stack(peers(kv, "replica"), 0), replica_at)
    length_rows = unswap(jnp.stack(peers(lengths[:, 0].astype(F32), "replica"), 0), replica_at)

    h = state[0]
    emitted = jnp.zeros_like(h)
    at_first = section_at == 0
    for tick in range(sections):
        batch = order[tick]
        hf = h.astype(F32)
        stats = jnp.stack([jnp.sum(hf, axis=-1), jnp.sum(hf * hf, axis=-1)], 0)
        stats = tree_sum(peers(stats, "replica")) / width_all
        mean = stats[0][:, None]
        var = stats[1][:, None] - mean * mean
        normed = ((hf - mean) * lax.rsqrt(var + 1e-05) * affine[0, tick] + affine[1, tick]).astype(BF)
        query_part_sum = jnp.dot(normed, wq[0], preferred_element_type=F32).astype(BF)
        query = tree_sum(peers(query_part_sum, "replica")).astype(BF)
        grouped = query.reshape(rows_mb, kv_dev, per_kv, HD)
        kv_now = lax.dynamic_index_in_dim(kv_rows, batch, 2, keepdims=False)
        lengths_now = lax.dynamic_index_in_dim(length_rows, batch, 1, keepdims=False)
        scores = jnp.einsum("rgjd,rgpd->rgjp", grouped, kv_now[:, 0], preferred_element_type=F32)
        scores = scores / jnp.sqrt(F32(HD))
        valid = spots.astype(F32)[None, None, None, :] < lengths_now[:, None, None, None]
        scores = jnp.where(valid, scores, -1e30)
        top = jnp.max(scores, axis=-1, keepdims=True)
        probs = jnp.exp(scores - top) * valid.astype(F32)
        weight = probs / jnp.sum(probs, axis=-1, keepdims=True)
        att = jnp.einsum("rgjp,rgpd->rgjd", weight, kv_now[:, 1].astype(F32))
        att = att.reshape(rows_mb, query_part).astype(BF)
        out = jnp.dot(att, wo[0], preferred_element_type=F32).astype(BF)
        out = tree_sum(peers(out, "tensor"))
        h = (hf + out).astype(BF)
        ring = [(i, (i + 1) % sections) for i in range(sections)]
        h = lax.ppermute(h, "section", ring)
        if tick > 0:
            emitted = lax.ppermute(emitted, "section", ring)
        arriving = -(tick + 1) % sections
        emitted = jnp.where(at_first, h, emitted)
        h = jnp.where(at_first, next_embed[arriving], h)
    return (h[None], emitted[None])


def solution(mesh):
    in_specs = (
        P("section", None, "replica"),
        P(None, None, "replica"),
        P(),
        P(None, "replica"),
        P("section", "tensor", "replica"),
        P("section", "tensor", "replica"),
        P("section", "replica", "tensor"),
        P("section", "tensor", "replica"),
        P("section", None, "replica", None, "tensor", None),
        P("section", None, "replica", None, "tensor", None),
    )
    out_specs = (P("section", None, "replica"), P("section", None, "replica"))
    return jax.shard_map(
        on_device, mesh=mesh, in_specs=in_specs, out_specs=out_specs, check_vma=False
    )
```

```python
import jax
import jax.numpy as jnp
from jax import lax
from jax.sharding import PartitionSpec as P

HD = 128
BF = jnp.bfloat16
F32 = jnp.float32


def swapped(block, axis, bits):
    route = [(i, i ^ bits) for i in range(lax.axis_size(axis))]
    return lax.ppermute(block, axis, route)


def peers(block, axis):
    count = lax.axis_size(axis)
    sent = jnp.broadcast_to(block[None], (count,) + block.shape)
    got = lax.all_to_all(sent, axis, 0, 0)
    return [got[i] for i in range(count)]


def tree_sum(pieces):
    pieces = [piece.astype(F32) for piece in pieces]
    while len(pieces) > 1:
        pieces = [pieces[i] + pieces[i + 1] for i in range(0, len(pieces), 2)]
    return pieces[0]


def unswap(rows, place):
    count = rows.shape[0]
    bit = 1
    while bit < count:
        flipped = rows.reshape((count // (2 * bit), 2, bit) + rows.shape[1:])[:, ::-1].reshape(rows.shape)
        rows = jnp.where((place & bit) > 0, flipped, rows)
        bit *= 2
    return rows


def on_device(state, next_embed, tenant, lengths, gain, bias, wq, wo, keys, values):
    sections = lax.axis_size("section")
    tensors = lax.axis_size("tensor")
    section_at = lax.axis_index("section")
    tensor_at = lax.axis_index("tensor")
    replica_at = lax.axis_index("replica")
    rows_mb = state.shape[1]
    width_part = state.shape[2]
    width_all = width_part * lax.axis_size("replica")
    query_part = wq.shape[2]
    heads_dev = query_part // HD
    key_heads = keys.shape[3]
    group = heads_dev * tensors // key_heads
    kv_dev = max(1, heads_dev // group)
    per_kv = heads_dev // kv_dev
    pos_dev = keys.shape[4]
    batches = tenant.shape[0]
    order = jnp.stack([(section_at - tick) % sections for tick in range(sections)])

    ids = tenant[order].reshape(-1)
    local = ids - tensor_at * gain.shape[1]
    onehot = (local[:, None] == jnp.arange(gain.shape[1])[None, :]).astype(BF)
    gain_mine = jnp.dot(onehot, gain[0], preferred_element_type=F32).astype(BF)
    bias_mine = jnp.dot(onehot, bias[0], preferred_element_type=F32).astype(BF)
    affine = jnp.stack([gain_mine, bias_mine], 0).reshape(2, sections, rows_mb, width_part)
    affine = tree_sum(peers(affine, "tensor"))

    kv = jnp.stack([keys[0, :, 0], values[0, :, 0]], 0)

    picks = jnp.stack(
        [
            lax.slice_in_dim(kv, i * heads_dev // group, i * heads_dev // group + kv_dev, axis=2)
            for i in range(tensors)
        ],
        0,
    )
    got = lax.all_to_all(picks, "tensor", 0, 0)
    kv = jnp.concatenate([got[i] for i in range(tensors)], 3)
    spots = jnp.arange(tensors * pos_dev)
    kv_rows = jnp.stack(peers(kv, "replica"), 0)
    length_rows = jnp.stack(peers(lengths[:, 0].astype(F32), "replica"), 0)

    h = state[0]
    emitted = jnp.zeros_like(h)
    at_first = section_at == 0
    for tick in range(sections):
        batch = order[tick]
        ring = [(i, (i + 1) % sections) for i in range(sections)]
        h_behind = lax.ppermute(h, "section", ring)
        if tick > 0:
            emitted_behind = lax.ppermute(emitted, "section", ring)
        hf = h.astype(F32)
        stats = jnp.stack([jnp.sum(hf, axis=-1), jnp.sum(hf * hf, axis=-1)], 0)
        stats = tree_sum(peers(stats, "replica")) / width_all
        mean = stats[0][:, None]
        var = stats[1][:, None] - mean * mean
        normed = ((hf - mean) * lax.rsqrt(var + 1e-05) * affine[0, tick] + affine[1, tick]).astype(BF)
        query_part_sum = jnp.dot(normed, wq[0], preferred_element_type=F32).astype(BF)
        query = tree_sum(peers(query_part_sum, "replica")).astype(BF)
        grouped = query.reshape(rows_mb, kv_dev, per_kv, HD)
        kv_now = lax.dynamic_index_in_dim(kv_rows, batch, 2, keepdims=False)
        lengths_now = lax.dynamic_index_in_dim(length_rows, batch, 1, keepdims=False)
        scores = jnp.einsum("rgjd,rgpd->rgjp", grouped, kv_now[:, 0], preferred_element_type=F32)
        scores = scores / jnp.sqrt(F32(HD))
        valid = spots.astype(F32)[None, None, None, :] < lengths_now[:, None, None, None]
        scores = jnp.where(valid, scores, -1e30)
        top = jnp.max(scores, axis=-1, keepdims=True)
        probs = jnp.exp(scores - top) * valid.astype(F32)
        weight = probs / jnp.sum(probs, axis=-1, keepdims=True)
        att = jnp.einsum("rgjp,rgpd->rgjd", weight, kv_now[:, 1].astype(F32))
        att = att.reshape(rows_mb, query_part).astype(BF)
        out = jnp.dot(att, wo[0], preferred_element_type=F32).astype(BF)
        sent = jnp.broadcast_to(out[None], (sections * tensors,) + out.shape)
        got = lax.all_to_all(sent, ("section", "tensor"), 0, 0)
        behind = (section_at + sections - 1) % sections
        got = lax.dynamic_slice_in_dim(got, behind * tensors, tensors, 0)
        out = tree_sum([got[i] for i in range(tensors)])
        h = (h_behind.astype(F32) + out).astype(BF)
        if tick > 0:
            emitted = emitted_behind
        arriving = -(tick + 1) % sections
        emitted = jnp.where(at_first, h, emitted)
        h = jnp.where(at_first, next_embed[arriving], h)
    return (h[None], emitted[None])


def solution(mesh):
    in_specs = (
        P("section", None, "replica"),
        P(None, None, "replica"),
        P(),
        P(None, "replica"),
        P("section", "tensor", "replica"),
        P("section", "tensor", "replica"),
        P("section", "replica", "tensor"),
        P("section", "tensor", "replica"),
        P("section", None, "replica", None, "tensor", None),
        P("section", None, "replica", None, "tensor", None),
    )
    out_specs = (P("section", None, "replica"), P("section", None, "replica"))
    return jax.shard_map(
        on_device, mesh=mesh, in_specs=in_specs, out_specs=out_specs, check_vma=False
    )
```

```python
import jax
import jax.numpy as jnp
from jax import lax
from jax.experimental import pallas as pl
from jax.experimental.pallas import tpu as pltpu
from jax.sharding import PartitionSpec as P

HD = 128
BF = jnp.bfloat16
F32 = jnp.float32
VMEM = pl.BlockSpec(memory_space=pltpu.VMEM)
LIMIT = 12 * 1024 * 1024


def swapped(block, axis, bits):
    route = [(i, i ^ bits) for i in range(lax.axis_size(axis))]
    return lax.ppermute(block, axis, route)


def peers(block, axis):
    return [block] + [swapped(block, axis, d) for d in range(1, lax.axis_size(axis))]


def from_behind(block, bits):
    sections, tensors = lax.axis_size("section"), lax.axis_size("tensor")
    route = [
        (s * tensors + (t ^ bits), (s + 1) % sections * tensors + t)
        for s in range(sections)
        for t in range(tensors)
    ]
    return lax.ppermute(block, ("section", "tensor"), route)


def tree_sum(pieces):
    pieces = [piece.astype(F32) for piece in pieces]
    while len(pieces) > 1:
        pieces = [pieces[i] + pieces[i + 1] for i in range(0, len(pieces), 2)]
    return pieces[0]


def hold_kernel(parts, after_ref, w_ref, out_ref, sems):
    rows = w_ref.shape[0] // parts
    copies = [
        pltpu.make_async_copy(
            w_ref.at[pl.ds(i * rows, rows)], out_ref.at[pl.ds(i * rows, rows)], sems.at[i]
        )
        for i in range(parts)
    ]
    for copy in copies:
        copy.start()
    for copy in copies:
        copy.wait()


def hold(weights, after):
    weights = pltpu.with_memory_space_constraint(weights, pltpu.HBM)
    parts = 8
    return pl.pallas_call(
        lambda *refs: hold_kernel(parts, *refs),
        out_shape=pltpu.VMEM(weights.shape, weights.dtype),
        in_specs=[VMEM, pl.BlockSpec(memory_space=pltpu.HBM)],
        out_specs=VMEM,
        scratch_shapes=[pltpu.SemaphoreType.DMA((parts,))],
        compiler_params=pltpu.CompilerParams(vmem_limit_bytes=LIMIT),
        cost_estimate=pl.CostEstimate(
            flops=0, bytes_accessed=2 * weights.size, transcendentals=0
        ),
    )(after, weights)


def tiled_dot(x, w_ref, out_ref):
    width = min(512, w_ref.shape[1])
    for i in range(w_ref.shape[1] // width):
        at = slice(i * width, (i + 1) * width)
        out_ref[:, at] = jnp.dot(x, w_ref[:, at], preferred_element_type=F32).astype(out_ref.dtype)


def times_kernel(x_ref, w_ref, out_ref):
    tiled_dot(x_ref[...], w_ref, out_ref)


def times(x, w, dtype):
    return pl.pallas_call(
        times_kernel,
        out_shape=jax.ShapeDtypeStruct((x.shape[0], w.shape[1]), dtype),
        in_specs=[VMEM, VMEM],
        out_specs=VMEM,
        compiler_params=pltpu.CompilerParams(vmem_limit_bytes=LIMIT),
        cost_estimate=pl.CostEstimate(
            flops=2 * x.shape[0] * w.size, bytes_accessed=2 * w.size, transcendentals=0
        ),
    )(x, w)


def attend_kernel(count, batch_ref, *refs):
    pieces, (keep_ref, kv_ref, w_ref, out_ref) = refs[:count], refs[count:]
    batch = batch_ref[0]
    query = tree_sum([piece[...] for piece in pieces]).astype(BF).astype(F32)
    slots, kv_dev = kv_ref.shape[0], kv_ref.shape[3]
    heads = query.shape[1] // HD
    per_kv = heads // kv_dev
    rows = query.shape[0]
    keep = jnp.concatenate([keep_ref[...]] * per_kv, 0)
    att = []
    for g in range(kv_dev):
        mine = jnp.concatenate(
            [query[:, h * HD : (h + 1) * HD] for h in range(g * per_kv, (g + 1) * per_kv)], 0
        ).astype(BF)
        keys = jnp.concatenate([kv_ref[i, 0, batch, g] for i in range(slots)], 0)
        values = jnp.concatenate([kv_ref[i, 1, batch, g] for i in range(slots)], 0)
        scores = lax.dot_general(
            mine, keys, (((1,), (1,)), ((), ())), preferred_element_type=F32
        )
        scores = scores * (HD**-0.5) + keep
        probs = jnp.exp(scores - jnp.max(scores, axis=-1, keepdims=True))
        total = jnp.sum(probs, axis=-1, keepdims=True)
        got = jnp.dot(probs.astype(BF), values, preferred_element_type=F32) / total
        att += [got[h * rows : (h + 1) * rows] for h in range(per_kv)]
    tiled_dot(jnp.concatenate(att, 1).astype(BF), w_ref, out_ref)


def attend(batch, pieces, keep, kv, w):
    count = len(pieces)
    return pl.pallas_call(
        lambda *refs: attend_kernel(count, *refs),
        out_shape=jax.ShapeDtypeStruct((pieces[0].shape[0], w.shape[1]), BF),
        in_specs=[pl.BlockSpec(memory_space=pltpu.SMEM)] + [VMEM] * (count + 3),
        out_specs=VMEM,
        compiler_params=pltpu.CompilerParams(vmem_limit_bytes=LIMIT),
        cost_estimate=pl.CostEstimate(
            flops=8 * w.size, bytes_accessed=2 * w.size, transcendentals=0
        ),
    )(batch.reshape(1).astype(jnp.int32), *pieces, keep, kv, w)


def on_device(state, next_embed, tenant, lengths, gain, bias, wq, wo, keys, values):
    sections = lax.axis_size("section")
    tensors = lax.axis_size("tensor")
    replicas = lax.axis_size("replica")
    section_at = lax.axis_index("section")
    tensor_at = lax.axis_index("tensor")
    replica_at = lax.axis_index("replica")
    rows_mb = state.shape[1]
    width_part = state.shape[2]
    width_all = width_part * replicas
    query_part = wq.shape[2]
    heads_dev = query_part // HD
    key_heads = keys.shape[3]
    group = heads_dev * tensors // key_heads
    kv_dev = max(1, heads_dev // group)
    pos_dev = keys.shape[4]
    batches = [(section_at - tick) % sections for tick in range(sections)]

    local = tenant.reshape(-1) - tensor_at * gain.shape[1]
    onehot = (local[:, None] == jnp.arange(gain.shape[1])[None, :]).astype(BF)
    shape = (sections, rows_mb, width_part)
    gain_mine = jnp.dot(onehot, gain[0], preferred_element_type=F32).astype(BF).reshape(shape)
    bias_mine = jnp.dot(onehot, bias[0], preferred_element_type=F32).astype(BF).reshape(shape)

    def affine_mine(tick):
        pick = lambda rows: lax.dynamic_index_in_dim(rows, batches[tick], 0, keepdims=False)
        return jnp.concatenate([pick(gain_mine), pick(bias_mine)], 0)

    affine = [tree_sum(peers(affine_mine(0), "tensor"))]

    def local_stats(hf):
        return jnp.concatenate([jnp.sum(hf, axis=-1), jnp.sum(hf * hf, axis=-1)])

    h = state[0]
    hf = h.astype(F32)
    first = peers(jnp.concatenate([local_stats(hf), lengths[:, 0].astype(F32)]), "replica")
    stats = tree_sum([piece[: 2 * rows_mb] for piece in first])

    kv = jnp.stack([keys[0, :, 0], values[0, :, 0]], 0)
    later = [affine_mine(tick) for tick in range(1, sections)]
    later = [] if sections == 1 else [jnp.concatenate(later, 0)]

    def heads_of(place):
        start = place * heads_dev // group
        return lax.dynamic_slice_in_dim(kv, start, kv_dev, 2)

    sent = [
        jnp.concatenate(later + [heads_of(tensor_at ^ d).reshape(-1, width_part)], 0)
        for d in range(tensors)
    ]
    got = [sent[0]] + [swapped(sent[d], "tensor", d) for d in range(1, tensors)]
    split = sum(rows.shape[0] for rows in later)
    if split:
        rest = tree_sum([piece[:split] for piece in got])
        affine += [rest[i : i + 2 * rows_mb] for i in range(0, split, 2 * rows_mb)]
    kv_shape = (2, sections, kv_dev, pos_dev, HD)
    kv = jnp.concatenate([piece[split:].reshape(kv_shape) for piece in got], 3)[None]
    turns = [0]
    bit = replicas // 2
    while bit:
        kv = jnp.concatenate([kv, swapped(kv, "replica", bit)], 0)
        turns = turns + [turn ^ bit for turn in turns]
        bit //= 2

    spots = jnp.concatenate([(tensor_at ^ d) * pos_dev + jnp.arange(pos_dev) for d in range(tensors)])
    spots = spots.astype(F32)

    def keep_of(tick):
        cols = []
        for turn in turns:
            length = lax.dynamic_index_in_dim(first[turn][2 * rows_mb :], batches[tick], 0)
            own = jnp.arange(rows_mb)[:, None] == (replica_at ^ turn)
            cols.append(jnp.where(own & (spots < length)[None, :], 0.0, -1e30))
        return jnp.concatenate(cols, 1)

    def scale_of(stats):
        mean = (stats[:rows_mb] / width_all)[:, None]
        var = (stats[rows_mb:] / width_all)[:, None] - mean * mean
        return mean, lax.rsqrt(var + 1e-05)

    wq_held = hold(wq[0], h)
    wo_held = None
    emitted = jnp.zeros_like(h)
    at_first = section_at == 0
    for tick in range(sections):
        gain_now, bias_now = affine[tick][:rows_mb], affine[tick][rows_mb:]
        if tick == 0:
            mean, rstd = scale_of(stats)
            normed = ((hf - mean) * rstd * gain_now + bias_now).astype(BF)
            query = times(normed, wq_held, BF)
            wo_held = hold(wo[0], query)
        else:
            mine = jnp.mean(hf, axis=-1, keepdims=True)
            centred = ((hf - mine) * gain_now).astype(BF)
            rows = jnp.concatenate([centred, affine[tick].astype(BF)], 0)
            stats = tree_sum(peers(local_stats(hf), "replica"))
            three = times(rows, wq_held, F32)
            mean, rstd = scale_of(stats)
            query = rstd * (three[:rows_mb] + (mine - mean) * three[rows_mb : 2 * rows_mb])
            query = (query + three[2 * rows_mb :]).astype(BF)
        if tick == 0:
            behind = from_behind(h, 0)
        else:
            both = from_behind(jnp.concatenate([h, emitted], 0), 0)
            behind, emitted = both[:rows_mb], both[rows_mb:]
        out = attend(batches[tick], peers(query, "replica"), keep_of(tick), kv, wo_held)
        out = tree_sum([from_behind(out, d) for d in range(tensors)])
        h = (behind.astype(F32) + out).astype(BF)
        arriving = -(tick + 1) % sections
        emitted = jnp.where(at_first, h, emitted)
        h = jnp.where(at_first, next_embed[arriving], h)
        hf = h.astype(F32)
    return (h[None], emitted[None])


def solution(mesh):
    in_specs = (
        P("section", None, "replica"),
        P(None, None, "replica"),
        P(),
        P(None, "replica"),
        P("section", "tensor", "replica"),
        P("section", "tensor", "replica"),
        P("section", "replica", "tensor"),
        P("section", "tensor", "replica"),
        P("section", None, "replica", None, "tensor", None),
        P("section", None, "replica", None, "tensor", None),
    )
    out_specs = (P("section", None, "replica"), P("section", None, "replica"))
    return jax.shard_map(
        on_device, mesh=mesh, in_specs=in_specs, out_specs=out_specs, check_vma=False
    )
```

```python
import jax
import jax.numpy as jnp
from jax import lax
from jax.experimental import pallas as pl
from jax.experimental.pallas import tpu as pltpu
from jax.sharding import PartitionSpec as P

HD = 128
BF = jnp.bfloat16
F32 = jnp.float32
VMEM = pl.BlockSpec(memory_space=pltpu.VMEM)
SMEM = pl.BlockSpec(memory_space=pltpu.SMEM)
HBM = pl.BlockSpec(memory_space=pltpu.HBM)
PARAMS = pltpu.CompilerParams(vmem_limit_bytes=12 * 1024 * 1024)


def in_hbm(x):
    return pltpu.with_memory_space_constraint(x, pltpu.HBM)


def shape(dims, dtype=BF):
    return jax.ShapeDtypeStruct(tuple(dims), dtype)


def cost(flops, size):
    return pl.CostEstimate(flops=flops, bytes_accessed=size, transcendentals=0)


def swapped(block, axis, bits):
    route = [(i, i ^ bits) for i in range(lax.axis_size(axis))]
    return lax.ppermute(block, axis, route)


def from_behind(block, bits):
    sections, tensors = lax.axis_size("section"), lax.axis_size("tensor")
    route = [
        (s * tensors + (t ^ bits), (s + 1) % sections * tensors + t)
        for s in range(sections)
        for t in range(tensors)
    ]
    return lax.ppermute(block, ("section", "tensor"), route)


def tree_sum(pieces):
    pieces = [piece.astype(F32) for piece in pieces]
    while len(pieces) > 1:
        pieces = [pieces[i] + pieces[i + 1] for i in range(0, len(pieces), 2)]
    return pieces[0]


def batch_at(tick, sections):
    return lax.rem(lax.axis_index("section") + (sections - tick), sections)


def pack_kernel(dims, ids_ref, gain_ref, bias_ref, keys_ref, values_ref, *refs):
    sections, tensors, rows, heads_dev, group, kv_dev = dims
    packs, later_ref = refs[:tensors], refs[tensors] if sections > 1 else None
    gains, biases, keys, values, sems = refs[-5:]
    copies = [
        pltpu.make_async_copy(source, target, sems.at[i])
        for i, (source, target) in enumerate(
            [(gain_ref, gains), (bias_ref, biases), (keys_ref, keys), (values_ref, values)]
        )
    ]
    for copy in copies:
        copy.start()
    at = lax.axis_index("tensor")
    tenants = gains.shape[0]
    count = sections * rows
    spot = lax.broadcasted_iota(jnp.int32, (count, tenants), 0)
    wanted = jnp.zeros((count, tenants), jnp.int32)
    for tick in range(sections):
        batch = batch_at(tick, sections)
        for i in range(rows):
            wanted = jnp.where(spot == tick * rows + i, ids_ref[batch, i], wanted)
    wanted = wanted - at * tenants
    onehot = jnp.where(wanted == lax.broadcasted_iota(jnp.int32, (count, tenants), 1), 1.0, 0.0)
    onehot = onehot.astype(BF)
    copies[2].wait()
    copies[3].wait()
    pos, lanes = keys.shape[2:]
    width = gains.shape[1]
    per = pos // (2 * rows)
    blocks = width // lanes // per
    for d in range(tensors):
        start = lax.bitwise_xor(at, d) * heads_dev // group
        for which, cache in enumerate((keys, values)):
            for b in range(sections):
                for g in range(kv_dev):
                    to = blocks + (which * sections + b) * kv_dev + g
                    packs[d][to] = cache[b, start + g]
    copies[0].wait()
    gain_rows = jnp.dot(onehot, gains[...], preferred_element_type=F32)
    copies[1].wait()
    bias_rows = jnp.dot(onehot, biases[...], preferred_element_type=F32)
    for tick in range(sections):
        mine = slice(tick * rows, (tick + 1) * rows)
        both = jnp.concatenate([gain_rows[mine], bias_rows[mine]], 0)
        for j in range(blocks):
            block = jnp.concatenate(
                [both[:, (j * per + k) * lanes : (j * per + k + 1) * lanes] for k in range(per)], 0
            ).astype(BF)
            if tick == 0:
                for d in range(tensors):
                    packs[d][j] = block
            else:
                later_ref[(tick - 1) * blocks + j] = block


def pack(dims, tenant, gain, bias, keys, values):
    sections, tensors, rows, heads_dev, group, kv_dev = dims
    pos = keys.shape[2]
    blocks = 2 * rows * gain.shape[1] // (pos * HD)
    out_shape = [shape((blocks + 2 * sections * kv_dev, pos, HD))] * tensors
    if sections > 1:
        out_shape += [shape(((sections - 1) * blocks, pos, HD))]
    return pl.pallas_call(
        lambda *refs: pack_kernel(dims, *refs),
        out_shape=out_shape,
        in_specs=[SMEM] + [HBM] * 4,
        out_specs=[VMEM] * len(out_shape),
        scratch_shapes=[pltpu.VMEM(x.shape, BF) for x in (gain, bias, keys, values)]
        + [pltpu.SemaphoreType.DMA((4,))],
        compiler_params=PARAMS,
        cost_estimate=cost(0, 4 * gain.size),
    )(tenant, in_hbm(gain), in_hbm(bias), in_hbm(keys), in_hbm(values))


def hold_kernel(parts, after_ref, w_ref, out_ref, sems):
    rows = w_ref.shape[0] // parts
    copies = [
        pltpu.make_async_copy(
            w_ref.at[pl.ds(i * rows, rows)], out_ref.at[pl.ds(i * rows, rows)], sems.at[i]
        )
        for i in range(parts)
    ]
    for copy in copies:
        copy.start()
    for copy in copies:
        copy.wait()


def hold(weights, after):
    parts = 8
    return pl.pallas_call(
        lambda *refs: hold_kernel(parts, *refs),
        out_shape=pltpu.VMEM(weights.shape, weights.dtype),
        in_specs=[VMEM, HBM],
        out_specs=VMEM,
        scratch_shapes=[pltpu.SemaphoreType.DMA((parts,))],
        compiler_params=PARAMS,
        cost_estimate=cost(0, 2 * weights.size),
    )(after, in_hbm(weights))


def tiles(w_ref):
    width = min(512, w_ref.shape[1])
    return [slice(i, i + width) for i in range(0, w_ref.shape[1], width)]


def thirds(x):
    high = x.astype(BF).astype(F32)
    middle = (x - high).astype(BF).astype(F32)
    return [high, middle, x - high - middle]


def query_sums(first_block, length, h, pieces, w_ref, out_ref):
    rows, width = h.shape
    pos, lanes = pieces[0].shape[1:]
    per = pos // (2 * rows)
    cols = []
    for j in range(width // lanes // per):
        block = tree_sum([piece[first_block + j] for piece in pieces])
        cols += [block[k * 2 * rows : (k + 1) * 2 * rows] for k in range(per)]
    affine = jnp.concatenate(cols, 1)
    total = jnp.sum(h, axis=-1, keepdims=True)
    squares = jnp.sum(h * h, axis=-1, keepdims=True)
    centred = (h - total * (1.0 / width)) * affine[:rows]
    x = jnp.concatenate([centred, affine], 0).astype(BF)
    count = w_ref.shape[1]
    for at in tiles(w_ref):
        got = jnp.dot(x, w_ref[:, at], preferred_element_type=F32)
        for k in range(3):
            to = slice(k * count + at.start, k * count + at.stop)
            out_ref[:, to] = got[k * rows : (k + 1) * rows].astype(BF)
    lane = lax.broadcasted_iota(jnp.int32, (rows, HD), 1)
    tail = jnp.full((rows, HD), length.astype(F32))
    for i, term in enumerate(thirds(total) + thirds(squares)):
        tail = jnp.where(lane == i, term, tail)
    out_ref[:, 3 * count :] = tail.astype(BF)


def first_kernel(tensors, sections, lengths_ref, h_ref, *refs):
    pieces, (w_ref, out_ref) = refs[:tensors], refs[tensors:]
    length = lengths_ref[batch_at(0, sections), 0]
    query_sums(0, length, h_ref[...].astype(F32), pieces, w_ref, out_ref)


def first_sums(sections, lengths, h, pieces, w):
    tensors = len(pieces)
    return pl.pallas_call(
        lambda *refs: first_kernel(tensors, sections, *refs),
        out_shape=shape((h.shape[0], 3 * w.shape[1] + HD)),
        in_specs=[SMEM] + [VMEM] * (tensors + 2),
        out_specs=VMEM,
        compiler_params=PARAMS,
        cost_estimate=cost(24 * w.size, 2 * w.size),
    )(lengths, h, *pieces, w)


def arrive(arrivals, next_ref):
    width = next_ref.shape[1]
    rest = arrivals[0][:, width:]
    came = tree_sum([arrival[:, :width] for arrival in arrivals]) + rest[:, :width].astype(F32)
    came = came.astype(BF).astype(F32)
    at_first = jnp.full(came.shape, lax.axis_index("section")) == 0
    carried = rest[:, width:].astype(F32) if rest.shape[1] > width else jnp.zeros_like(came)
    h = jnp.where(at_first, next_ref[...].astype(F32), came)
    return h, jnp.where(at_first, came, carried)


def later_kernel(tensors, sections, tick, lengths_ref, *refs):
    arrivals, next_ref = refs[:tensors], refs[tensors]
    pieces, (w_ref, out_ref, carry_ref) = refs[tensors + 1 : 2 * tensors + 1], refs[2 * tensors + 1 :]
    h, emitted = arrive(arrivals, next_ref)
    width = h.shape[1]
    carry_ref[:, :width] = h.astype(BF)
    carry_ref[:, width:] = emitted.astype(BF)
    length = lengths_ref[batch_at(tick, sections), 0]
    blocks = 2 * h.shape[0] * width // (pieces[0].shape[1] * HD)
    query_sums((tick - 1) * blocks, length, h, pieces, w_ref, out_ref)


def later_sums(sections, tick, lengths, arrivals, following, pieces, w):
    tensors = len(pieces)
    rows, width = following.shape
    return pl.pallas_call(
        lambda *refs: later_kernel(tensors, sections, tick, *refs),
        out_shape=[shape((rows, 3 * w.shape[1] + HD)), shape((rows, 2 * width))],
        in_specs=[SMEM] + [VMEM] * (2 * tensors + 2),
        out_specs=[VMEM] * 2,
        compiler_params=PARAMS,
        cost_estimate=cost(24 * w.size, 2 * w.size),
    )(lengths, *arrivals, following, *pieces, w)


def last_kernel(tensors, *refs):
    state_ref, emitted_ref = refs[-2:]
    h, emitted = arrive(refs[:tensors], refs[tensors])
    state_ref[0] = h.astype(BF)
    emitted_ref[0] = emitted.astype(BF)


def last(arrivals, following):
    return pl.pallas_call(
        lambda *refs: last_kernel(len(arrivals), *refs),
        out_shape=[shape((1,) + following.shape)] * 2,
        in_specs=[VMEM] * (len(arrivals) + 1),
        out_specs=[VMEM] * 2,
        compiler_params=PARAMS,
    )(*arrivals, following)


def attend_kernel(dims, turns, tick, *refs):
    sections, tensors, rows, kv_dev = dims
    count = len(turns)
    pieces, (kv_ref, carry_ref, w_ref, out_ref, full_ref) = refs[:count], refs[count:]
    span = w_ref.shape[0]
    width = w_ref.shape[1]
    batch = batch_at(tick, sections)

    tails = [piece[:, 3 * span :].astype(F32) for piece in pieces]
    totals = [tail[:, 0:1] + tail[:, 1:2] + tail[:, 2:3] for tail in tails]
    squares = [tail[:, 3:4] + tail[:, 4:5] + tail[:, 5:6] for tail in tails]
    scale = 1.0 / (width * count)
    mean = tree_sum(totals) * scale
    rstd = lax.rsqrt(tree_sum(squares) * scale - mean * mean + 1e-05)
    query = tree_sum(
        [
            piece[:, :span].astype(F32)
            + (total * (1.0 / width) - mean) * piece[:, span : 2 * span].astype(F32)
            for piece, total in zip(pieces, totals)
        ]
    )
    query = rstd * query + tree_sum([piece[:, 2 * span : 3 * span] for piece in pieces])
    query = query.astype(BF).astype(F32)

    pos = kv_ref.shape[3]
    tensor_at, replica_at = lax.axis_index("tensor"), lax.axis_index("replica")
    cols = lax.broadcasted_iota(jnp.int32, (rows, tensors * pos), 1)
    row = lax.broadcasted_iota(jnp.int32, (rows, tensors * pos), 0)
    spots = jnp.bitwise_xor(cols // pos, tensor_at) * pos + cols % pos
    spots = spots.astype(F32)
    keep = []
    for turn in turns:
        valid = jnp.logical_and(row == jnp.bitwise_xor(replica_at, turn), spots < tails[turn][:, 6:7])
        keep.append(jnp.where(valid, 0.0, -1e30))
    per_kv = span // HD // kv_dev
    keep = jnp.concatenate([jnp.concatenate(keep, 1)] * per_kv, 0)

    att = []
    for g in range(kv_dev):
        mine = jnp.concatenate(
            [query[:, h * HD : (h + 1) * HD] for h in range(g * per_kv, (g + 1) * per_kv)], 0
        ).astype(BF)
        keys, values = (
            jnp.concatenate(
                [
                    kv_ref[i, d, (which * sections + batch) * kv_dev + g]
                    for i in range(count)
                    for d in range(tensors)
                ],
                0,
            )
            for which in range(2)
        )
        scores = lax.dot_general(mine, keys, (((1,), (1,)), ((), ())), preferred_element_type=F32)
        scores = scores * (HD**-0.5) + keep
        probs = jnp.exp(scores - jnp.max(scores, axis=-1, keepdims=True))
        total = jnp.sum(probs, axis=-1, keepdims=True)
        got = jnp.dot(probs.astype(BF), values, preferred_element_type=F32) / total
        att += [got[h * rows : (h + 1) * rows] for h in range(per_kv)]
    att = jnp.concatenate(att, 1).astype(BF)
    for at in tiles(w_ref):
        got = jnp.dot(att, w_ref[:, at], preferred_element_type=F32).astype(BF)
        out_ref[:, at] = got
        full_ref[:, at] = got
    full_ref[:, width:] = carry_ref[...]


def attend(dims, turns, tick, pieces, kv, carry, w):
    rows, width = carry.shape[0], w.shape[1]
    return pl.pallas_call(
        lambda *refs: attend_kernel(dims, turns, tick, *refs),
        out_shape=[shape((rows, width)), shape((rows, width + carry.shape[1]))],
        in_specs=[VMEM] * (len(pieces) + 3),
        out_specs=[VMEM] * 2,
        compiler_params=PARAMS,
        cost_estimate=cost(8 * w.size, 2 * w.size),
    )(*pieces, kv, carry, w)


def on_device(state, next_embed, tenant, lengths, gain, bias, wq, wo, keys, values):
    sections = lax.axis_size("section")
    tensors = lax.axis_size("tensor")
    replicas = lax.axis_size("replica")
    rows, width = state.shape[1:]
    heads_dev = wq.shape[2] // HD
    group = heads_dev * tensors // keys.shape[3]
    kv_dev = max(1, heads_dev // group)
    pos = keys.shape[4]
    dims = (sections, tensors, rows, heads_dev, group, kv_dev)

    packs = pack(dims, tenant, gain[0], bias[0], keys[0, :, 0], values[0, :, 0])
    packs, later = packs[:tensors], packs[tensors:]
    got = [packs[0]] + [swapped(packs[d], "tensor", d) for d in range(1, tensors)]
    wq_held = hold(wq[0], packs[0])

    blocks = 2 * rows * width // (pos * HD)
    kv = jnp.stack([piece[blocks:] for piece in got], 0)[None]
    turns = [0]
    bit = replicas // 2
    while bit:
        kv = jnp.concatenate([kv, swapped(kv, "replica", bit)], 0)
        turns = turns + [turn ^ bit for turn in turns]
        if bit == replicas // 2 and later:
            later = list(lax.optimization_barrier((later[0], kv))[:1])
            later = later + [swapped(later[0], "tensor", d) for d in range(1, tensors)]
        bit //= 2

    carry = state[0]
    wo_held = None
    arrivals = None
    for tick in range(sections):
        following = next_embed[-tick % sections]
        if tick == 0:
            sums = first_sums(sections, lengths, carry, got, wq_held)
            wo_held = hold(wo[0], sums)
        else:
            sums, carry = later_sums(sections, tick, lengths, arrivals, following, later, wq_held)
        pieces = [sums] + [swapped(sums, "replica", d) for d in range(1, replicas)]
        out, full = attend(
            (sections, tensors, rows, kv_dev), turns, tick, pieces, kv, carry, wo_held
        )
        arrivals = [from_behind(full, 0)] + [from_behind(out, d) for d in range(1, tensors)]
    return tuple(last(arrivals, next_embed[0]))


def solution(mesh):
    in_specs = (
        P("section", None, "replica"),
        P(None, None, "replica"),
        P(),
        P(None, "replica"),
        P("section", "tensor", "replica"),
        P("section", "tensor", "replica"),
        P("section", "replica", "tensor"),
        P("section", "tensor", "replica"),
        P("section", None, "replica", None, "tensor", None),
        P("section", None, "replica", None, "tensor", None),
    )
    out_specs = (P("section", None, "replica"), P("section", None, "replica"))
    return jax.shard_map(
        on_device, mesh=mesh, in_specs=in_specs, out_specs=out_specs, check_vma=False
    )
```

```python
import jax
import jax.numpy as jnp
from jax import lax
from jax.experimental import pallas as pl
from jax.experimental.pallas import tpu as pltpu
from jax.sharding import PartitionSpec as P

HD = 128
BF = jnp.bfloat16
F32 = jnp.float32
VMEM = pl.BlockSpec(memory_space=pltpu.VMEM)
SMEM = pl.BlockSpec(memory_space=pltpu.SMEM)
HBM = pl.BlockSpec(memory_space=pltpu.HBM)
PARAMS = pltpu.CompilerParams(vmem_limit_bytes=12 * 1024 * 1024)


def in_hbm(x):
    return pltpu.with_memory_space_constraint(x, pltpu.HBM)


def shape(dims, dtype=BF):
    return jax.ShapeDtypeStruct(tuple(dims), dtype)


def cost(flops, size):
    return pl.CostEstimate(flops=flops, bytes_accessed=size, transcendentals=0)


def swapped(block, axis, bits):
    route = [(i, i ^ bits) for i in range(lax.axis_size(axis))]
    return lax.ppermute(block, axis, route)


def from_behind(block, bits):
    sections, tensors = lax.axis_size("section"), lax.axis_size("tensor")
    route = [
        (s * tensors + (t ^ bits), (s + 1) % sections * tensors + t)
        for s in range(sections)
        for t in range(tensors)
    ]
    return lax.ppermute(block, ("section", "tensor"), route)


def tree_sum(pieces):
    pieces = [piece.astype(F32) for piece in pieces]
    while len(pieces) > 1:
        pieces = [pieces[i] + pieces[i + 1] for i in range(0, len(pieces), 2)]
    return pieces[0]


def batch_at(tick, sections):
    return lax.rem(lax.axis_index("section") + (sections - tick), sections)


def pack_kernel(dims, *refs):
    sections, tensors, rows, heads_dev, group, kv_dev = dims
    sources, refs = refs[:8], refs[8:]
    packs, (h_ref, next_ref, lengths_ref) = refs[:tensors], refs[tensors : tensors + 3]
    ids, lengths, gains, biases, keys, values, sems = refs[tensors + 3 :]
    targets = (ids, lengths, keys, values, gains, biases, h_ref, next_ref)
    copies = [
        pltpu.make_async_copy(source, target, sems.at[i])
        for i, (source, target) in enumerate(zip(sources, targets))
    ]
    for copy in copies:
        copy.start()
    at = lax.axis_index("tensor")
    tenants = gains.shape[0]
    count = sections * rows
    spot = lax.broadcasted_iota(jnp.int32, (count, tenants), 0)
    line = lax.broadcasted_iota(jnp.int32, lengths_ref.shape, 0)
    wanted = jnp.zeros((count, tenants), jnp.int32)
    kept = jnp.zeros(lengths_ref.shape, jnp.int32)
    copies[0].wait()
    copies[1].wait()
    for tick in range(sections):
        batch = batch_at(tick, sections)
        kept = jnp.where(line == tick, lengths[batch], kept)
        for i in range(rows):
            wanted = jnp.where(spot == tick * rows + i, ids[batch, i], wanted)
    lengths_ref[...] = kept.astype(F32)
    wanted = wanted - at * tenants
    onehot = jnp.where(wanted == lax.broadcasted_iota(jnp.int32, (count, tenants), 1), 1.0, 0.0)
    onehot = onehot.astype(BF)
    copies[2].wait()
    copies[3].wait()
    pos, lanes = keys.shape[2:]
    width = gains.shape[1]
    per = pos // (2 * rows)
    blocks = width // lanes // per
    for d in range(tensors):
        start = lax.bitwise_xor(at, d) * heads_dev // group
        for which, cache in enumerate((keys, values)):
            for b in range(sections):
                for g in range(kv_dev):
                    to = sections * blocks + (which * sections + b) * kv_dev + g
                    packs[d][to] = cache[b, start + g]
    copies[4].wait()
    gain_rows = jnp.dot(onehot, gains[...], preferred_element_type=F32)
    copies[5].wait()
    bias_rows = jnp.dot(onehot, biases[...], preferred_element_type=F32)
    for tick in range(sections):
        mine = slice(tick * rows, (tick + 1) * rows)
        both = jnp.concatenate([gain_rows[mine], bias_rows[mine]], 0)
        for j in range(blocks):
            block = jnp.concatenate(
                [both[:, (j * per + k) * lanes : (j * per + k + 1) * lanes] for k in range(per)], 0
            ).astype(BF)
            for d in range(tensors):
                packs[d][tick * blocks + j] = block
    copies[6].wait()
    copies[7].wait()


def pack(dims, tenant, lengths, gain, bias, keys, values, h, following):
    sections, tensors, rows, heads_dev, group, kv_dev = dims
    pos = keys.shape[2]
    blocks = 2 * rows * gain.shape[1] // (pos * HD)
    out_shape = [shape((sections * (blocks + 2 * kv_dev), pos, HD))] * tensors
    out_shape += [shape(h.shape), shape(following.shape), shape((sections, HD), F32)]
    operands = (tenant, lengths, keys, values, gain, bias, h, following)
    return pl.pallas_call(
        lambda *refs: pack_kernel(dims, *refs),
        out_shape=out_shape,
        in_specs=[HBM] * len(operands),
        out_specs=[VMEM] * len(out_shape),
        scratch_shapes=[pltpu.SMEM(x.shape, jnp.int32) for x in (tenant, lengths)]
        + [pltpu.VMEM(x.shape, BF) for x in (gain, bias, keys, values)]
        + [pltpu.SemaphoreType.DMA((len(operands),))],
        compiler_params=PARAMS,
        cost_estimate=cost(0, 4 * gain.size),
    )(*[in_hbm(x) for x in operands])


def join_kernel(count, first, refs):
    out_ref = refs[-1]
    for i in range(count):
        out_ref[i] = refs[i][first:]


def join(pieces, first, after):
    count = len(pieces)
    dims = pieces[0].shape
    return pl.pallas_call(
        lambda *refs: join_kernel(count, first, refs),
        out_shape=shape((count, dims[0] - first) + dims[1:]),
        in_specs=[VMEM] * count + [pl.BlockSpec(memory_space=pl.ANY)] * len(after),
        out_specs=VMEM,
        compiler_params=PARAMS,
    )(*pieces, *after)


def hold_kernel(parts, after_ref, wq_ref, wo_ref, wq_out, wo_out, sems):
    copies = []
    for source, target in ((wq_ref, wq_out), (wo_ref, wo_out)):
        rows = source.shape[0] // parts
        for i in range(parts):
            at = pl.ds(i * rows, rows)
            copies.append(
                pltpu.make_async_copy(source.at[at], target.at[at], sems.at[len(copies)])
            )
    for copy in copies:
        copy.start()
    for copy in copies:
        copy.wait()


def hold(wq, wo, after):
    parts = 8
    return pl.pallas_call(
        lambda *refs: hold_kernel(parts, *refs),
        out_shape=[pltpu.VMEM(wq.shape, BF), pltpu.VMEM(wo.shape, BF)],
        in_specs=[pl.BlockSpec(memory_space=pl.ANY), HBM, HBM],
        out_specs=[VMEM] * 2,
        scratch_shapes=[pltpu.SemaphoreType.DMA((2 * parts,))],
        compiler_params=PARAMS,
        cost_estimate=cost(0, 4 * wq.size),
    )(after, in_hbm(wq), in_hbm(wo))


def tiles(w_ref):
    width = min(512, w_ref.shape[1])
    return [slice(i, i + width) for i in range(0, w_ref.shape[1], width)]


def thirds(x):
    high = x.astype(BF).astype(F32)
    middle = (x - high).astype(BF).astype(F32)
    return [high, middle, x - high - middle]


def query_sums(first_block, length, h, pieces, w_ref, out_ref):
    rows, width = h.shape
    pos, lanes = pieces[0].shape[1:]
    per = pos // (2 * rows)
    cols = []
    for j in range(width // lanes // per):
        block = tree_sum([piece[first_block + j] for piece in pieces])
        cols += [block[k * 2 * rows : (k + 1) * 2 * rows] for k in range(per)]
    affine = jnp.concatenate(cols, 1)
    total = jnp.sum(h, axis=-1, keepdims=True)
    squares = jnp.sum(h * h, axis=-1, keepdims=True)
    centred = (h - total * (1.0 / width)) * affine[:rows]
    x = jnp.concatenate([centred, affine], 0).astype(BF)
    count = w_ref.shape[1]
    for at in tiles(w_ref):
        got = jnp.dot(x, w_ref[:, at], preferred_element_type=F32)
        for k in range(3):
            to = slice(k * count + at.start, k * count + at.stop)
            out_ref[:, to] = got[k * rows : (k + 1) * rows].astype(BF)
    lane = lax.broadcasted_iota(jnp.int32, (rows, HD), 1)
    tail = jnp.broadcast_to(length, (rows, HD))
    for i, term in enumerate(thirds(total) + thirds(squares)):
        tail = jnp.where(lane == i, term, tail)
    out_ref[:, 3 * count :] = tail.astype(BF)


def first_kernel(tensors, lengths_ref, h_ref, *refs):
    pieces, (w_ref, out_ref) = refs[:tensors], refs[tensors:]
    query_sums(0, lengths_ref[0:1], h_ref[...].astype(F32), pieces, w_ref, out_ref)


def first_sums(lengths, h, pieces, w):
    tensors = len(pieces)
    return pl.pallas_call(
        lambda *refs: first_kernel(tensors, *refs),
        out_shape=shape((h.shape[0], 3 * w.shape[1] + HD)),
        in_specs=[VMEM] * (tensors + 3),
        out_specs=VMEM,
        compiler_params=PARAMS,
        cost_estimate=cost(24 * w.size, 2 * w.size),
    )(lengths, h, *pieces, w)


def arrive(arrivals, following):
    width = following.shape[1]
    rest = arrivals[0][:, width:]
    came = tree_sum([arrival[:, :width] for arrival in arrivals]) + rest[:, :width].astype(F32)
    came = came.astype(BF).astype(F32)
    at_first = jnp.full(came.shape, lax.axis_index("section")) == 0
    carried = rest[:, width:].astype(F32) if rest.shape[1] > width else jnp.zeros_like(came)
    h = jnp.where(at_first, following.astype(F32), came)
    return h, jnp.where(at_first, came, carried)


def later_kernel(tensors, tick, lengths_ref, *refs):
    arrivals, next_ref = refs[:tensors], refs[tensors]
    pieces, (w_ref, out_ref, carry_ref) = refs[tensors + 1 : 2 * tensors + 1], refs[2 * tensors + 1 :]
    h, emitted = arrive(arrivals, next_ref[-tick % next_ref.shape[0]])
    width = h.shape[1]
    carry_ref[:, :width] = h.astype(BF)
    carry_ref[:, width:] = emitted.astype(BF)
    blocks = 2 * h.shape[0] * width // (pieces[0].shape[1] * HD)
    query_sums(tick * blocks, lengths_ref[tick : tick + 1], h, pieces, w_ref, out_ref)


def later_sums(tick, lengths, arrivals, following, pieces, w):
    tensors = len(pieces)
    rows, width = following.shape[1:]
    return pl.pallas_call(
        lambda *refs: later_kernel(tensors, tick, *refs),
        out_shape=[shape((rows, 3 * w.shape[1] + HD)), shape((rows, 2 * width))],
        in_specs=[VMEM] * (2 * tensors + 3),
        out_specs=[VMEM] * 2,
        compiler_params=PARAMS,
        cost_estimate=cost(24 * w.size, 2 * w.size),
    )(lengths, *arrivals, following, *pieces, w)


def last_kernel(tensors, *refs):
    state_ref, emitted_ref = refs[-2:]
    h, emitted = arrive(refs[:tensors], refs[tensors][0])
    state_ref[0] = h.astype(BF)
    emitted_ref[0] = emitted.astype(BF)


def last(arrivals, following):
    return pl.pallas_call(
        lambda *refs: last_kernel(len(arrivals), *refs),
        out_shape=[shape((1,) + following.shape[1:])] * 2,
        in_specs=[VMEM] * (len(arrivals) + 1),
        out_specs=[VMEM] * 2,
        compiler_params=PARAMS,
    )(*arrivals, following)


def attend_kernel(dims, turns, tick, *refs):
    sections, tensors, rows, kv_dev = dims
    count = len(turns)
    pieces, (carry_ref, w_ref), refs = refs[:count], refs[count : count + 2], refs[count + 2 :]
    caches, (out_ref, full_ref) = refs[:-2], refs[-2:]
    each = caches[0].shape[0] // tensors
    span = w_ref.shape[0]
    width = w_ref.shape[1]
    batch = batch_at(tick, sections)

    tails = [piece[:, 3 * span :].astype(F32) for piece in pieces]
    totals = [tail[:, 0:1] + tail[:, 1:2] + tail[:, 2:3] for tail in tails]
    squares = [tail[:, 3:4] + tail[:, 4:5] + tail[:, 5:6] for tail in tails]
    scale = 1.0 / (width * count)
    mean = tree_sum(totals) * scale
    rstd = lax.rsqrt(tree_sum(squares) * scale - mean * mean + 1e-05)
    query = tree_sum(
        [
            piece[:, :span].astype(F32)
            + (total * (1.0 / width) - mean) * piece[:, span : 2 * span].astype(F32)
            for piece, total in zip(pieces, totals)
        ]
    )
    query = rstd * query + tree_sum([piece[:, 2 * span : 3 * span] for piece in pieces])
    query = query.astype(BF).astype(F32)

    pos = caches[0].shape[2]
    tensor_at, replica_at = lax.axis_index("tensor"), lax.axis_index("replica")
    cols = lax.broadcasted_iota(jnp.int32, (rows, tensors * pos), 1)
    row = lax.broadcasted_iota(jnp.int32, (rows, tensors * pos), 0)
    spots = jnp.bitwise_xor(cols // pos, tensor_at) * pos + cols % pos
    spots = spots.astype(F32)
    keep = []
    for turn in turns:
        valid = jnp.logical_and(row == jnp.bitwise_xor(replica_at, turn), spots < tails[turn][:, 6:7])
        keep.append(jnp.where(valid, 0.0, -1e30))
    per_kv = span // HD // kv_dev
    keep = jnp.concatenate([jnp.concatenate(keep, 1)] * per_kv, 0)

    att = []
    for g in range(kv_dev):
        mine = jnp.concatenate(
            [query[:, h * HD : (h + 1) * HD] for h in range(g * per_kv, (g + 1) * per_kv)], 0
        ).astype(BF)
        keys, values = (
            jnp.concatenate(
                [
                    cache[i, (which * sections + batch) * kv_dev + g]
                    for cache in caches
                    for i in range(each * tensors)
                ],
                0,
            )
            for which in range(2)
        )
        scores = lax.dot_general(mine, keys, (((1,), (1,)), ((), ())), preferred_element_type=F32)
        scores = scores * (HD**-0.5) + keep
        probs = jnp.exp(scores - jnp.max(scores, axis=-1, keepdims=True))
        total = jnp.sum(probs, axis=-1, keepdims=True)
        got = jnp.dot(probs.astype(BF), values, preferred_element_type=F32) / total
        att += [got[h * rows : (h + 1) * rows] for h in range(per_kv)]
    att = jnp.concatenate(att, 1).astype(BF)
    for at in tiles(w_ref):
        got = jnp.dot(att, w_ref[:, at], preferred_element_type=F32).astype(BF)
        out_ref[:, at] = got
        full_ref[:, at] = got
    full_ref[:, width:] = carry_ref[...]


def attend(dims, turns, tick, pieces, caches, carry, w):
    rows, width = carry.shape[0], w.shape[1]
    return pl.pallas_call(
        lambda *refs: attend_kernel(dims, turns, tick, *refs),
        out_shape=[shape((rows, width)), shape((rows, width + carry.shape[1]))],
        in_specs=[VMEM] * (len(pieces) + len(caches) + 2),
        out_specs=[VMEM] * 2,
        compiler_params=PARAMS,
        cost_estimate=cost(8 * w.size, 2 * w.size),
    )(*pieces, carry, w, *caches)


def on_device(state, next_embed, tenant, lengths, gain, bias, wq, wo, keys, values):
    sections = lax.axis_size("section")
    tensors = lax.axis_size("tensor")
    replicas = lax.axis_size("replica")
    rows, width = state.shape[1:]
    heads_dev = wq.shape[2] // HD
    group = heads_dev * tensors // keys.shape[3]
    kv_dev = max(1, heads_dev // group)
    pos = keys.shape[4]
    dims = (sections, tensors, rows, heads_dev, group, kv_dev)

    *packs, carry, following, lengths = pack(
        dims,
        tenant,
        lengths.reshape(-1),
        gain[0],
        bias[0],
        keys[0, :, 0],
        values[0, :, 0],
        state[0],
        next_embed,
    )
    got = [packs[0]] + [swapped(packs[d], "tensor", d) for d in range(1, tensors)]
    wq_held, wo_held = hold(wq[0], wo[0], packs[0])

    blocks = 2 * rows * width // (pos * HD)
    kv = join(got, sections * blocks, [wq_held, wo_held])
    turns, bit = [0], replicas // 2
    caches, waiting = [kv], None
    if bit:
        waiting = swapped(kv, "replica", bit)
    arrivals = None
    for tick in range(sections):
        if tick == 0:
            sums = first_sums(lengths, carry, got, wq_held)
            while bit:
                turns = turns + [turn ^ bit for turn in turns]
                caches, bit = [kv, waiting], bit // 2
                if bit:
                    both = join(caches, 0, [sums])
                    kv = both.reshape((-1,) + both.shape[2:])
                    waiting = swapped(kv, "replica", bit)
        else:
            sums, carry = later_sums(tick, lengths, arrivals, following, got, wq_held)
        pieces = [sums] + [swapped(sums, "replica", d) for d in range(1, replicas)]
        out, full = attend(
            (sections, tensors, rows, kv_dev), turns, tick, pieces, caches, carry, wo_held
        )
        arrivals = [from_behind(full, 0)] + [from_behind(out, d) for d in range(1, tensors)]
    return tuple(last(arrivals, following))


def solution(mesh):
    in_specs = (
        P("section", None, "replica"),
        P(None, None, "replica"),
        P(),
        P(None, "replica"),
        P("section", "tensor", "replica"),
        P("section", "tensor", "replica"),
        P("section", "replica", "tensor"),
        P("section", "tensor", "replica"),
        P("section", None, "replica", None, "tensor", None),
        P("section", None, "replica", None, "tensor", None),
    )
    out_specs = (P("section", None, "replica"), P("section", None, "replica"))
    return jax.shard_map(
        on_device, mesh=mesh, in_specs=in_specs, out_specs=out_specs, check_vma=False
    )
```

```python
import jax
import jax.numpy as jnp
from jax import lax
from jax.experimental import pallas as pl
from jax.experimental.pallas import tpu as pltpu
from jax.sharding import PartitionSpec as P

HD = 128
BF = jnp.bfloat16
F32 = jnp.float32
VMEM = pl.BlockSpec(memory_space=pltpu.VMEM)
SMEM = pl.BlockSpec(memory_space=pltpu.SMEM)
HBM = pl.BlockSpec(memory_space=pltpu.HBM)
PARAMS = pltpu.CompilerParams(vmem_limit_bytes=12 * 1024 * 1024)


def in_hbm(x):
    return pltpu.with_memory_space_constraint(x, pltpu.HBM)


def shape(dims, dtype=BF):
    return jax.ShapeDtypeStruct(tuple(dims), dtype)


def cost(flops, size):
    return pl.CostEstimate(flops=flops, bytes_accessed=size, transcendentals=0)


def swapped(block, axis, bits):
    route = [(i, i ^ bits) for i in range(lax.axis_size(axis))]
    return lax.ppermute(block, axis, route)


def from_behind(block, bits):
    sections, tensors = lax.axis_size("section"), lax.axis_size("tensor")
    route = [
        (s * tensors + (t ^ bits), (s + 1) % sections * tensors + t)
        for s in range(sections)
        for t in range(tensors)
    ]
    return lax.ppermute(block, ("section", "tensor"), route)


def tree_sum(pieces):
    pieces = [piece.astype(F32) for piece in pieces]
    while len(pieces) > 1:
        pieces = [pieces[i] + pieces[i + 1] for i in range(0, len(pieces), 2)]
    return pieces[0]


def batch_at(tick, sections):
    return lax.rem(lax.axis_index("section") + (sections - tick), sections)


def pack_kernel(dims, *refs):
    sections, tensors, rows, heads_dev, group, kv_dev = dims
    sources, refs = refs[:8], refs[8:]
    packs, (h_ref, next_ref, lengths_ref) = refs[:tensors], refs[tensors : tensors + 3]
    ids, lengths, gains, biases, keys, values, sems = refs[tensors + 3 :]
    targets = (ids, lengths, keys, values, gains, biases, h_ref, next_ref)
    copies = [
        pltpu.make_async_copy(source, target, sems.at[i])
        for i, (source, target) in enumerate(zip(sources, targets))
    ]
    for copy in copies:
        copy.start()
    at = lax.axis_index("tensor")
    tenants = gains.shape[0]
    count = sections * rows
    spot = lax.broadcasted_iota(jnp.int32, (count, tenants), 0)
    line = lax.broadcasted_iota(jnp.int32, lengths_ref.shape, 0)
    wanted = jnp.zeros((count, tenants), jnp.int32)
    kept = jnp.zeros(lengths_ref.shape, jnp.int32)
    copies[0].wait()
    copies[1].wait()
    for tick in range(sections):
        batch = batch_at(tick, sections)
        kept = jnp.where(line == tick, lengths[batch], kept)
        for i in range(rows):
            wanted = jnp.where(spot == tick * rows + i, ids[batch, i], wanted)
    lengths_ref[...] = kept.astype(F32)
    wanted = wanted - at * tenants
    onehot = jnp.where(wanted == lax.broadcasted_iota(jnp.int32, (count, tenants), 1), 1.0, 0.0)
    onehot = onehot.astype(BF)
    copies[2].wait()
    copies[3].wait()
    pos, lanes = keys.shape[2:]
    width = gains.shape[1]
    per = pos // (2 * rows)
    blocks = width // lanes // per
    for d in range(tensors):
        start = lax.bitwise_xor(at, d) * heads_dev // group
        for which, cache in enumerate((keys, values)):
            for b in range(sections):
                for g in range(kv_dev):
                    to = sections * blocks + (which * sections + b) * kv_dev + g
                    packs[d][to] = cache[b, start + g]
    copies[4].wait()
    gain_rows = jnp.dot(onehot, gains[...], preferred_element_type=F32)
    copies[5].wait()
    bias_rows = jnp.dot(onehot, biases[...], preferred_element_type=F32)
    for tick in range(sections):
        mine = slice(tick * rows, (tick + 1) * rows)
        both = jnp.concatenate([gain_rows[mine], bias_rows[mine]], 0)
        for j in range(blocks):
            block = jnp.concatenate(
                [both[:, (j * per + k) * lanes : (j * per + k + 1) * lanes] for k in range(per)], 0
            ).astype(BF)
            for d in range(tensors):
                packs[d][tick * blocks + j] = block
    copies[6].wait()
    copies[7].wait()


def pack(dims, tenant, lengths, gain, bias, keys, values, h, following):
    sections, tensors, rows, heads_dev, group, kv_dev = dims
    pos = keys.shape[2]
    blocks = 2 * rows * gain.shape[1] // (pos * HD)
    out_shape = [shape((sections * (blocks + 2 * kv_dev), pos, HD))] * tensors
    out_shape += [shape(h.shape), shape(following.shape), shape((sections, HD), F32)]
    operands = (tenant, lengths, keys, values, gain, bias, h, following)
    return pl.pallas_call(
        lambda *refs: pack_kernel(dims, *refs),
        out_shape=out_shape,
        in_specs=[HBM] * len(operands),
        out_specs=[VMEM] * len(out_shape),
        scratch_shapes=[pltpu.SMEM(x.shape, jnp.int32) for x in (tenant, lengths)]
        + [pltpu.VMEM(x.shape, BF) for x in (gain, bias, keys, values)]
        + [pltpu.SemaphoreType.DMA((len(operands),))],
        compiler_params=PARAMS,
        cost_estimate=cost(0, 4 * gain.size),
    )(*[in_hbm(x) for x in operands])


def join_kernel(count, first, refs):
    out_ref = refs[-1]
    for i in range(count):
        out_ref[i] = refs[i][first:]


def join(pieces, first, after):
    count = len(pieces)
    dims = pieces[0].shape
    return pl.pallas_call(
        lambda *refs: join_kernel(count, first, refs),
        out_shape=shape((count, dims[0] - first) + dims[1:]),
        in_specs=[VMEM] * count + [pl.BlockSpec(memory_space=pl.ANY)] * len(after),
        out_specs=VMEM,
        compiler_params=PARAMS,
    )(*pieces, *after)


def hold_kernel(parts, after_ref, wq_ref, wo_ref, wq_out, wo_out, sems):
    copies = []
    for source, target in ((wq_ref, wq_out), (wo_ref, wo_out)):
        rows = source.shape[0] // parts
        for i in range(parts):
            at = pl.ds(i * rows, rows)
            copies.append(
                pltpu.make_async_copy(source.at[at], target.at[at], sems.at[len(copies)])
            )
    for copy in copies:
        copy.start()
    for copy in copies:
        copy.wait()


def hold(wq, wo, after):
    parts = 8
    return pl.pallas_call(
        lambda *refs: hold_kernel(parts, *refs),
        out_shape=[pltpu.VMEM(wq.shape, BF), pltpu.VMEM(wo.shape, BF)],
        in_specs=[pl.BlockSpec(memory_space=pl.ANY), HBM, HBM],
        out_specs=[VMEM] * 2,
        scratch_shapes=[pltpu.SemaphoreType.DMA((2 * parts,))],
        compiler_params=PARAMS,
        cost_estimate=cost(0, 4 * wq.size),
    )(after, in_hbm(wq), in_hbm(wo))


def tiles(w_ref):
    width = min(512, w_ref.shape[1])
    return [slice(i, i + width) for i in range(0, w_ref.shape[1], width)]


def thirds(x):
    high = x.astype(BF).astype(F32)
    middle = (x - high).astype(BF).astype(F32)
    return [high, middle, x - high - middle]


def query_sums(first_block, length, h, pieces, w_ref, out_ref):
    rows, width = h.shape
    pos, lanes = pieces[0].shape[1:]
    per = pos // (2 * rows)
    cols = []
    for j in range(width // lanes // per):
        block = tree_sum([piece[first_block + j] for piece in pieces])
        cols += [block[k * 2 * rows : (k + 1) * 2 * rows] for k in range(per)]
    affine = jnp.concatenate(cols, 1)
    total = jnp.sum(h, axis=-1, keepdims=True)
    squares = jnp.sum(h * h, axis=-1, keepdims=True)
    centred = (h - total * (1.0 / width)) * affine[:rows]
    x = jnp.concatenate([centred, affine], 0).astype(BF)
    count = w_ref.shape[1]
    for at in tiles(w_ref):
        got = jnp.dot(x, w_ref[:, at], preferred_element_type=F32)
        for k in range(3):
            to = slice(k * count + at.start, k * count + at.stop)
            out_ref[:, to] = got[k * rows : (k + 1) * rows].astype(BF)
    lane = lax.broadcasted_iota(jnp.int32, (rows, HD), 1)
    tail = jnp.broadcast_to(length, (rows, HD))
    for i, term in enumerate(thirds(total) + thirds(squares)):
        tail = jnp.where(lane == i, term, tail)
    out_ref[:, 3 * count :] = tail.astype(BF)


def first_kernel(tensors, lengths_ref, h_ref, *refs):
    pieces, (w_ref, out_ref) = refs[:tensors], refs[tensors:]
    query_sums(0, lengths_ref[0:1], h_ref[...].astype(F32), pieces, w_ref, out_ref)


def first_sums(lengths, h, pieces, w):
    tensors = len(pieces)
    return pl.pallas_call(
        lambda *refs: first_kernel(tensors, *refs),
        out_shape=shape((h.shape[0], 3 * w.shape[1] + HD)),
        in_specs=[VMEM] * (tensors + 3),
        out_specs=VMEM,
        compiler_params=PARAMS,
        cost_estimate=cost(24 * w.size, 2 * w.size),
    )(lengths, h, *pieces, w)


def arrive(arrivals, following):
    width = following.shape[1]
    rest = arrivals[0][:, width:]
    came = tree_sum([arrival[:, :width] for arrival in arrivals]) + rest[:, :width].astype(F32)
    came = came.astype(BF).astype(F32)
    at_first = jnp.full(came.shape, lax.axis_index("section")) == 0
    carried = rest[:, width:].astype(F32) if rest.shape[1] > width else jnp.zeros_like(came)
    h = jnp.where(at_first, following.astype(F32), came)
    return h, jnp.where(at_first, came, carried)


def later_kernel(count, tick, lengths_ref, *refs):
    arrivals, next_ref = refs[:count], refs[count]
    pieces, (w_ref, out_ref, carry_ref) = refs[count + 1 : -3], refs[-3:]
    h, emitted = arrive(arrivals, next_ref[-tick % next_ref.shape[0]])
    width = h.shape[1]
    carry_ref[:, :width] = h.astype(BF)
    carry_ref[:, width:] = emitted.astype(BF)
    blocks = 2 * h.shape[0] * width // (pieces[0].shape[1] * HD)
    query_sums(tick * blocks, lengths_ref[tick : tick + 1], h, pieces, w_ref, out_ref)


def later_sums(tick, lengths, arrivals, following, pieces, w):
    rows, width = following.shape[1:]
    return pl.pallas_call(
        lambda *refs: later_kernel(len(arrivals), tick, *refs),
        out_shape=[shape((rows, 3 * w.shape[1] + HD)), shape((rows, 2 * width))],
        in_specs=[VMEM] * (len(arrivals) + len(pieces) + 3),
        out_specs=[VMEM] * 2,
        compiler_params=PARAMS,
        cost_estimate=cost(24 * w.size, 2 * w.size),
    )(lengths, *arrivals, following, *pieces, w)


def last_kernel(count, *refs):
    state_ref, emitted_ref = refs[-2:]
    h, emitted = arrive(refs[:count], refs[count][0])
    state_ref[0] = h.astype(BF)
    emitted_ref[0] = emitted.astype(BF)


def last(arrivals, following):
    return pl.pallas_call(
        lambda *refs: last_kernel(len(arrivals), *refs),
        out_shape=[shape((1,) + following.shape[1:])] * 2,
        in_specs=[VMEM] * (len(arrivals) + 1),
        out_specs=[VMEM] * 2,
        compiler_params=PARAMS,
    )(*arrivals, following)


def attend_kernel(dims, turns, tick, *refs):
    sections, tensors, rows, kv_dev = dims
    count = len(turns)
    pieces, w_ref, caches, out_ref = refs[:count], refs[count], refs[count + 1 : -1], refs[-1]
    each = caches[0].shape[0] // tensors
    span = w_ref.shape[0]
    width = w_ref.shape[1]
    batch = batch_at(tick, sections)

    tails = [piece[:, 3 * span :].astype(F32) for piece in pieces]
    totals = [tail[:, 0:1] + tail[:, 1:2] + tail[:, 2:3] for tail in tails]
    squares = [tail[:, 3:4] + tail[:, 4:5] + tail[:, 5:6] for tail in tails]
    scale = 1.0 / (width * count)
    mean = tree_sum(totals) * scale
    rstd = lax.rsqrt(tree_sum(squares) * scale - mean * mean + 1e-05)
    query = tree_sum(
        [
            piece[:, :span].astype(F32)
            + (total * (1.0 / width) - mean) * piece[:, span : 2 * span].astype(F32)
            for piece, total in zip(pieces, totals)
        ]
    )
    query = rstd * query + tree_sum([piece[:, 2 * span : 3 * span] for piece in pieces])
    query = query.astype(BF).astype(F32)

    pos = caches[0].shape[2]
    tensor_at, replica_at = lax.axis_index("tensor"), lax.axis_index("replica")
    cols = lax.broadcasted_iota(jnp.int32, (rows, tensors * pos), 1)
    row = lax.broadcasted_iota(jnp.int32, (rows, tensors * pos), 0)
    spots = jnp.bitwise_xor(cols // pos, tensor_at) * pos + cols % pos
    spots = spots.astype(F32)
    keep = []
    for turn in turns:
        valid = jnp.logical_and(row == jnp.bitwise_xor(replica_at, turn), spots < tails[turn][:, 6:7])
        keep.append(jnp.where(valid, 0.0, -1e30))
    per_kv = span // HD // kv_dev
    keep = jnp.concatenate([jnp.concatenate(keep, 1)] * per_kv, 0)

    att = []
    for g in range(kv_dev):
        mine = jnp.concatenate(
            [query[:, h * HD : (h + 1) * HD] for h in range(g * per_kv, (g + 1) * per_kv)], 0
        ).astype(BF)
        keys, values = (
            jnp.concatenate(
                [
                    cache[i, (which * sections + batch) * kv_dev + g]
                    for cache in caches
                    for i in range(each * tensors)
                ],
                0,
            )
            for which in range(2)
        )
        scores = lax.dot_general(mine, keys, (((1,), (1,)), ((), ())), preferred_element_type=F32)
        scores = scores * (HD**-0.5) + keep
        probs = jnp.exp(scores - jnp.max(scores, axis=-1, keepdims=True))
        total = jnp.sum(probs, axis=-1, keepdims=True)
        got = jnp.dot(probs.astype(BF), values, preferred_element_type=F32) / total
        att += [got[h * rows : (h + 1) * rows] for h in range(per_kv)]
    att = jnp.concatenate(att, 1).astype(BF)
    for at in tiles(w_ref):
        out_ref[:, at] = jnp.dot(att, w_ref[:, at], preferred_element_type=F32).astype(BF)


def attend(dims, turns, tick, pieces, caches, w):
    return pl.pallas_call(
        lambda *refs: attend_kernel(dims, turns, tick, *refs),
        out_shape=shape((dims[2], w.shape[1])),
        in_specs=[VMEM] * (len(pieces) + len(caches) + 1),
        out_specs=VMEM,
        compiler_params=PARAMS,
        cost_estimate=cost(8 * w.size, 2 * w.size),
    )(*pieces, w, *caches)


def pair_kernel(mine_ref, other_ref, carry_ref, out_ref, full_ref):
    width = mine_ref.shape[1]
    both = (mine_ref[...].astype(F32) + other_ref[...].astype(F32)).astype(BF)
    out_ref[...] = both
    full_ref[:, :width] = both
    full_ref[:, width:] = carry_ref[...]


def pair(mine, other, carry):
    return pl.pallas_call(
        pair_kernel,
        out_shape=[shape(mine.shape), shape((mine.shape[0], mine.shape[1] + carry.shape[1]))],
        in_specs=[VMEM] * 3,
        out_specs=[VMEM] * 2,
        compiler_params=PARAMS,
    )(mine, other, carry)


def on_device(state, next_embed, tenant, lengths, gain, bias, wq, wo, keys, values):
    sections = lax.axis_size("section")
    tensors = lax.axis_size("tensor")
    replicas = lax.axis_size("replica")
    rows, width = state.shape[1:]
    heads_dev = wq.shape[2] // HD
    group = heads_dev * tensors // keys.shape[3]
    kv_dev = max(1, heads_dev // group)
    pos = keys.shape[4]
    dims = (sections, tensors, rows, heads_dev, group, kv_dev)

    *packs, carry, following, lengths = pack(
        dims,
        tenant,
        lengths.reshape(-1),
        gain[0],
        bias[0],
        keys[0, :, 0],
        values[0, :, 0],
        state[0],
        next_embed,
    )
    got = [packs[0]] + [swapped(packs[d], "tensor", d) for d in range(1, tensors)]
    wq_held, wo_held = hold(wq[0], wo[0], packs[0])

    blocks = 2 * rows * width // (pos * HD)
    kv = join(got, sections * blocks, [wq_held, wo_held])
    turns, bit = [0], replicas // 2
    caches, waiting = [kv], None
    if bit:
        waiting = swapped(kv, "replica", bit)
    arrivals = None
    for tick in range(sections):
        if tick == 0:
            sums = first_sums(lengths, carry, got, wq_held)
        else:
            sums, carry = later_sums(tick, lengths, arrivals, following, got, wq_held)
        pieces = [sums] + [swapped(sums, "replica", d) for d in range(1, replicas)]
        if tick == 0:
            while bit:
                turns = turns + [turn ^ bit for turn in turns]
                caches, bit = [kv, waiting], bit // 2
                if bit:
                    both = join(caches, 0, pieces[2:])
                    kv = both.reshape((-1,) + both.shape[2:])
                    waiting = swapped(kv, "replica", bit)
        out = attend((sections, tensors, rows, kv_dev), turns, tick, pieces, caches, wo_held)
        out, full = pair(out, swapped(out, "tensor", 1), carry)
        arrivals = [from_behind(full, 0)] + [from_behind(out, d) for d in range(2, tensors, 2)]
    return tuple(last(arrivals, following))


def solution(mesh):
    in_specs = (
        P("section", None, "replica"),
        P(None, None, "replica"),
        P(),
        P(None, "replica"),
        P("section", "tensor", "replica"),
        P("section", "tensor", "replica"),
        P("section", "replica", "tensor"),
        P("section", "tensor", "replica"),
        P("section", None, "replica", None, "tensor", None),
        P("section", None, "replica", None, "tensor", None),
    )
    out_specs = (P("section", None, "replica"), P("section", None, "replica"))
    return jax.shard_map(
        on_device, mesh=mesh, in_specs=in_specs, out_specs=out_specs, check_vma=False
    )
```

```python
import jax
import jax.numpy as jnp
from jax import lax
from jax.experimental import pallas as pl
from jax.experimental.pallas import tpu as pltpu
from jax.sharding import PartitionSpec as P

HD = 128
BF = jnp.bfloat16
F32 = jnp.float32
VMEM = pl.BlockSpec(memory_space=pltpu.VMEM)
SMEM = pl.BlockSpec(memory_space=pltpu.SMEM)
HBM = pl.BlockSpec(memory_space=pltpu.HBM)
PARAMS = pltpu.CompilerParams(vmem_limit_bytes=12 * 1024 * 1024)


def in_hbm(x):
    return pltpu.with_memory_space_constraint(x, pltpu.HBM)


def shape(dims, dtype=BF):
    return jax.ShapeDtypeStruct(tuple(dims), dtype)


def cost(flops, size):
    return pl.CostEstimate(flops=flops, bytes_accessed=size, transcendentals=0)


def swapped(block, axis, bits):
    route = [(i, i ^ bits) for i in range(lax.axis_size(axis))]
    return lax.ppermute(block, axis, route)


def from_behind(block, bits):
    sections, tensors = lax.axis_size("section"), lax.axis_size("tensor")
    route = [
        (s * tensors + (t ^ bits), (s + 1) % sections * tensors + t)
        for s in range(sections)
        for t in range(tensors)
    ]
    return lax.ppermute(block, ("section", "tensor"), route)


def tree_sum(pieces):
    pieces = [piece.astype(F32) for piece in pieces]
    while len(pieces) > 1:
        pieces = [pieces[i] + pieces[i + 1] for i in range(0, len(pieces), 2)]
    return pieces[0]


def batch_at(tick, sections):
    return lax.rem(lax.axis_index("section") + (sections - tick), sections)


def pack_kernel(dims, *refs):
    sections, tensors, rows, heads_dev, group, kv_dev = dims
    sources, refs = refs[:8], refs[8:]
    packs, (h_ref, next_ref, lengths_ref) = refs[:tensors], refs[tensors : tensors + 3]
    ids, lengths, gains, biases, keys, values, sems = refs[tensors + 3 :]
    targets = (ids, lengths, keys, values, gains, biases, h_ref, next_ref)
    copies = [
        pltpu.make_async_copy(source, target, sems.at[i])
        for i, (source, target) in enumerate(zip(sources, targets))
    ]
    for copy in copies:
        copy.start()
    at = lax.axis_index("tensor")
    tenants = gains.shape[0]
    count = sections * rows
    spot = lax.broadcasted_iota(jnp.int32, (count, tenants), 0)
    line = lax.broadcasted_iota(jnp.int32, lengths_ref.shape, 0)
    wanted = jnp.zeros((count, tenants), jnp.int32)
    kept = jnp.zeros(lengths_ref.shape, jnp.int32)
    copies[0].wait()
    copies[1].wait()
    for tick in range(sections):
        batch = batch_at(tick, sections)
        kept = jnp.where(line == tick, lengths[batch], kept)
        for i in range(rows):
            wanted = jnp.where(spot == tick * rows + i, ids[batch, i], wanted)
    lengths_ref[...] = kept.astype(F32)
    wanted = wanted - at * tenants
    onehot = jnp.where(wanted == lax.broadcasted_iota(jnp.int32, (count, tenants), 1), 1.0, 0.0)
    onehot = onehot.astype(BF)
    copies[2].wait()
    copies[3].wait()
    pos, lanes = keys.shape[2:]
    width = gains.shape[1]
    per = pos // (2 * rows)
    blocks = width // lanes // per
    for d in range(tensors):
        start = lax.bitwise_xor(at, d) * heads_dev // group
        for which, cache in enumerate((keys, values)):
            for b in range(sections):
                for g in range(kv_dev):
                    to = sections * blocks + (which * sections + b) * kv_dev + g
                    packs[d][to] = cache[b, start + g]
    copies[4].wait()
    gain_rows = jnp.dot(onehot, gains[...], preferred_element_type=F32)
    copies[5].wait()
    bias_rows = jnp.dot(onehot, biases[...], preferred_element_type=F32)
    for tick in range(sections):
        mine = slice(tick * rows, (tick + 1) * rows)
        both = jnp.concatenate([gain_rows[mine], bias_rows[mine]], 0)
        for j in range(blocks):
            block = jnp.concatenate(
                [both[:, (j * per + k) * lanes : (j * per + k + 1) * lanes] for k in range(per)], 0
            ).astype(BF)
            for d in range(tensors):
                packs[d][tick * blocks + j] = block
    copies[6].wait()
    copies[7].wait()


def pack(dims, tenant, lengths, gain, bias, keys, values, h, following):
    sections, tensors, rows, heads_dev, group, kv_dev = dims
    pos = keys.shape[2]
    blocks = 2 * rows * gain.shape[1] // (pos * HD)
    out_shape = [shape((sections * (blocks + 2 * kv_dev), pos, HD))] * tensors
    out_shape += [shape(h.shape), shape(following.shape), shape((sections, HD), F32)]
    operands = (tenant, lengths, keys, values, gain, bias, h, following)
    return pl.pallas_call(
        lambda *refs: pack_kernel(dims, *refs),
        out_shape=out_shape,
        in_specs=[HBM] * len(operands),
        out_specs=[VMEM] * len(out_shape),
        scratch_shapes=[pltpu.SMEM(x.shape, jnp.int32) for x in (tenant, lengths)]
        + [pltpu.VMEM(x.shape, BF) for x in (gain, bias, keys, values)]
        + [pltpu.SemaphoreType.DMA((len(operands),))],
        compiler_params=PARAMS,
        cost_estimate=cost(0, 4 * gain.size),
    )(*[in_hbm(x) for x in operands])


def join_kernel(count, first, refs):
    out_ref = refs[-1]
    for i in range(count):
        out_ref[i] = refs[i][first:]


def join(pieces, first, after):
    count = len(pieces)
    dims = pieces[0].shape
    return pl.pallas_call(
        lambda *refs: join_kernel(count, first, refs),
        out_shape=shape((count, dims[0] - first) + dims[1:]),
        in_specs=[VMEM] * count + [pl.BlockSpec(memory_space=pl.ANY)] * len(after),
        out_specs=VMEM,
        compiler_params=PARAMS,
    )(*pieces, *after)


def hold_kernel(parts, after_ref, wq_ref, wo_ref, wq_out, wo_out, sems):
    copies = []
    for source, target in ((wq_ref, wq_out), (wo_ref, wo_out)):
        rows = source.shape[0] // parts
        for i in range(parts):
            at = pl.ds(i * rows, rows)
            copies.append(
                pltpu.make_async_copy(source.at[at], target.at[at], sems.at[len(copies)])
            )
    for copy in copies:
        copy.start()
    for copy in copies:
        copy.wait()


def hold(wq, wo, after):
    parts = 8
    return pl.pallas_call(
        lambda *refs: hold_kernel(parts, *refs),
        out_shape=[pltpu.VMEM(wq.shape, BF), pltpu.VMEM(wo.shape, BF)],
        in_specs=[pl.BlockSpec(memory_space=pl.ANY), HBM, HBM],
        out_specs=[VMEM] * 2,
        scratch_shapes=[pltpu.SemaphoreType.DMA((2 * parts,))],
        compiler_params=PARAMS,
        cost_estimate=cost(0, 4 * wq.size),
    )(after, in_hbm(wq), in_hbm(wo))


def tiles(w_ref):
    width = min(512, w_ref.shape[1])
    return [slice(i, i + width) for i in range(0, w_ref.shape[1], width)]


def thirds(x):
    high = x.astype(BF).astype(F32)
    middle = (x - high).astype(BF).astype(F32)
    return [high, middle, x - high - middle]


def query_sums(first_block, length, h, pieces, w_ref, out_ref):
    rows, width = h.shape
    pos, lanes = pieces[0].shape[1:]
    per = pos // (2 * rows)
    cols = []
    for j in range(width // lanes // per):
        block = tree_sum([piece[first_block + j] for piece in pieces])
        cols += [block[k * 2 * rows : (k + 1) * 2 * rows] for k in range(per)]
    affine = jnp.concatenate(cols, 1)
    total = jnp.sum(h, axis=-1, keepdims=True)
    squares = jnp.sum(h * h, axis=-1, keepdims=True)
    centred = (h - total * (1.0 / width)) * affine[:rows]
    x = jnp.concatenate([centred, affine], 0).astype(BF)
    count = w_ref.shape[1]
    for at in tiles(w_ref):
        got = jnp.dot(x, w_ref[:, at], preferred_element_type=F32)
        for k in range(3):
            to = slice(k * count + at.start, k * count + at.stop)
            out_ref[:, to] = got[k * rows : (k + 1) * rows].astype(BF)
    lane = lax.broadcasted_iota(jnp.int32, (rows, HD), 1)
    tail = jnp.broadcast_to(length, (rows, HD))
    for i, term in enumerate(thirds(total) + thirds(squares)):
        tail = jnp.where(lane == i, term, tail)
    out_ref[:, 3 * count :] = tail.astype(BF)


def first_kernel(tensors, lengths_ref, h_ref, *refs):
    pieces, (w_ref, out_ref) = refs[:tensors], refs[tensors:]
    query_sums(0, lengths_ref[0:1], h_ref[...].astype(F32), pieces, w_ref, out_ref)


def first_sums(lengths, h, pieces, w):
    tensors = len(pieces)
    return pl.pallas_call(
        lambda *refs: first_kernel(tensors, *refs),
        out_shape=shape((h.shape[0], 3 * w.shape[1] + HD)),
        in_specs=[VMEM] * (tensors + 3),
        out_specs=VMEM,
        compiler_params=PARAMS,
        cost_estimate=cost(24 * w.size, 2 * w.size),
    )(lengths, h, *pieces, w)


def arrive(arrivals, following, tick):
    sections, rows, width = following.shape
    rest = arrivals[0][:, width:].astype(F32)
    section = jnp.full((rows, width), lax.axis_index("section"))
    left, carried = rest[:, :width], jnp.zeros((rows, width), F32)
    if sections == 2 and tick > 0:
        left = jnp.where(section == 1, following[-tick % sections].astype(F32), rest)
        carried = rest
    elif tick > 0:
        carried = rest[:, width:]
    came = tree_sum([arrival[:, :width] for arrival in arrivals]) + left
    came = came.astype(BF).astype(F32)
    h = jnp.where(section == 0, following[-(tick + 1) % sections].astype(F32), came)
    return h, jnp.where(section == 0, came, carried)


def later_kernel(count, tick, lengths_ref, *refs):
    arrivals, next_ref = refs[:count], refs[count]
    pieces, (w_ref, out_ref, carry_ref) = refs[count + 1 : -3], refs[-3:]
    h, emitted = arrive(arrivals, next_ref, tick - 1)
    width = h.shape[1]
    if carry_ref.shape[1] == width:
        first = jnp.full(h.shape, lax.axis_index("section")) == 0
        carry_ref[...] = jnp.where(first, emitted, h).astype(BF)
    else:
        carry_ref[:, :width] = h.astype(BF)
        carry_ref[:, width:] = emitted.astype(BF)
    blocks = 2 * h.shape[0] * width // (pieces[0].shape[1] * HD)
    query_sums(tick * blocks, lengths_ref[tick : tick + 1], h, pieces, w_ref, out_ref)


def later_sums(tick, lengths, arrivals, following, pieces, w):
    rows, width = following.shape[1:]
    parts = 1 if following.shape[0] == 2 else 2
    return pl.pallas_call(
        lambda *refs: later_kernel(len(arrivals), tick, *refs),
        out_shape=[shape((rows, 3 * w.shape[1] + HD)), shape((rows, width * parts))],
        in_specs=[VMEM] * (len(arrivals) + len(pieces) + 3),
        out_specs=[VMEM] * 2,
        compiler_params=PARAMS,
        cost_estimate=cost(24 * w.size, 2 * w.size),
    )(lengths, *arrivals, following, *pieces, w)


def last_kernel(count, *refs):
    state_ref, emitted_ref = refs[-2:]
    h, emitted = arrive(refs[:count], refs[count], refs[count].shape[0] - 1)
    state_ref[0] = h.astype(BF)
    emitted_ref[0] = emitted.astype(BF)


def last(arrivals, following):
    return pl.pallas_call(
        lambda *refs: last_kernel(len(arrivals), *refs),
        out_shape=[shape((1,) + following.shape[1:])] * 2,
        in_specs=[VMEM] * (len(arrivals) + 1),
        out_specs=[VMEM] * 2,
        compiler_params=PARAMS,
    )(*arrivals, following)


def attend_kernel(dims, turns, tick, *refs):
    sections, tensors, rows, kv_dev = dims
    count = len(turns)
    pieces, (carry_ref, w_ref), refs = refs[:count], refs[count : count + 2], refs[count + 2 :]
    caches, (out_ref, full_ref) = refs[:-2], refs[-2:]
    each = caches[0].shape[0] // tensors
    span = w_ref.shape[0]
    width = w_ref.shape[1]
    batch = batch_at(tick, sections)

    tails = [piece[:, 3 * span :].astype(F32) for piece in pieces]
    totals = [tail[:, 0:1] + tail[:, 1:2] + tail[:, 2:3] for tail in tails]
    squares = [tail[:, 3:4] + tail[:, 4:5] + tail[:, 5:6] for tail in tails]
    scale = 1.0 / (width * count)
    mean = tree_sum(totals) * scale
    rstd = lax.rsqrt(tree_sum(squares) * scale - mean * mean + 1e-05)
    query = tree_sum(
        [
            piece[:, :span].astype(F32)
            + (total * (1.0 / width) - mean) * piece[:, span : 2 * span].astype(F32)
            for piece, total in zip(pieces, totals)
        ]
    )
    query = rstd * query + tree_sum([piece[:, 2 * span : 3 * span] for piece in pieces])
    query = query.astype(BF).astype(F32)

    pos = caches[0].shape[2]
    tensor_at, replica_at = lax.axis_index("tensor"), lax.axis_index("replica")
    cols = lax.broadcasted_iota(jnp.int32, (rows, tensors * pos), 1)
    row = lax.broadcasted_iota(jnp.int32, (rows, tensors * pos), 0)
    spots = jnp.bitwise_xor(cols // pos, tensor_at) * pos + cols % pos
    spots = spots.astype(F32)
    keep = []
    for turn in turns:
        valid = jnp.logical_and(row == jnp.bitwise_xor(replica_at, turn), spots < tails[turn][:, 6:7])
        keep.append(jnp.where(valid, 0.0, -1e30))
    per_kv = span // HD // kv_dev
    keep = jnp.concatenate([jnp.concatenate(keep, 1)] * per_kv, 0)

    sums = [0.0] * len(tiles(w_ref))
    for g in range(kv_dev):
        mine = jnp.concatenate(
            [query[:, h * HD : (h + 1) * HD] for h in range(g * per_kv, (g + 1) * per_kv)], 0
        ).astype(BF)
        keys, values = (
            jnp.concatenate(
                [
                    cache[i, (which * sections + batch) * kv_dev + g]
                    for cache in caches
                    for i in range(each * tensors)
                ],
                0,
            )
            for which in range(2)
        )
        scores = lax.dot_general(mine, keys, (((1,), (1,)), ((), ())), preferred_element_type=F32)
        scores = scores * (HD**-0.5) + keep
        probs = jnp.exp(scores - jnp.max(scores, axis=-1, keepdims=True))
        total = jnp.sum(probs, axis=-1, keepdims=True)
        got = jnp.dot(probs.astype(BF), values, preferred_element_type=F32) / total
        att = jnp.concatenate([got[h * rows : (h + 1) * rows] for h in range(per_kv)], 1)
        att = att.astype(BF)
        depth = slice(g * per_kv * HD, (g + 1) * per_kv * HD)
        for i, at in enumerate(tiles(w_ref)):
            sums[i] += jnp.dot(att, w_ref[depth, at], preferred_element_type=F32)
    for got, at in zip(sums, tiles(w_ref)):
        out_ref[:, at] = got.astype(BF)
        full_ref[:, at] = got.astype(BF)
    full_ref[:, width:] = carry_ref[...]


def attend(dims, turns, tick, pieces, caches, carry, w):
    rows, width = carry.shape[0], w.shape[1]
    return pl.pallas_call(
        lambda *refs: attend_kernel(dims, turns, tick, *refs),
        out_shape=[shape((rows, width)), shape((rows, width + carry.shape[1]))],
        in_specs=[VMEM] * (len(pieces) + len(caches) + 2),
        out_specs=[VMEM] * 2,
        compiler_params=PARAMS,
        cost_estimate=cost(8 * w.size, 2 * w.size),
    )(*pieces, carry, w, *caches)


def on_device(state, next_embed, tenant, lengths, gain, bias, wq, wo, keys, values):
    sections = lax.axis_size("section")
    tensors = lax.axis_size("tensor")
    replicas = lax.axis_size("replica")
    rows, width = state.shape[1:]
    heads_dev = wq.shape[2] // HD
    group = heads_dev * tensors // keys.shape[3]
    kv_dev = max(1, heads_dev // group)
    pos = keys.shape[4]
    dims = (sections, tensors, rows, heads_dev, group, kv_dev)

    *packs, carry, following, lengths = pack(
        dims,
        tenant,
        lengths.reshape(-1),
        gain[0],
        bias[0],
        keys[0, :, 0],
        values[0, :, 0],
        state[0],
        next_embed,
    )
    got = [packs[0]] + [swapped(packs[d], "tensor", d) for d in range(1, tensors)]
    wq_held, wo_held = hold(wq[0], wo[0], packs[0])

    blocks = 2 * rows * width // (pos * HD)
    kv = join(got, sections * blocks, [wq_held, wo_held])
    turns, bit = [0], replicas // 2
    caches, waiting = [kv], None
    if bit:
        waiting = swapped(kv, "replica", bit)
    arrivals = None
    for tick in range(sections):
        if tick == 0:
            sums = first_sums(lengths, carry, got, wq_held)
        else:
            sums, carry = later_sums(tick, lengths, arrivals, following, got, wq_held)
        pieces = [sums] + [swapped(sums, "replica", d) for d in range(1, replicas)]
        if tick == 0:
            while bit:
                turns = turns + [turn ^ bit for turn in turns]
                caches, bit = [kv, waiting], bit // 2
                if bit:
                    both = join(caches, 0, pieces[2:])
                    kv = both.reshape((-1,) + both.shape[2:])
                    waiting = swapped(kv, "replica", bit)
        out, full = attend(
            (sections, tensors, rows, kv_dev), turns, tick, pieces, caches, carry, wo_held
        )
        arrivals = [from_behind(full, 0)] + [from_behind(out, d) for d in range(1, tensors)]
    return tuple(last(arrivals, following))


def solution(mesh):
    in_specs = (
        P("section", None, "replica"),
        P(None, None, "replica"),
        P(),
        P(None, "replica"),
        P("section", "tensor", "replica"),
        P("section", "tensor", "replica"),
        P("section", "replica", "tensor"),
        P("section", "tensor", "replica"),
        P("section", None, "replica", None, "tensor", None),
        P("section", None, "replica", None, "tensor", None),
    )
    out_specs = (P("section", None, "replica"), P("section", None, "replica"))
    return jax.shard_map(
        on_device, mesh=mesh, in_specs=in_specs, out_specs=out_specs, check_vma=False
    )
```

```python
import jax
import jax.numpy as jnp
from jax import lax
from jax.experimental import pallas as pl
from jax.experimental.pallas import tpu as pltpu
from jax.sharding import PartitionSpec as P

HD = 128
BF = jnp.bfloat16
F32 = jnp.float32
VMEM = pl.BlockSpec(memory_space=pltpu.VMEM)
SMEM = pl.BlockSpec(memory_space=pltpu.SMEM)
HBM = pl.BlockSpec(memory_space=pltpu.HBM)
PARAMS = pltpu.CompilerParams(vmem_limit_bytes=12 * 1024 * 1024)


def in_hbm(x):
    return pltpu.with_memory_space_constraint(x, pltpu.HBM)


def shape(dims, dtype=BF):
    return jax.ShapeDtypeStruct(tuple(dims), dtype)


def cost(flops, size):
    return pl.CostEstimate(flops=flops, bytes_accessed=size, transcendentals=0)


def swapped(block, axis, bits):
    route = [(i, i ^ bits) for i in range(lax.axis_size(axis))]
    return lax.ppermute(block, axis, route)


def from_behind(block, bits):
    sections, tensors = lax.axis_size("section"), lax.axis_size("tensor")
    route = [
        (s * tensors + (t ^ bits), (s + 1) % sections * tensors + t)
        for s in range(sections)
        for t in range(tensors)
    ]
    return lax.ppermute(block, ("section", "tensor"), route)


def tree_sum(pieces):
    pieces = [piece.astype(F32) for piece in pieces]
    while len(pieces) > 1:
        pieces = [pieces[i] + pieces[i + 1] for i in range(0, len(pieces), 2)]
    return pieces[0]


def batch_at(tick, sections):
    return lax.rem(lax.axis_index("section") + (sections - tick), sections)


def pack_kernel(dims, *refs):
    sections, tensors, rows, heads_dev, group, kv_dev = dims
    sources, refs = refs[:8], refs[8:]
    packs, (h_ref, next_ref, facts_ref) = refs[:tensors], refs[tensors : tensors + 3]
    ids, lengths, gains, biases, keys, values, sems = refs[tensors + 3 :]
    targets = (ids, lengths, keys, values, gains, biases, h_ref, next_ref)
    copies = [
        pltpu.make_async_copy(source, target, sems.at[i])
        for i, (source, target) in enumerate(zip(sources, targets))
    ]
    for copy in copies:
        copy.start()
    at = lax.axis_index("tensor")
    tenants = gains.shape[0]
    count = sections * rows
    spot = lax.broadcasted_iota(jnp.int32, (count, tenants), 0)
    lane = lax.broadcasted_iota(jnp.int32, facts_ref.shape, 1)
    wanted = jnp.zeros((count, tenants), jnp.int32)
    facts = jnp.zeros(facts_ref.shape, jnp.int32)
    copies[0].wait()
    copies[1].wait()
    for tick in range(sections):
        batch = batch_at(tick, sections)
        facts = jnp.where(lane == tick + 2, lengths[batch], facts)
        for i in range(rows):
            wanted = jnp.where(spot == tick * rows + i, ids[batch, i], wanted)
    wanted = wanted - at * tenants
    onehot = jnp.where(wanted == lax.broadcasted_iota(jnp.int32, (count, tenants), 1), 1.0, 0.0)
    onehot = onehot.astype(BF)
    copies[2].wait()
    copies[3].wait()
    pos, lanes = keys.shape[2:]
    width = gains.shape[1]
    per = pos // (2 * rows)
    blocks = width // lanes // per
    for d in range(tensors):
        start = lax.bitwise_xor(at, d) * heads_dev // group
        for which, cache in enumerate((keys, values)):
            for b in range(sections):
                for g in range(kv_dev):
                    to = sections * blocks + (which * sections + b) * kv_dev + g
                    packs[d][to] = cache[b, start + g]
    copies[4].wait()
    gain_rows = jnp.dot(onehot, gains[...], preferred_element_type=F32)
    copies[5].wait()
    bias_rows = jnp.dot(onehot, biases[...], preferred_element_type=F32)
    for tick in range(sections):
        mine = slice(tick * rows, (tick + 1) * rows)
        both = jnp.concatenate([gain_rows[mine], bias_rows[mine]], 0)
        for j in range(blocks):
            block = jnp.concatenate(
                [both[:, (j * per + k) * lanes : (j * per + k + 1) * lanes] for k in range(per)], 0
            ).astype(BF)
            for d in range(tensors):
                packs[d][tick * blocks + j] = block
    copies[6].wait()
    h = h_ref[...].astype(F32)
    facts = jnp.where(lane == 0, jnp.sum(h, axis=-1, keepdims=True), facts.astype(F32))
    facts_ref[...] = jnp.where(lane == 1, jnp.sum(h * h, axis=-1, keepdims=True), facts)
    copies[7].wait()


def pack(dims, tenant, lengths, gain, bias, keys, values, h, following):
    sections, tensors, rows, heads_dev, group, kv_dev = dims
    pos = keys.shape[2]
    blocks = 2 * rows * gain.shape[1] // (pos * HD)
    out_shape = [shape((sections * (blocks + 2 * kv_dev), pos, HD))] * tensors
    out_shape += [shape(h.shape), shape(following.shape), shape((rows, HD), F32)]
    operands = (tenant, lengths, keys, values, gain, bias, h, following)
    return pl.pallas_call(
        lambda *refs: pack_kernel(dims, *refs),
        out_shape=out_shape,
        in_specs=[HBM] * len(operands),
        out_specs=[VMEM] * len(out_shape),
        scratch_shapes=[pltpu.SMEM(x.shape, jnp.int32) for x in (tenant, lengths)]
        + [pltpu.VMEM(x.shape, BF) for x in (gain, bias, keys, values)]
        + [pltpu.SemaphoreType.DMA((len(operands),))],
        compiler_params=PARAMS,
        cost_estimate=cost(0, 4 * gain.size),
    )(*[in_hbm(x) for x in operands])


def join_kernel(count, first, refs):
    out_ref = refs[-1]
    for i in range(count):
        out_ref[i] = refs[i][first:]


def join(pieces, first, after):
    count = len(pieces)
    dims = pieces[0].shape
    return pl.pallas_call(
        lambda *refs: join_kernel(count, first, refs),
        out_shape=shape((count, dims[0] - first) + dims[1:], pieces[0].dtype),
        in_specs=[VMEM] * count + [pl.BlockSpec(memory_space=pl.ANY)] * len(after),
        out_specs=VMEM,
        compiler_params=PARAMS,
    )(*pieces, *after)


def hold_kernel(parts, after_ref, w_ref, out_ref, sems):
    rows = w_ref.shape[0] // parts
    copies = [
        pltpu.make_async_copy(
            w_ref.at[pl.ds(i * rows, rows)], out_ref.at[pl.ds(i * rows, rows)], sems.at[i]
        )
        for i in range(parts)
    ]
    for copy in copies:
        copy.start()
    for copy in copies:
        copy.wait()


def hold(w, after):
    parts = 8
    return pl.pallas_call(
        lambda *refs: hold_kernel(parts, *refs),
        out_shape=pltpu.VMEM(w.shape, BF),
        in_specs=[pl.BlockSpec(memory_space=pl.ANY), HBM],
        out_specs=VMEM,
        scratch_shapes=[pltpu.SemaphoreType.DMA((parts,))],
        compiler_params=PARAMS,
        cost_estimate=cost(0, 2 * w.size),
    )(after, in_hbm(w))


def tiles(w_ref):
    width = min(512, w_ref.shape[1])
    return [slice(i, i + width) for i in range(0, w_ref.shape[1], width)]


def thirds(x):
    high = x.astype(BF).astype(F32)
    middle = (x - high).astype(BF).astype(F32)
    return [high, middle, x - high - middle]


def affine_rows(first_block, rows, width, pieces):
    pos, lanes = pieces[0].shape[1:]
    per = pos // (2 * rows)
    cols = []
    for j in range(width // lanes // per):
        block = tree_sum([piece[first_block + j] for piece in pieces])
        cols += [block[k * 2 * rows : (k + 1) * 2 * rows] for k in range(per)]
    return jnp.concatenate(cols, 1)


def scales(total, squares, width):
    mean = total * (1.0 / width)
    return mean, lax.rsqrt(squares * (1.0 / width) - mean * mean + 1e-05)


def query_sums(first_block, h, pieces, w_ref, out_ref):
    rows, width = h.shape
    affine = affine_rows(first_block, rows, width, pieces)
    total = jnp.sum(h, axis=-1, keepdims=True)
    squares = jnp.sum(h * h, axis=-1, keepdims=True)
    centred = (h - total * (1.0 / width)) * affine[:rows]
    x = jnp.concatenate([centred, affine], 0).astype(BF)
    count = w_ref.shape[1]
    for at in tiles(w_ref):
        got = jnp.dot(x, w_ref[:, at], preferred_element_type=F32)
        for k in range(3):
            to = slice(k * count + at.start, k * count + at.stop)
            out_ref[:, to] = got[k * rows : (k + 1) * rows].astype(BF)
    lane = lax.broadcasted_iota(jnp.int32, (rows, HD), 1)
    tail = jnp.zeros((rows, HD), F32)
    for i, term in enumerate(thirds(total) + thirds(squares)):
        tail = jnp.where(lane == i, term, tail)
    out_ref[:, 3 * count :] = tail.astype(BF)


def first_kernel(tensors, h_ref, *refs):
    pieces, facts, (w_ref, out_ref) = refs[:tensors], refs[tensors:-2], refs[-2:]
    rows, width = h_ref.shape
    facts = [ref[i] for ref in facts for i in range(ref.shape[0])]
    facts = tree_sum(facts)
    replicas = lax.axis_size("replica")
    mean, rstd = scales(facts[:, 0:1], facts[:, 1:2], width * replicas)
    affine = affine_rows(0, rows, width, pieces)
    x = (h_ref[...].astype(F32) - mean) * rstd * affine[:rows] + affine[rows:]
    x = x.astype(BF)
    for at in tiles(w_ref):
        out_ref[:, at] = jnp.dot(x, w_ref[:, at], preferred_element_type=F32).astype(BF)


def first_sums(h, pieces, facts, w):
    tensors = len(pieces)
    return pl.pallas_call(
        lambda *refs: first_kernel(tensors, *refs),
        out_shape=shape((h.shape[0], w.shape[1])),
        in_specs=[VMEM] * (tensors + len(facts) + 2),
        out_specs=VMEM,
        compiler_params=PARAMS,
        cost_estimate=cost(24 * w.size, 2 * w.size),
    )(h, *pieces, *facts, w)


def arrive(arrivals, following, tick):
    sections, rows, width = following.shape
    rest = arrivals[0][:, width:].astype(F32)
    section = jnp.full((rows, width), lax.axis_index("section"))
    left, carried = rest[:, :width], jnp.zeros((rows, width), F32)
    if sections == 2 and tick > 0:
        left = jnp.where(section == 1, following[-tick % sections].astype(F32), rest)
        carried = rest
    elif tick > 0:
        carried = rest[:, width:]
    came = tree_sum([arrival[:, :width] for arrival in arrivals]) + left
    came = came.astype(BF).astype(F32)
    h = jnp.where(section == 0, following[-(tick + 1) % sections].astype(F32), came)
    return h, jnp.where(section == 0, came, carried)


def later_kernel(count, tick, *refs):
    arrivals, next_ref = refs[:count], refs[count]
    pieces, (w_ref, out_ref, carry_ref) = refs[count + 1 : -3], refs[-3:]
    h, emitted = arrive(arrivals, next_ref, tick - 1)
    width = h.shape[1]
    if carry_ref.shape[1] == width:
        first = jnp.full(h.shape, lax.axis_index("section")) == 0
        carry_ref[...] = jnp.where(first, emitted, h).astype(BF)
    else:
        carry_ref[:, :width] = h.astype(BF)
        carry_ref[:, width:] = emitted.astype(BF)
    blocks = 2 * h.shape[0] * width // (pieces[0].shape[1] * HD)
    query_sums(tick * blocks, h, pieces, w_ref, out_ref)


def later_sums(tick, arrivals, following, pieces, w):
    rows, width = following.shape[1:]
    parts = 1 if following.shape[0] == 2 else 2
    return pl.pallas_call(
        lambda *refs: later_kernel(len(arrivals), tick, *refs),
        out_shape=[shape((rows, 3 * w.shape[1] + HD)), shape((rows, width * parts))],
        in_specs=[VMEM] * (len(arrivals) + len(pieces) + 2),
        out_specs=[VMEM] * 2,
        compiler_params=PARAMS,
        cost_estimate=cost(24 * w.size, 2 * w.size),
    )(*arrivals, following, *pieces, w)


def last_kernel(count, *refs):
    state_ref, emitted_ref = refs[-2:]
    h, emitted = arrive(refs[:count], refs[count], refs[count].shape[0] - 1)
    state_ref[0] = h.astype(BF)
    emitted_ref[0] = emitted.astype(BF)


def last(arrivals, following):
    return pl.pallas_call(
        lambda *refs: last_kernel(len(arrivals), *refs),
        out_shape=[shape((1,) + following.shape[1:])] * 2,
        in_specs=[VMEM] * (len(arrivals) + 1),
        out_specs=[VMEM] * 2,
        compiler_params=PARAMS,
    )(*arrivals, following)


def attend_kernel(dims, turns, tick, *refs):
    sections, tensors, rows, kv_dev = dims
    count = len(turns)
    pieces, (carry_ref, w_ref), refs = refs[:count], refs[count : count + 2], refs[count + 2 :]
    (out_ref, full_ref), refs = refs[-2:], refs[:-2]
    caches, facts = refs[: len(refs) // 2], refs[len(refs) // 2 :]
    each = caches[0].shape[0] // tensors
    facts = [ref[i] for ref in facts for i in range(ref.shape[0])]
    span = w_ref.shape[0]
    width = w_ref.shape[1]
    batch = batch_at(tick, sections)

    if tick == 0:
        query = tree_sum([piece[...] for piece in pieces])
    else:
        tails = [piece[:, 3 * span :].astype(F32) for piece in pieces]
        totals = [tail[:, 0:1] + tail[:, 1:2] + tail[:, 2:3] for tail in tails]
        squares = [tail[:, 3:4] + tail[:, 4:5] + tail[:, 5:6] for tail in tails]
        mean, rstd = scales(tree_sum(totals), tree_sum(squares), width * count)
        query = tree_sum(
            [
                piece[:, :span].astype(F32)
                + (total * (1.0 / width) - mean) * piece[:, span : 2 * span].astype(F32)
                for piece, total in zip(pieces, totals)
            ]
        )
        query = rstd * query + tree_sum([piece[:, 2 * span : 3 * span] for piece in pieces])
    query = query.astype(BF).astype(F32)

    pos = caches[0].shape[2]
    tensor_at, replica_at = lax.axis_index("tensor"), lax.axis_index("replica")
    cols = lax.broadcasted_iota(jnp.int32, (rows, tensors * pos), 1)
    row = lax.broadcasted_iota(jnp.int32, (rows, tensors * pos), 0)
    spots = jnp.bitwise_xor(cols // pos, tensor_at) * pos + cols % pos
    spots = spots.astype(F32)
    keep = []
    for turn, fact in zip(turns, facts):
        length = fact[:, tick + 2 : tick + 3]
        valid = jnp.logical_and(row == jnp.bitwise_xor(replica_at, turn), spots < length)
        keep.append(jnp.where(valid, 0.0, -1e30))
    per_kv = span // HD // kv_dev
    keep = jnp.concatenate([jnp.concatenate(keep, 1)] * per_kv, 0)

    att = []
    for g in range(kv_dev):
        mine = jnp.concatenate(
            [query[:, h * HD : (h + 1) * HD] for h in range(g * per_kv, (g + 1) * per_kv)], 0
        ).astype(BF)
        keys, values = (
            jnp.concatenate(
                [
                    cache[i, (which * sections + batch) * kv_dev + g]
                    for cache in caches
                    for i in range(each * tensors)
                ],
                0,
            )
            for which in range(2)
        )
        scores = lax.dot_general(mine, keys, (((1,), (1,)), ((), ())), preferred_element_type=F32)
        scores = scores * (HD**-0.5) + keep
        probs = jnp.exp(scores - jnp.max(scores, axis=-1, keepdims=True))
        total = jnp.sum(probs, axis=-1, keepdims=True)
        got = jnp.dot(probs.astype(BF), values, preferred_element_type=F32) / total
        att += [got[h * rows : (h + 1) * rows] for h in range(per_kv)]
    att = jnp.concatenate(att, 1).astype(BF)
    for at in tiles(w_ref):
        got = jnp.dot(att, w_ref[:, at], preferred_element_type=F32).astype(BF)
        out_ref[:, at] = got
        full_ref[:, at] = got
    full_ref[:, width:] = carry_ref[...]


def attend(dims, turns, tick, pieces, caches, facts, carry, w):
    rows, width = carry.shape[0], w.shape[1]
    return pl.pallas_call(
        lambda *refs: attend_kernel(dims, turns, tick, *refs),
        out_shape=[shape((rows, width)), shape((rows, width + carry.shape[1]))],
        in_specs=[VMEM] * (len(pieces) + len(caches) + len(facts) + 2),
        out_specs=[VMEM] * 2,
        compiler_params=PARAMS,
        cost_estimate=cost(8 * w.size, 2 * w.size),
    )(*pieces, carry, w, *caches, *facts)


def on_device(state, next_embed, tenant, lengths, gain, bias, wq, wo, keys, values):
    sections = lax.axis_size("section")
    tensors = lax.axis_size("tensor")
    replicas = lax.axis_size("replica")
    rows, width = state.shape[1:]
    heads_dev = wq.shape[2] // HD
    group = heads_dev * tensors // keys.shape[3]
    kv_dev = max(1, heads_dev // group)
    pos = keys.shape[4]
    dims = (sections, tensors, rows, heads_dev, group, kv_dev)

    *packs, carry, following, facts = pack(
        dims,
        tenant,
        lengths.reshape(-1),
        gain[0],
        bias[0],
        keys[0, :, 0],
        values[0, :, 0],
        state[0],
        next_embed,
    )
    got = [packs[0]] + [swapped(packs[d], "tensor", d) for d in range(1, tensors)]
    wq_held = hold(wq[0], packs[0])

    facts = [facts[None]]
    bit = replicas // 2
    while bit:
        if len(facts) > 1:
            both = join(facts, 0, [wq_held])
            facts = [both.reshape((-1,) + both.shape[2:])]
        facts = [facts[0], swapped(facts[0], "replica", bit)]
        bit //= 2

    wo_held = hold(wo[0], facts[0])

    blocks = 2 * rows * width // (pos * HD)
    kv = join(got, sections * blocks, [wo_held, facts[-1]])
    turns, bit = [0], replicas // 2
    caches, waiting = [kv], None
    if bit:
        waiting = swapped(kv, "replica", bit)
    arrivals = None
    for tick in range(sections):
        if tick == 0:
            sums = first_sums(carry, got, facts, wq_held)
        else:
            sums, carry = later_sums(tick, arrivals, following, got, wq_held)
        pieces = [sums] + [swapped(sums, "replica", d) for d in range(1, replicas)]
        if tick == 0:
            while bit:
                turns = turns + [turn ^ bit for turn in turns]
                caches, bit = [kv, waiting], bit // 2
                if bit:
                    both = join(caches, 0, pieces[2:])
                    kv = both.reshape((-1,) + both.shape[2:])
                    waiting = swapped(kv, "replica", bit)
        out, full = attend(
            (sections, tensors, rows, kv_dev), turns, tick, pieces, caches, facts, carry, wo_held
        )
        arrivals = [from_behind(full, 0)] + [from_behind(out, d) for d in range(1, tensors)]
    return tuple(last(arrivals, following))


def solution(mesh):
    in_specs = (
        P("section", None, "replica"),
        P(None, None, "replica"),
        P(),
        P(None, "replica"),
        P("section", "tensor", "replica"),
        P("section", "tensor", "replica"),
        P("section", "replica", "tensor"),
        P("section", "tensor", "replica"),
        P("section", None, "replica", None, "tensor", None),
        P("section", None, "replica", None, "tensor", None),
    )
    out_specs = (P("section", None, "replica"), P("section", None, "replica"))
    return jax.shard_map(
        on_device, mesh=mesh, in_specs=in_specs, out_specs=out_specs, check_vma=False
    )
```

```python
import jax
import jax.numpy as jnp
from jax import lax
from jax.experimental import pallas as pl
from jax.experimental.pallas import tpu as pltpu
from jax.sharding import PartitionSpec as P

HD = 128
NEAR = 2
BF = jnp.bfloat16
F32 = jnp.float32
VMEM = pl.BlockSpec(memory_space=pltpu.VMEM)
SMEM = pl.BlockSpec(memory_space=pltpu.SMEM)
HBM = pl.BlockSpec(memory_space=pltpu.HBM)
PARAMS = pltpu.CompilerParams(vmem_limit_bytes=12 * 1024 * 1024)


def in_hbm(x):
    return pltpu.with_memory_space_constraint(x, pltpu.HBM)


def shape(dims, dtype=BF):
    return jax.ShapeDtypeStruct(tuple(dims), dtype)


def cost(flops, size):
    return pl.CostEstimate(flops=flops, bytes_accessed=size, transcendentals=0)


def swapped(block, axis, bits):
    route = [(i, i ^ bits) for i in range(lax.axis_size(axis))]
    return lax.ppermute(block, axis, route)


def from_behind(block, bits):
    sections, tensors = lax.axis_size("section"), lax.axis_size("tensor")
    route = [
        (s * tensors + (t ^ bits), (s + 1) % sections * tensors + t)
        for s in range(sections)
        for t in range(tensors)
    ]
    return lax.ppermute(block, ("section", "tensor"), route)


def tree_sum(pieces):
    pieces = [piece.astype(F32) for piece in pieces]
    while len(pieces) > 1:
        pieces = [pieces[i] + pieces[i + 1] for i in range(0, len(pieces), 2)]
    return pieces[0]


def batch_at(tick, sections):
    return lax.rem(lax.axis_index("section") + (sections - tick), sections)


def pack_kernel(dims, *refs):
    sections, tensors, rows, heads_dev, group, kv_dev = dims
    sources, refs = refs[:8], refs[8:]
    packs, (far_ref, h_ref, next_ref, lengths_ref) = refs[:tensors], refs[tensors : tensors + 4]
    ids, lengths, gains, biases, keys, values, sems = refs[tensors + 4 :]
    held = 2 * sections * kv_dev
    targets = (ids, lengths, keys, values, gains, biases, h_ref, next_ref)
    copies = [
        pltpu.make_async_copy(source, target, sems.at[i])
        for i, (source, target) in enumerate(zip(sources, targets))
    ]
    for copy in copies:
        copy.start()
    at = lax.axis_index("tensor")
    tenants = gains.shape[0]
    count = sections * rows
    spot = lax.broadcasted_iota(jnp.int32, (count, tenants), 0)
    line = lax.broadcasted_iota(jnp.int32, lengths_ref.shape, 0)
    wanted = jnp.zeros((count, tenants), jnp.int32)
    kept = jnp.zeros(lengths_ref.shape, jnp.int32)
    copies[0].wait()
    copies[1].wait()
    for tick in range(sections):
        batch = batch_at(tick, sections)
        kept = jnp.where(line == tick, lengths[batch], kept)
        for i in range(rows):
            wanted = jnp.where(spot == tick * rows + i, ids[batch, i], wanted)
    lengths_ref[...] = kept.astype(F32)
    wanted = wanted - at * tenants
    onehot = jnp.where(wanted == lax.broadcasted_iota(jnp.int32, (count, tenants), 1), 1.0, 0.0)
    onehot = onehot.astype(BF)
    copies[2].wait()
    copies[3].wait()
    pos, lanes = keys.shape[2:]
    width = gains.shape[1]
    per = pos // (2 * rows)
    blocks = width // lanes // per
    for d in range(tensors):
        start = lax.bitwise_xor(at, d) * heads_dev // group
        for which, cache in enumerate((keys, values)):
            for b in range(sections):
                for g in range(kv_dev):
                    to = (which * sections + b) * kv_dev + g
                    packs[d][to] = cache[b, start + g]
    copies[4].wait()
    gain_rows = jnp.dot(onehot, gains[...], preferred_element_type=F32)
    copies[5].wait()
    bias_rows = jnp.dot(onehot, biases[...], preferred_element_type=F32)
    for tick in range(sections):
        mine = slice(tick * rows, (tick + 1) * rows)
        both = jnp.concatenate([gain_rows[mine], bias_rows[mine]], 0)
        for j in range(blocks):
            block = jnp.concatenate(
                [both[:, (j * per + k) * lanes : (j * per + k + 1) * lanes] for k in range(per)], 0
            ).astype(BF)
            for d in range(tensors if tick == 0 else min(tensors, NEAR)):
                packs[d][held + tick * blocks + j] = block
            if tick > 0:
                far_ref[(tick - 1) * blocks + j] = block
    copies[6].wait()
    copies[7].wait()


def pack(dims, tenant, lengths, gain, bias, keys, values, h, following):
    sections, tensors, rows, heads_dev, group, kv_dev = dims
    pos = keys.shape[2]
    blocks = 2 * rows * gain.shape[1] // (pos * HD)
    held, later = 2 * sections * kv_dev, (sections - 1) * blocks
    out_shape = [
        shape((held + blocks + (later if d < NEAR else 0), pos, HD)) for d in range(tensors)
    ]
    out_shape += [shape((later, pos, HD))]
    out_shape += [shape(h.shape), shape(following.shape), shape((sections, HD), F32)]
    operands = (tenant, lengths, keys, values, gain, bias, h, following)
    return pl.pallas_call(
        lambda *refs: pack_kernel(dims, *refs),
        out_shape=out_shape,
        in_specs=[HBM] * len(operands),
        out_specs=[VMEM] * len(out_shape),
        scratch_shapes=[pltpu.SMEM(x.shape, jnp.int32) for x in (tenant, lengths)]
        + [pltpu.VMEM(x.shape, BF) for x in (gain, bias, keys, values)]
        + [pltpu.SemaphoreType.DMA((len(operands),))],
        compiler_params=PARAMS,
        cost_estimate=cost(0, 4 * gain.size),
    )(*[in_hbm(x) for x in operands])


def join_kernel(count, size, refs):
    out_ref = refs[-1]
    for i in range(count):
        out_ref[i] = refs[i][:size]


def join(pieces, size, after):
    count = len(pieces)
    dims = pieces[0].shape
    return pl.pallas_call(
        lambda *refs: join_kernel(count, size, refs),
        out_shape=shape((count, size) + dims[1:]),
        in_specs=[VMEM] * count + [pl.BlockSpec(memory_space=pl.ANY)] * len(after),
        out_specs=VMEM,
        compiler_params=PARAMS,
    )(*pieces, *after)


def hold_kernel(parts, after_ref, wq_ref, wo_ref, wq_out, wo_out, sems):
    copies = []
    for source, target in ((wq_ref, wq_out), (wo_ref, wo_out)):
        rows = source.shape[0] // parts
        for i in range(parts):
            at = pl.ds(i * rows, rows)
            copies.append(
                pltpu.make_async_copy(source.at[at], target.at[at], sems.at[len(copies)])
            )
    for copy in copies:
        copy.start()
    for copy in copies:
        copy.wait()


def hold(wq, wo, after):
    parts = 8
    return pl.pallas_call(
        lambda *refs: hold_kernel(parts, *refs),
        out_shape=[pltpu.VMEM(wq.shape, BF), pltpu.VMEM(wo.shape, BF)],
        in_specs=[pl.BlockSpec(memory_space=pl.ANY), HBM, HBM],
        out_specs=[VMEM] * 2,
        scratch_shapes=[pltpu.SemaphoreType.DMA((2 * parts,))],
        compiler_params=PARAMS,
        cost_estimate=cost(0, 4 * wq.size),
    )(after, in_hbm(wq), in_hbm(wo))


def tiles(w_ref):
    width = min(512, w_ref.shape[1])
    return [slice(i, i + width) for i in range(0, w_ref.shape[1], width)]


def thirds(x):
    high = x.astype(BF).astype(F32)
    middle = (x - high).astype(BF).astype(F32)
    return [high, middle, x - high - middle]


def query_sums(first_blocks, length, h, pieces, w_ref, out_ref):
    rows, width = h.shape
    pos, lanes = pieces[0].shape[1:]
    per = pos // (2 * rows)
    cols = []
    for j in range(width // lanes // per):
        block = tree_sum([piece[first + j] for first, piece in zip(first_blocks, pieces)])
        cols += [block[k * 2 * rows : (k + 1) * 2 * rows] for k in range(per)]
    affine = jnp.concatenate(cols, 1)
    total = jnp.sum(h, axis=-1, keepdims=True)
    squares = jnp.sum(h * h, axis=-1, keepdims=True)
    centred = (h - total * (1.0 / width)) * affine[:rows]
    x = jnp.concatenate([centred, affine], 0).astype(BF)
    count = w_ref.shape[1]
    for at in tiles(w_ref):
        got = jnp.dot(x, w_ref[:, at], preferred_element_type=F32)
        for k in range(3):
            to = slice(k * count + at.start, k * count + at.stop)
            out_ref[:, to] = got[k * rows : (k + 1) * rows].astype(BF)
    lane = lax.broadcasted_iota(jnp.int32, (rows, HD), 1)
    tail = jnp.broadcast_to(length, (rows, HD))
    for i, term in enumerate(thirds(total) + thirds(squares)):
        tail = jnp.where(lane == i, term, tail)
    out_ref[:, 3 * count :] = tail.astype(BF)


def first_kernel(tensors, held, lengths_ref, h_ref, *refs):
    pieces, (w_ref, out_ref) = refs[:tensors], refs[tensors:]
    query_sums([held] * tensors, lengths_ref[0:1], h_ref[...].astype(F32), pieces, w_ref, out_ref)


def first_sums(held, lengths, h, pieces, w):
    tensors = len(pieces)
    return pl.pallas_call(
        lambda *refs: first_kernel(tensors, held, *refs),
        out_shape=shape((h.shape[0], 3 * w.shape[1] + HD)),
        in_specs=[VMEM] * (tensors + 3),
        out_specs=VMEM,
        compiler_params=PARAMS,
        cost_estimate=cost(24 * w.size, 2 * w.size),
    )(lengths, h, *pieces, w)


def arrive(arrivals, following, tick):
    sections, rows, width = following.shape
    rest = arrivals[0][:, width:].astype(F32)
    section = jnp.full((rows, width), lax.axis_index("section"))
    left, carried = rest[:, :width], jnp.zeros((rows, width), F32)
    if sections == 2 and tick > 0:
        left = jnp.where(section == 1, following[-tick % sections].astype(F32), rest)
        carried = rest
    elif tick > 0:
        carried = rest[:, width:]
    came = tree_sum([arrival[:, :width] for arrival in arrivals]) + left
    came = came.astype(BF).astype(F32)
    h = jnp.where(section == 0, following[-(tick + 1) % sections].astype(F32), came)
    return h, jnp.where(section == 0, came, carried)


def later_kernel(count, tick, held, lengths_ref, *refs):
    arrivals, next_ref = refs[:count], refs[count]
    pieces, (w_ref, out_ref, carry_ref) = refs[count + 1 : -3], refs[-3:]
    h, emitted = arrive(arrivals, next_ref, tick - 1)
    width = h.shape[1]
    if carry_ref.shape[1] == width:
        first = jnp.full(h.shape, lax.axis_index("section")) == 0
        carry_ref[...] = jnp.where(first, emitted, h).astype(BF)
    else:
        carry_ref[:, :width] = h.astype(BF)
        carry_ref[:, width:] = emitted.astype(BF)
    blocks = 2 * h.shape[0] * width // (pieces[0].shape[1] * HD)
    firsts = [held + tick * blocks if d < NEAR else (tick - 1) * blocks for d in range(len(pieces))]
    query_sums(firsts, lengths_ref[tick : tick + 1], h, pieces, w_ref, out_ref)


def later_sums(tick, held, lengths, arrivals, following, pieces, w):
    rows, width = following.shape[1:]
    parts = 1 if following.shape[0] == 2 else 2
    return pl.pallas_call(
        lambda *refs: later_kernel(len(arrivals), tick, held, *refs),
        out_shape=[shape((rows, 3 * w.shape[1] + HD)), shape((rows, width * parts))],
        in_specs=[VMEM] * (len(arrivals) + len(pieces) + 3),
        out_specs=[VMEM] * 2,
        compiler_params=PARAMS,
        cost_estimate=cost(24 * w.size, 2 * w.size),
    )(lengths, *arrivals, following, *pieces, w)


def last_kernel(count, *refs):
    state_ref, emitted_ref = refs[-2:]
    h, emitted = arrive(refs[:count], refs[count], refs[count].shape[0] - 1)
    state_ref[0] = h.astype(BF)
    emitted_ref[0] = emitted.astype(BF)


def last(arrivals, following):
    return pl.pallas_call(
        lambda *refs: last_kernel(len(arrivals), *refs),
        out_shape=[shape((1,) + following.shape[1:])] * 2,
        in_specs=[VMEM] * (len(arrivals) + 1),
        out_specs=[VMEM] * 2,
        compiler_params=PARAMS,
    )(*arrivals, following)


def attend_kernel(dims, turns, tick, *refs):
    sections, tensors, rows, kv_dev = dims
    count = len(turns)
    pieces, (carry_ref, w_ref), refs = refs[:count], refs[count : count + 2], refs[count + 2 :]
    caches, (out_ref, full_ref) = refs[:-2], refs[-2:]
    each = caches[0].shape[0] // tensors
    span = w_ref.shape[0]
    width = w_ref.shape[1]
    batch = batch_at(tick, sections)

    tails = [piece[:, 3 * span :].astype(F32) for piece in pieces]
    totals = [tail[:, 0:1] + tail[:, 1:2] + tail[:, 2:3] for tail in tails]
    squares = [tail[:, 3:4] + tail[:, 4:5] + tail[:, 5:6] for tail in tails]
    scale = 1.0 / (width * count)
    mean = tree_sum(totals) * scale
    rstd = lax.rsqrt(tree_sum(squares) * scale - mean * mean + 1e-05)
    query = tree_sum(
        [
            piece[:, :span].astype(F32)
            + (total * (1.0 / width) - mean) * piece[:, span : 2 * span].astype(F32)
            for piece, total in zip(pieces, totals)
        ]
    )
    query = rstd * query + tree_sum([piece[:, 2 * span : 3 * span] for piece in pieces])
    query = query.astype(BF).astype(F32)

    pos = caches[0].shape[2]
    tensor_at, replica_at = lax.axis_index("tensor"), lax.axis_index("replica")
    cols = lax.broadcasted_iota(jnp.int32, (rows, tensors * pos), 1)
    row = lax.broadcasted_iota(jnp.int32, (rows, tensors * pos), 0)
    spots = jnp.bitwise_xor(cols // pos, tensor_at) * pos + cols % pos
    spots = spots.astype(F32)
    keep = []
    for turn in turns:
        valid = jnp.logical_and(row == jnp.bitwise_xor(replica_at, turn), spots < tails[turn][:, 6:7])
        keep.append(jnp.where(valid, 0.0, -1e30))
    per_kv = span // HD // kv_dev
    keep = jnp.concatenate([jnp.concatenate(keep, 1)] * per_kv, 0)

    att = []
    for g in range(kv_dev):
        mine = jnp.concatenate(
            [query[:, h * HD : (h + 1) * HD] for h in range(g * per_kv, (g + 1) * per_kv)], 0
        ).astype(BF)
        keys, values = (
            jnp.concatenate(
                [
                    cache[i, (which * sections + batch) * kv_dev + g]
                    for cache in caches
                    for i in range(each * tensors)
                ],
                0,
            )
            for which in range(2)
        )
        scores = lax.dot_general(mine, keys, (((1,), (1,)), ((), ())), preferred_element_type=F32)
        scores = scores * (HD**-0.5) + keep
        probs = jnp.exp(scores - jnp.max(scores, axis=-1, keepdims=True))
        total = jnp.sum(probs, axis=-1, keepdims=True)
        got = jnp.dot(probs.astype(BF), values, preferred_element_type=F32) / total
        att += [got[h * rows : (h + 1) * rows] for h in range(per_kv)]
    att = jnp.concatenate(att, 1).astype(BF)
    for at in tiles(w_ref):
        got = jnp.dot(att, w_ref[:, at], preferred_element_type=F32).astype(BF)
        out_ref[:, at] = got
        full_ref[:, at] = got
    full_ref[:, width:] = carry_ref[...]


def attend(dims, turns, tick, pieces, caches, carry, w):
    rows, width = carry.shape[0], w.shape[1]
    return pl.pallas_call(
        lambda *refs: attend_kernel(dims, turns, tick, *refs),
        out_shape=[shape((rows, width)), shape((rows, width + carry.shape[1]))],
        in_specs=[VMEM] * (len(pieces) + len(caches) + 2),
        out_specs=[VMEM] * 2,
        compiler_params=PARAMS,
        cost_estimate=cost(8 * w.size, 2 * w.size),
    )(*pieces, carry, w, *caches)


def on_device(state, next_embed, tenant, lengths, gain, bias, wq, wo, keys, values):
    sections = lax.axis_size("section")
    tensors = lax.axis_size("tensor")
    replicas = lax.axis_size("replica")
    rows, width = state.shape[1:]
    heads_dev = wq.shape[2] // HD
    group = heads_dev * tensors // keys.shape[3]
    kv_dev = max(1, heads_dev // group)
    dims = (sections, tensors, rows, heads_dev, group, kv_dev)

    *packs, far, carry, following, lengths = pack(
        dims,
        tenant,
        lengths.reshape(-1),
        gain[0],
        bias[0],
        keys[0, :, 0],
        values[0, :, 0],
        state[0],
        next_embed,
    )
    got = [packs[0]] + [swapped(packs[d], "tensor", d) for d in range(1, tensors)]
    later = got[:NEAR] + [swapped(far, "tensor", d) for d in range(NEAR, tensors)]
    wq_held, wo_held = hold(wq[0], wo[0], packs[0])

    held = 2 * sections * kv_dev
    kv = join(got, held, [wq_held, wo_held])
    turns, bit = [0], replicas // 2
    caches, waiting = [kv], None
    if bit:
        waiting = swapped(kv, "replica", bit)
    arrivals = None
    for tick in range(sections):
        if tick == 0:
            sums = first_sums(held, lengths, carry, got, wq_held)
        else:
            sums, carry = later_sums(tick, held, lengths, arrivals, following, later, wq_held)
        pieces = [sums] + [swapped(sums, "replica", d) for d in range(1, replicas)]
        if tick == 0:
            while bit:
                turns = turns + [turn ^ bit for turn in turns]
                caches, bit = [kv, waiting], bit // 2
                if bit:
                    both = join(caches, kv.shape[0], pieces[2:])
                    kv = both.reshape((-1,) + both.shape[2:])
                    waiting = swapped(kv, "replica", bit)
        out, full = attend(
            (sections, tensors, rows, kv_dev), turns, tick, pieces, caches, carry, wo_held
        )
        arrivals = [from_behind(full, 0)] + [from_behind(out, d) for d in range(1, tensors)]
    return tuple(last(arrivals, following))


def solution(mesh):
    in_specs = (
        P("section", None, "replica"),
        P(None, None, "replica"),
        P(),
        P(None, "replica"),
        P("section", "tensor", "replica"),
        P("section", "tensor", "replica"),
        P("section", "replica", "tensor"),
        P("section", "tensor", "replica"),
        P("section", None, "replica", None, "tensor", None),
        P("section", None, "replica", None, "tensor", None),
    )
    out_specs = (P("section", None, "replica"), P("section", None, "replica"))
    return jax.shard_map(
        on_device, mesh=mesh, in_specs=in_specs, out_specs=out_specs, check_vma=False
    )
```

```python
import jax
import jax.numpy as jnp
from jax import lax
from jax.experimental import pallas as pl
from jax.experimental.pallas import tpu as pltpu
from jax.sharding import PartitionSpec as P

HD = 128
NEAR = 2
BF = jnp.bfloat16
F32 = jnp.float32
VMEM = pl.BlockSpec(memory_space=pltpu.VMEM)
SMEM = pl.BlockSpec(memory_space=pltpu.SMEM)
HBM = pl.BlockSpec(memory_space=pltpu.HBM)
PARAMS = pltpu.CompilerParams(vmem_limit_bytes=12 * 1024 * 1024)


def in_hbm(x):
    return pltpu.with_memory_space_constraint(x, pltpu.HBM)


def shape(dims, dtype=BF):
    return jax.ShapeDtypeStruct(tuple(dims), dtype)


def cost(flops, size):
    return pl.CostEstimate(flops=flops, bytes_accessed=size, transcendentals=0)


def swapped(block, axis, bits):
    route = [(i, i ^ bits) for i in range(lax.axis_size(axis))]
    return lax.ppermute(block, axis, route)


def from_behind(block, bits):
    sections, tensors = lax.axis_size("section"), lax.axis_size("tensor")
    route = [
        (s * tensors + (t ^ bits), (s + 1) % sections * tensors + t)
        for s in range(sections)
        for t in range(tensors)
    ]
    return lax.ppermute(block, ("section", "tensor"), route)


def tree_sum(pieces):
    pieces = [piece.astype(F32) for piece in pieces]
    while len(pieces) > 1:
        pieces = [pieces[i] + pieces[i + 1] for i in range(0, len(pieces), 2)]
    return pieces[0]


def batch_at(tick, sections):
    return lax.rem(lax.axis_index("section") + (sections - tick), sections)


def pack_kernel(dims, *refs):
    sections, tensors, rows, heads_dev, group, kv_dev = dims
    sources, refs = refs[:8], refs[8:]
    packs, (h_ref, next_ref, lengths_ref) = refs[:tensors], refs[tensors : tensors + 3]
    ids, lengths, gains, biases, keys, values, sems = refs[tensors + 3 :]
    held = 2 * sections * kv_dev
    targets = (ids, lengths, keys, values, gains, biases, h_ref, next_ref)
    copies = [
        pltpu.make_async_copy(source, target, sems.at[i])
        for i, (source, target) in enumerate(zip(sources, targets))
    ]
    for copy in copies:
        copy.start()
    at = lax.axis_index("tensor")
    tenants = gains.shape[0]
    count = sections * rows
    spot = lax.broadcasted_iota(jnp.int32, (count, tenants), 0)
    line = lax.broadcasted_iota(jnp.int32, lengths_ref.shape, 0)
    wanted = jnp.zeros((count, tenants), jnp.int32)
    kept = jnp.zeros(lengths_ref.shape, jnp.int32)
    copies[0].wait()
    copies[1].wait()
    for tick in range(sections):
        batch = batch_at(tick, sections)
        kept = jnp.where(line == tick, lengths[batch], kept)
        for i in range(rows):
            wanted = jnp.where(spot == tick * rows + i, ids[batch, i], wanted)
    lengths_ref[...] = kept.astype(F32)
    wanted = wanted - at * tenants
    onehot = jnp.where(wanted == lax.broadcasted_iota(jnp.int32, (count, tenants), 1), 1.0, 0.0)
    onehot = onehot.astype(BF)
    copies[2].wait()
    copies[3].wait()
    pos, lanes = keys.shape[2:]
    width = gains.shape[1]
    per = pos // (2 * rows)
    blocks = width // lanes // per
    for d in range(tensors):
        start = lax.bitwise_xor(at, d) * heads_dev // group
        for which, cache in enumerate((keys, values)):
            for b in range(sections):
                for g in range(kv_dev):
                    to = (which * sections + b) * kv_dev + g
                    packs[d][to] = cache[b, start + g]
    copies[4].wait()
    gain_rows = jnp.dot(onehot, gains[...], preferred_element_type=F32)
    copies[5].wait()
    bias_rows = jnp.dot(onehot, biases[...], preferred_element_type=F32)
    for tick in range(sections):
        mine = slice(tick * rows, (tick + 1) * rows)
        both = jnp.concatenate([gain_rows[mine], bias_rows[mine]], 0)
        for j in range(blocks):
            block = jnp.concatenate(
                [both[:, (j * per + k) * lanes : (j * per + k + 1) * lanes] for k in range(per)], 0
            ).astype(BF)
            for d in range(tensors if tick == 0 else min(tensors, NEAR)):
                packs[d][held + tick * blocks + j] = block
    copies[6].wait()
    copies[7].wait()


def pack(dims, tenant, lengths, gain, bias, keys, values, h, following):
    sections, tensors, rows, heads_dev, group, kv_dev = dims
    pos = keys.shape[2]
    blocks = 2 * rows * gain.shape[1] // (pos * HD)
    held, later = 2 * sections * kv_dev, (sections - 1) * blocks
    out_shape = [
        shape((held + blocks + (later if d < NEAR else 0), pos, HD)) for d in range(tensors)
    ]
    out_shape += [shape(h.shape), shape(following.shape), shape((sections, HD), F32)]
    operands = (tenant, lengths, keys, values, gain, bias, h, following)
    return pl.pallas_call(
        lambda *refs: pack_kernel(dims, *refs),
        out_shape=out_shape,
        in_specs=[HBM] * len(operands),
        out_specs=[VMEM] * len(out_shape),
        scratch_shapes=[pltpu.SMEM(x.shape, jnp.int32) for x in (tenant, lengths)]
        + [pltpu.VMEM(x.shape, BF) for x in (gain, bias, keys, values)]
        + [pltpu.SemaphoreType.DMA((len(operands),))],
        compiler_params=PARAMS,
        cost_estimate=cost(0, 4 * gain.size),
    )(*[in_hbm(x) for x in operands])


def join_kernel(count, size, refs):
    out_ref = refs[-1]
    for i in range(count):
        out_ref[i] = refs[i][:size]


def join(pieces, size, after):
    count = len(pieces)
    dims = pieces[0].shape
    return pl.pallas_call(
        lambda *refs: join_kernel(count, size, refs),
        out_shape=shape((count, size) + dims[1:]),
        in_specs=[VMEM] * count + [pl.BlockSpec(memory_space=pl.ANY)] * len(after),
        out_specs=VMEM,
        compiler_params=PARAMS,
    )(*pieces, *after)


def hold_kernel(parts, after_ref, wq_ref, wo_ref, wq_out, wo_out, sems):
    copies = []
    for source, target in ((wq_ref, wq_out), (wo_ref, wo_out)):
        rows = source.shape[0] // parts
        for i in range(parts):
            at = pl.ds(i * rows, rows)
            copies.append(
                pltpu.make_async_copy(source.at[at], target.at[at], sems.at[len(copies)])
            )
    for copy in copies:
        copy.start()
    for copy in copies:
        copy.wait()


def hold(wq, wo, after):
    parts = 16
    return pl.pallas_call(
        lambda *refs: hold_kernel(parts, *refs),
        out_shape=[pltpu.VMEM(wq.shape, BF), pltpu.VMEM(wo.shape, BF)],
        in_specs=[pl.BlockSpec(memory_space=pl.ANY), HBM, HBM],
        out_specs=[VMEM] * 2,
        scratch_shapes=[pltpu.SemaphoreType.DMA((2 * parts,))],
        compiler_params=PARAMS,
        cost_estimate=cost(0, 4 * wq.size),
    )(after, in_hbm(wq), in_hbm(wo))


def tiles(w_ref):
    width = min(512, w_ref.shape[1])
    return [slice(i, i + width) for i in range(0, w_ref.shape[1], width)]


def thirds(x):
    high = x.astype(BF).astype(F32)
    middle = (x - high).astype(BF).astype(F32)
    return [high, middle, x - high - middle]


def query_sums(first_blocks, length, h, pieces, w_ref, out_ref):
    rows, width = h.shape
    pos, lanes = pieces[0].shape[1:]
    per = pos // (2 * rows)
    cols = []
    for j in range(width // lanes // per):
        block = tree_sum([piece[first + j] for first, piece in zip(first_blocks, pieces)])
        cols += [block[k * 2 * rows : (k + 1) * 2 * rows] for k in range(per)]
    affine = jnp.concatenate(cols, 1)
    total = jnp.sum(h, axis=-1, keepdims=True)
    squares = jnp.sum(h * h, axis=-1, keepdims=True)
    centred = (h - total * (1.0 / width)) * affine[:rows]
    x = jnp.concatenate([centred, affine], 0).astype(BF)
    count = w_ref.shape[1]
    for at in tiles(w_ref):
        got = jnp.dot(x, w_ref[:, at], preferred_element_type=F32)
        for k in range(3):
            to = slice(k * count + at.start, k * count + at.stop)
            out_ref[:, to] = got[k * rows : (k + 1) * rows].astype(BF)
    lane = lax.broadcasted_iota(jnp.int32, (rows, HD), 1)
    tail = jnp.broadcast_to(length, (rows, HD))
    for i, term in enumerate(thirds(total) + thirds(squares)):
        tail = jnp.where(lane == i, term, tail)
    out_ref[:, 3 * count :] = tail.astype(BF)


def first_kernel(tensors, held, lengths_ref, h_ref, *refs):
    pieces, (w_ref, out_ref) = refs[:tensors], refs[tensors:]
    query_sums([held] * tensors, lengths_ref[0:1], h_ref[...].astype(F32), pieces, w_ref, out_ref)


def first_sums(held, lengths, h, pieces, w):
    tensors = len(pieces)
    return pl.pallas_call(
        lambda *refs: first_kernel(tensors, held, *refs),
        out_shape=shape((h.shape[0], 3 * w.shape[1] + HD)),
        in_specs=[VMEM] * (tensors + 3),
        out_specs=VMEM,
        compiler_params=PARAMS,
        cost_estimate=cost(24 * w.size, 2 * w.size),
    )(lengths, h, *pieces, w)


def arrive(arrivals, following, tick):
    sections, rows, width = following.shape
    rest = arrivals[0][:, width:].astype(F32)
    section = jnp.full((rows, width), lax.axis_index("section"))
    left, carried = rest[:, :width], jnp.zeros((rows, width), F32)
    if sections == 2 and tick > 0:
        left = jnp.where(section == 1, following[-tick % sections].astype(F32), rest)
        carried = rest
    elif tick > 0:
        carried = rest[:, width:]
    came = tree_sum([arrival[:, :width] for arrival in arrivals]) + left
    came = came.astype(BF).astype(F32)
    h = jnp.where(section == 0, following[-(tick + 1) % sections].astype(F32), came)
    return h, jnp.where(section == 0, came, carried)


def later_kernel(count, tick, lengths_ref, *refs):
    arrivals, next_ref = refs[:count], refs[count]
    pieces, (w_ref, out_ref, carry_ref) = refs[count + 1 : -3], refs[-3:]
    h, emitted = arrive(arrivals, next_ref, tick - 1)
    width = h.shape[1]
    if carry_ref.shape[1] == width:
        first = jnp.full(h.shape, lax.axis_index("section")) == 0
        carry_ref[...] = jnp.where(first, emitted, h).astype(BF)
    else:
        carry_ref[:, :width] = h.astype(BF)
        carry_ref[:, width:] = emitted.astype(BF)
    blocks = 2 * h.shape[0] * width // (pieces[0].shape[1] * HD)
    query_sums([(tick - 1) * blocks] * len(pieces), lengths_ref[tick : tick + 1], h, pieces, w_ref, out_ref)


def later_sums(tick, lengths, arrivals, following, pieces, w):
    rows, width = following.shape[1:]
    parts = 1 if following.shape[0] == 2 else 2
    return pl.pallas_call(
        lambda *refs: later_kernel(len(arrivals), tick, *refs),
        out_shape=[shape((rows, 3 * w.shape[1] + HD)), shape((rows, width * parts))],
        in_specs=[VMEM] * (len(arrivals) + len(pieces) + 3),
        out_specs=[VMEM] * 2,
        compiler_params=PARAMS,
        cost_estimate=cost(24 * w.size, 2 * w.size),
    )(lengths, *arrivals, following, *pieces, w)


def last_kernel(count, *refs):
    state_ref, emitted_ref = refs[-2:]
    h, emitted = arrive(refs[:count], refs[count], refs[count].shape[0] - 1)
    state_ref[0] = h.astype(BF)
    emitted_ref[0] = emitted.astype(BF)


def last(arrivals, following):
    return pl.pallas_call(
        lambda *refs: last_kernel(len(arrivals), *refs),
        out_shape=[shape((1,) + following.shape[1:])] * 2,
        in_specs=[VMEM] * (len(arrivals) + 1),
        out_specs=[VMEM] * 2,
        compiler_params=PARAMS,
    )(*arrivals, following)


def attend_kernel(dims, turns, tick, *refs):
    sections, tensors, rows, kv_dev = dims
    count = len(turns)
    pieces, (carry_ref, w_ref), refs = refs[:count], refs[count : count + 2], refs[count + 2 :]
    caches, (out_ref, full_ref) = refs[:-2], refs[-2:]
    each = caches[0].shape[0] // tensors
    span = w_ref.shape[0]
    width = w_ref.shape[1]
    batch = batch_at(tick, sections)

    tails = [piece[:, 3 * span :].astype(F32) for piece in pieces]
    totals = [tail[:, 0:1] + tail[:, 1:2] + tail[:, 2:3] for tail in tails]
    squares = [tail[:, 3:4] + tail[:, 4:5] + tail[:, 5:6] for tail in tails]
    scale = 1.0 / (width * count)
    mean = tree_sum(totals) * scale
    rstd = lax.rsqrt(tree_sum(squares) * scale - mean * mean + 1e-05)
    query = tree_sum(
        [
            piece[:, :span].astype(F32)
            + (total * (1.0 / width) - mean) * piece[:, span : 2 * span].astype(F32)
            for piece, total in zip(pieces, totals)
        ]
    )
    query = rstd * query + tree_sum([piece[:, 2 * span : 3 * span] for piece in pieces])
    query = query.astype(BF).astype(F32)

    pos = caches[0].shape[2]
    tensor_at, replica_at = lax.axis_index("tensor"), lax.axis_index("replica")
    cols = lax.broadcasted_iota(jnp.int32, (rows, tensors * pos), 1)
    row = lax.broadcasted_iota(jnp.int32, (rows, tensors * pos), 0)
    spots = jnp.bitwise_xor(cols // pos, tensor_at) * pos + cols % pos
    spots = spots.astype(F32)
    keep = []
    for turn in turns:
        valid = jnp.logical_and(row == jnp.bitwise_xor(replica_at, turn), spots < tails[turn][:, 6:7])
        keep.append(jnp.where(valid, 0.0, -1e30))
    per_kv = span // HD // kv_dev
    keep = jnp.concatenate([jnp.concatenate(keep, 1)] * per_kv, 0)

    att = []
    for g in range(kv_dev):
        mine = jnp.concatenate(
            [query[:, h * HD : (h + 1) * HD] for h in range(g * per_kv, (g + 1) * per_kv)], 0
        ).astype(BF)
        keys, values = (
            jnp.concatenate(
                [
                    cache[i, (which * sections + batch) * kv_dev + g]
                    for cache in caches
                    for i in range(each * tensors)
                ],
                0,
            )
            for which in range(2)
        )
        scores = lax.dot_general(mine, keys, (((1,), (1,)), ((), ())), preferred_element_type=F32)
        scores = scores * (HD**-0.5) + keep
        probs = jnp.exp(scores - jnp.max(scores, axis=-1, keepdims=True))
        total = jnp.sum(probs, axis=-1, keepdims=True)
        got = jnp.dot(probs.astype(BF), values, preferred_element_type=F32) / total
        att += [got[h * rows : (h + 1) * rows] for h in range(per_kv)]
    att = jnp.concatenate(att, 1).astype(BF)
    for at in tiles(w_ref):
        got = jnp.dot(att, w_ref[:, at], preferred_element_type=F32).astype(BF)
        out_ref[:, at] = got
        full_ref[:, at] = got
    full_ref[:, width:] = carry_ref[...]


def attend(dims, turns, tick, pieces, caches, carry, w):
    rows, width = carry.shape[0], w.shape[1]
    return pl.pallas_call(
        lambda *refs: attend_kernel(dims, turns, tick, *refs),
        out_shape=[shape((rows, width)), shape((rows, width + carry.shape[1]))],
        in_specs=[VMEM] * (len(pieces) + len(caches) + 2),
        out_specs=[VMEM] * 2,
        compiler_params=PARAMS,
        cost_estimate=cost(8 * w.size, 2 * w.size),
    )(*pieces, carry, w, *caches)


def on_device(state, next_embed, tenant, lengths, gain, bias, wq, wo, keys, values):
    sections = lax.axis_size("section")
    tensors = lax.axis_size("tensor")
    replicas = lax.axis_size("replica")
    rows, width = state.shape[1:]
    heads_dev = wq.shape[2] // HD
    group = heads_dev * tensors // keys.shape[3]
    kv_dev = max(1, heads_dev // group)
    dims = (sections, tensors, rows, heads_dev, group, kv_dev)

    *packs, carry, following, lengths = pack(
        dims,
        tenant,
        lengths.reshape(-1),
        gain[0],
        bias[0],
        keys[0, :, 0],
        values[0, :, 0],
        state[0],
        next_embed,
    )
    got = [packs[0]] + [swapped(packs[d], "tensor", d) for d in range(1, tensors)]
    wq_held, wo_held = hold(wq[0], wo[0], packs[0])

    held = 2 * sections * kv_dev
    kv = join(got, held, [wq_held, wo_held])

    later = [piece[held + 2 * rows * width // (keys.shape[4] * HD) :] for piece in got[:NEAR]]
    bit = NEAR
    while bit < tensors:
        later = [sum(later)]
        later = later + [swapped(later[0], "tensor", bit)]
        bit *= 2
    turns, bit = [0], replicas // 2
    caches, waiting = [kv], None
    if bit:
        waiting = swapped(kv, "replica", bit)
    arrivals = None
    for tick in range(sections):
        if tick == 0:
            sums = first_sums(held, lengths, carry, got, wq_held)
        else:
            sums, carry = later_sums(tick, lengths, arrivals, following, later, wq_held)
        pieces = [sums] + [swapped(sums, "replica", d) for d in range(1, replicas)]
        if tick == 0:
            while bit:
                turns = turns + [turn ^ bit for turn in turns]
                caches, bit = [kv, waiting], bit // 2
                if bit:
                    both = join(caches, kv.shape[0], pieces[2:])
                    kv = both.reshape((-1,) + both.shape[2:])
                    waiting = swapped(kv, "replica", bit)
        out, full = attend(
            (sections, tensors, rows, kv_dev), turns, tick, pieces, caches, carry, wo_held
        )
        arrivals = [from_behind(full, 0)] + [from_behind(out, d) for d in range(1, tensors)]
    return tuple(last(arrivals, following))


def solution(mesh):
    in_specs = (
        P("section", None, "replica"),
        P(None, None, "replica"),
        P(),
        P(None, "replica"),
        P("section", "tensor", "replica"),
        P("section", "tensor", "replica"),
        P("section", "replica", "tensor"),
        P("section", "tensor", "replica"),
        P("section", None, "replica", None, "tensor", None),
        P("section", None, "replica", None, "tensor", None),
    )
    out_specs = (P("section", None, "replica"), P("section", None, "replica"))
    return jax.shard_map(
        on_device, mesh=mesh, in_specs=in_specs, out_specs=out_specs, check_vma=False
    )
```

```python
import jax
import jax.numpy as jnp
from jax import lax
from jax.experimental import pallas as pl
from jax.experimental.pallas import tpu as pltpu
from jax.sharding import PartitionSpec as P

HD = 128
NEAR = 2
BF = jnp.bfloat16
F32 = jnp.float32
VMEM = pl.BlockSpec(memory_space=pltpu.VMEM)
SMEM = pl.BlockSpec(memory_space=pltpu.SMEM)
HBM = pl.BlockSpec(memory_space=pltpu.HBM)
PARAMS = pltpu.CompilerParams(vmem_limit_bytes=12 * 1024 * 1024)


def in_hbm(x):
    return pltpu.with_memory_space_constraint(x, pltpu.HBM)


def shape(dims, dtype=BF):
    return jax.ShapeDtypeStruct(tuple(dims), dtype)


def cost(flops, size):
    return pl.CostEstimate(flops=flops, bytes_accessed=size, transcendentals=0)


def swapped(block, axis, bits):
    route = [(i, i ^ bits) for i in range(lax.axis_size(axis))]
    return lax.ppermute(block, axis, route)


def from_behind(block, bits):
    sections, tensors = lax.axis_size("section"), lax.axis_size("tensor")
    route = [
        (s * tensors + (t ^ bits), (s + 1) % sections * tensors + t)
        for s in range(sections)
        for t in range(tensors)
    ]
    return lax.ppermute(block, ("section", "tensor"), route)


def tree_sum(pieces):
    pieces = [piece.astype(F32) for piece in pieces]
    while len(pieces) > 1:
        pieces = [pieces[i] + pieces[i + 1] for i in range(0, len(pieces), 2)]
    return pieces[0]


def batch_at(tick, sections):
    return lax.rem(lax.axis_index("section") + (sections - tick), sections)


def pack_kernel(dims, *refs):
    sections, tensors, rows, heads_dev, group, kv_dev = dims
    sources, refs = refs[:8], refs[8:]
    packs, (h_ref, next_ref, lengths_ref) = refs[:tensors], refs[tensors : tensors + 3]
    ids, lengths, gains, biases, keys, values, sems = refs[tensors + 3 :]
    held = 2 * sections * kv_dev
    targets = (ids, lengths, keys, values, gains, biases, h_ref, next_ref)
    copies = [
        pltpu.make_async_copy(source, target, sems.at[i])
        for i, (source, target) in enumerate(zip(sources, targets))
    ]
    for copy in copies:
        copy.start()
    at = lax.axis_index("tensor")
    tenants = gains.shape[0]
    count = sections * rows
    spot = lax.broadcasted_iota(jnp.int32, (count, tenants), 0)
    line = lax.broadcasted_iota(jnp.int32, lengths_ref.shape, 0)
    wanted = jnp.zeros((count, tenants), jnp.int32)
    kept = jnp.zeros(lengths_ref.shape, jnp.int32)
    copies[0].wait()
    copies[1].wait()
    for tick in range(sections):
        batch = batch_at(tick, sections)
        kept = jnp.where(line == tick, lengths[batch], kept)
        for i in range(rows):
            wanted = jnp.where(spot == tick * rows + i, ids[batch, i], wanted)
    lengths_ref[...] = kept.astype(F32)
    wanted = wanted - at * tenants
    onehot = jnp.where(wanted == lax.broadcasted_iota(jnp.int32, (count, tenants), 1), 1.0, 0.0)
    onehot = onehot.astype(BF)
    copies[2].wait()
    copies[3].wait()
    pos, lanes = keys.shape[2:]
    width = gains.shape[1]
    per = pos // (2 * rows)
    blocks = width // lanes // per
    for d in range(tensors):
        start = lax.bitwise_xor(at, d) * heads_dev // group
        for which, cache in enumerate((keys, values)):
            for b in range(sections):
                for g in range(kv_dev):
                    to = (which * sections + b) * kv_dev + g
                    packs[d][to] = cache[b, start + g]
    copies[4].wait()
    gain_rows = jnp.dot(onehot, gains[...], preferred_element_type=F32)
    copies[5].wait()
    bias_rows = jnp.dot(onehot, biases[...], preferred_element_type=F32)
    for tick in range(sections):
        mine = slice(tick * rows, (tick + 1) * rows)
        both = jnp.concatenate([gain_rows[mine], bias_rows[mine]], 0)
        for j in range(blocks):
            block = jnp.concatenate(
                [both[:, (j * per + k) * lanes : (j * per + k + 1) * lanes] for k in range(per)], 0
            ).astype(BF)
            for d in range(tensors if tick == 0 else min(tensors, NEAR)):
                packs[d][held + tick * blocks + j] = block
    copies[6].wait()
    copies[7].wait()


def pack(dims, tenant, lengths, gain, bias, keys, values, h, following):
    sections, tensors, rows, heads_dev, group, kv_dev = dims
    pos = keys.shape[2]
    blocks = 2 * rows * gain.shape[1] // (pos * HD)
    held, later = 2 * sections * kv_dev, (sections - 1) * blocks
    out_shape = [
        shape((held + blocks + (later if d < NEAR else 0), pos, HD)) for d in range(tensors)
    ]
    out_shape += [shape(h.shape), shape(following.shape), shape((sections, HD), F32)]
    operands = (tenant, lengths, keys, values, gain, bias, h, following)
    return pl.pallas_call(
        lambda *refs: pack_kernel(dims, *refs),
        out_shape=out_shape,
        in_specs=[HBM] * len(operands),
        out_specs=[VMEM] * len(out_shape),
        scratch_shapes=[pltpu.SMEM(x.shape, jnp.int32) for x in (tenant, lengths)]
        + [pltpu.VMEM(x.shape, BF) for x in (gain, bias, keys, values)]
        + [pltpu.SemaphoreType.DMA((len(operands),))],
        compiler_params=PARAMS,
        cost_estimate=cost(0, 4 * gain.size),
    )(*[in_hbm(x) for x in operands])


def join_kernel(count, size, refs):
    out_ref = refs[-1]
    for i in range(count):
        out_ref[i] = refs[i][:size]


def join(pieces, size, after):
    count = len(pieces)
    dims = pieces[0].shape
    return pl.pallas_call(
        lambda *refs: join_kernel(count, size, refs),
        out_shape=shape((count, size) + dims[1:]),
        in_specs=[VMEM] * count + [pl.BlockSpec(memory_space=pl.ANY)] * len(after),
        out_specs=VMEM,
        compiler_params=PARAMS,
    )(*pieces, *after)


def hold_kernel(parts, after_ref, wq_ref, wo_ref, wq_out, wo_out, sems):
    copies = []
    for source, target in ((wq_ref, wq_out), (wo_ref, wo_out)):
        rows = source.shape[0] // parts
        for i in range(parts):
            at = pl.ds(i * rows, rows)
            copies.append(
                pltpu.make_async_copy(source.at[at], target.at[at], sems.at[len(copies)])
            )
    for copy in copies:
        copy.start()
    for copy in copies:
        copy.wait()


def hold(wq, wo, after):
    parts = 16
    return pl.pallas_call(
        lambda *refs: hold_kernel(parts, *refs),
        out_shape=[pltpu.VMEM(wq.shape, BF), pltpu.VMEM(wo.shape, BF)],
        in_specs=[pl.BlockSpec(memory_space=pl.ANY), HBM, HBM],
        out_specs=[VMEM] * 2,
        scratch_shapes=[pltpu.SemaphoreType.DMA((2 * parts,))],
        compiler_params=PARAMS,
        cost_estimate=cost(0, 4 * wq.size),
    )(after, in_hbm(wq), in_hbm(wo))


def tiles(w_ref):
    width = min(512, w_ref.shape[1])
    return [slice(i, i + width) for i in range(0, w_ref.shape[1], width)]


def thirds(x):
    high = x.astype(BF).astype(F32)
    middle = (x - high).astype(BF).astype(F32)
    return [high, middle, x - high - middle]


def query_sums(first_blocks, length, h, pieces, w_ref, out_ref):
    rows, width = h.shape
    pos, lanes = pieces[0].shape[1:]
    per = pos // (2 * rows)
    cols = []
    for j in range(width // lanes // per):
        block = tree_sum([piece[first + j] for first, piece in zip(first_blocks, pieces)])
        cols += [block[k * 2 * rows : (k + 1) * 2 * rows] for k in range(per)]
    affine = jnp.concatenate(cols, 1)
    total = jnp.sum(h, axis=-1, keepdims=True)
    squares = jnp.sum(h * h, axis=-1, keepdims=True)
    centred = (h - total * (1.0 / width)) * affine[:rows]
    x = jnp.concatenate([centred, affine], 0).astype(BF)
    count = w_ref.shape[1]
    for at in tiles(w_ref):
        got = jnp.dot(x, w_ref[:, at], preferred_element_type=F32)
        for k in range(3):
            to = slice(k * count + at.start, k * count + at.stop)
            out_ref[:, to] = got[k * rows : (k + 1) * rows].astype(BF)
    lane = lax.broadcasted_iota(jnp.int32, (rows, HD), 1)
    tail = jnp.broadcast_to(length, (rows, HD))
    for i, term in enumerate(thirds(total) + thirds(squares)):
        tail = jnp.where(lane == i, term, tail)
    out_ref[:, 3 * count :] = tail.astype(BF)


def first_kernel(tensors, held, lengths_ref, h_ref, *refs):
    pieces, (w_ref, _, out_ref) = refs[:tensors], refs[tensors:]
    query_sums([held] * tensors, lengths_ref[0:1], h_ref[...].astype(F32), pieces, w_ref, out_ref)


def first_sums(held, lengths, h, pieces, w, after):
    tensors = len(pieces)
    return pl.pallas_call(
        lambda *refs: first_kernel(tensors, held, *refs),
        out_shape=shape((h.shape[0], 3 * w.shape[1] + HD)),
        in_specs=[VMEM] * (tensors + 3) + [pl.BlockSpec(memory_space=pl.ANY)],
        out_specs=VMEM,
        compiler_params=PARAMS,
        cost_estimate=cost(24 * w.size, 2 * w.size),
    )(lengths, h, *pieces, w, after)


def arrive(arrivals, following, tick):
    sections, rows, width = following.shape
    rest = arrivals[0][:, width:].astype(F32)
    section = jnp.full((rows, width), lax.axis_index("section"))
    left, carried = rest[:, :width], jnp.zeros((rows, width), F32)
    if sections == 2 and tick > 0:
        left = jnp.where(section == 1, following[-tick % sections].astype(F32), rest)
        carried = rest
    elif tick > 0:
        carried = rest[:, width:]
    came = tree_sum([arrival[:, :width] for arrival in arrivals]) + left
    came = came.astype(BF).astype(F32)
    h = jnp.where(section == 0, following[-(tick + 1) % sections].astype(F32), came)
    return h, jnp.where(section == 0, came, carried)


def later_kernel(count, tick, lengths_ref, *refs):
    arrivals, next_ref = refs[:count], refs[count]
    pieces, (w_ref, out_ref, carry_ref) = refs[count + 1 : -3], refs[-3:]
    h, emitted = arrive(arrivals, next_ref, tick - 1)
    width = h.shape[1]
    if carry_ref.shape[1] == width:
        first = jnp.full(h.shape, lax.axis_index("section")) == 0
        carry_ref[...] = jnp.where(first, emitted, h).astype(BF)
    else:
        carry_ref[:, :width] = h.astype(BF)
        carry_ref[:, width:] = emitted.astype(BF)
    blocks = 2 * h.shape[0] * width // (pieces[0].shape[1] * HD)
    query_sums([(tick - 1) * blocks] * len(pieces), lengths_ref[tick : tick + 1], h, pieces, w_ref, out_ref)


def later_sums(tick, lengths, arrivals, following, pieces, w):
    rows, width = following.shape[1:]
    parts = 1 if following.shape[0] == 2 else 2
    return pl.pallas_call(
        lambda *refs: later_kernel(len(arrivals), tick, *refs),
        out_shape=[shape((rows, 3 * w.shape[1] + HD)), shape((rows, width * parts))],
        in_specs=[VMEM] * (len(arrivals) + len(pieces) + 3),
        out_specs=[VMEM] * 2,
        compiler_params=PARAMS,
        cost_estimate=cost(24 * w.size, 2 * w.size),
    )(lengths, *arrivals, following, *pieces, w)


def last_kernel(count, *refs):
    state_ref, emitted_ref = refs[-2:]
    h, emitted = arrive(refs[:count], refs[count], refs[count].shape[0] - 1)
    state_ref[0] = h.astype(BF)
    emitted_ref[0] = emitted.astype(BF)


def last(arrivals, following):
    return pl.pallas_call(
        lambda *refs: last_kernel(len(arrivals), *refs),
        out_shape=[shape((1,) + following.shape[1:])] * 2,
        in_specs=[VMEM] * (len(arrivals) + 1),
        out_specs=[VMEM] * 2,
        compiler_params=PARAMS,
    )(*arrivals, following)


def attend_kernel(dims, turns, tick, *refs):
    sections, tensors, rows, kv_dev = dims
    count = len(turns)
    pieces, (carry_ref, w_ref), refs = refs[:count], refs[count : count + 2], refs[count + 2 :]
    caches, (out_ref, full_ref) = refs[:-2], refs[-2:]
    each = caches[0].shape[0] // tensors
    span = w_ref.shape[0]
    width = w_ref.shape[1]
    batch = batch_at(tick, sections)

    tails = [piece[:, 3 * span :].astype(F32) for piece in pieces]
    totals = [tail[:, 0:1] + tail[:, 1:2] + tail[:, 2:3] for tail in tails]
    squares = [tail[:, 3:4] + tail[:, 4:5] + tail[:, 5:6] for tail in tails]
    scale = 1.0 / (width * count)
    mean = tree_sum(totals) * scale
    rstd = lax.rsqrt(tree_sum(squares) * scale - mean * mean + 1e-05)
    query = tree_sum(
        [
            piece[:, :span].astype(F32)
            + (total * (1.0 / width) - mean) * piece[:, span : 2 * span].astype(F32)
            for piece, total in zip(pieces, totals)
        ]
    )
    query = rstd * query + tree_sum([piece[:, 2 * span : 3 * span] for piece in pieces])
    query = query.astype(BF).astype(F32)

    pos = caches[0].shape[2]
    tensor_at, replica_at = lax.axis_index("tensor"), lax.axis_index("replica")
    cols = lax.broadcasted_iota(jnp.int32, (rows, tensors * pos), 1)
    row = lax.broadcasted_iota(jnp.int32, (rows, tensors * pos), 0)
    spots = jnp.bitwise_xor(cols // pos, tensor_at) * pos + cols % pos
    spots = spots.astype(F32)
    keep = []
    for turn in turns:
        valid = jnp.logical_and(row == jnp.bitwise_xor(replica_at, turn), spots < tails[turn][:, 6:7])
        keep.append(jnp.where(valid, 0.0, -1e30))
    per_kv = span // HD // kv_dev
    keep = jnp.concatenate([jnp.concatenate(keep, 1)] * per_kv, 0)

    att = []
    for g in range(kv_dev):
        mine = jnp.concatenate(
            [query[:, h * HD : (h + 1) * HD] for h in range(g * per_kv, (g + 1) * per_kv)], 0
        ).astype(BF)
        keys, values = (
            jnp.concatenate(
                [
                    cache[i, (which * sections + batch) * kv_dev + g]
                    for cache in caches
                    for i in range(each * tensors)
                ],
                0,
            )
            for which in range(2)
        )
        scores = lax.dot_general(mine, keys, (((1,), (1,)), ((), ())), preferred_element_type=F32)
        scores = scores * (HD**-0.5) + keep
        probs = jnp.exp(scores - jnp.max(scores, axis=-1, keepdims=True))
        total = jnp.sum(probs, axis=-1, keepdims=True)
        got = jnp.dot(probs.astype(BF), values, preferred_element_type=F32) / total
        att += [got[h * rows : (h + 1) * rows] for h in range(per_kv)]
    att = jnp.concatenate(att, 1).astype(BF)
    for at in tiles(w_ref):
        got = jnp.dot(att, w_ref[:, at], preferred_element_type=F32).astype(BF)
        out_ref[:, at] = got
        full_ref[:, at] = got
    full_ref[:, width:] = carry_ref[...]


def attend(dims, turns, tick, pieces, caches, carry, w):
    rows, width = carry.shape[0], w.shape[1]
    return pl.pallas_call(
        lambda *refs: attend_kernel(dims, turns, tick, *refs),
        out_shape=[shape((rows, width)), shape((rows, width + carry.shape[1]))],
        in_specs=[VMEM] * (len(pieces) + len(caches) + 2),
        out_specs=[VMEM] * 2,
        compiler_params=PARAMS,
        cost_estimate=cost(8 * w.size, 2 * w.size),
    )(*pieces, carry, w, *caches)


def on_device(state, next_embed, tenant, lengths, gain, bias, wq, wo, keys, values):
    sections = lax.axis_size("section")
    tensors = lax.axis_size("tensor")
    replicas = lax.axis_size("replica")
    rows, width = state.shape[1:]
    heads_dev = wq.shape[2] // HD
    group = heads_dev * tensors // keys.shape[3]
    kv_dev = max(1, heads_dev // group)
    dims = (sections, tensors, rows, heads_dev, group, kv_dev)

    *packs, carry, following, lengths = pack(
        dims,
        tenant,
        lengths.reshape(-1),
        gain[0],
        bias[0],
        keys[0, :, 0],
        values[0, :, 0],
        state[0],
        next_embed,
    )
    got = [packs[0]] + [swapped(packs[d], "tensor", d) for d in range(1, tensors)]
    wq_held, wo_held = hold(wq[0], wo[0], packs[0])

    held = 2 * sections * kv_dev
    kv = join(got, held, [wq_held, wo_held])

    later = [piece[held + 2 * rows * width // (keys.shape[4] * HD) :] for piece in got[:NEAR]]
    bit = NEAR
    while bit < tensors:
        later = [sum(later)]
        later = later + [swapped(later[0], "tensor", bit)]
        bit *= 2
    turns, bit = [0], replicas // 2
    caches, waiting = [kv], None
    if bit:
        waiting = swapped(kv, "replica", bit)
    arrivals = None
    for tick in range(sections):
        if tick == 0:
            sums = first_sums(held, lengths, carry, got, wq_held, later[0] if later else kv)
        else:
            sums, carry = later_sums(tick, lengths, arrivals, following, later, wq_held)
        pieces = [sums] + [swapped(sums, "replica", d) for d in range(1, replicas)]
        if tick == 0:
            while bit:
                turns = turns + [turn ^ bit for turn in turns]
                caches, bit = [kv, waiting], bit // 2
                if bit:
                    both = join(caches, kv.shape[0], pieces[2:] + later[-1:])
                    kv = both.reshape((-1,) + both.shape[2:])
                    waiting = swapped(kv, "replica", bit)
        out, full = attend(
            (sections, tensors, rows, kv_dev), turns, tick, pieces, caches, carry, wo_held
        )
        arrivals = [from_behind(full, 0)] + [from_behind(out, d) for d in range(1, tensors)]
    return tuple(last(arrivals, following))


def solution(mesh):
    in_specs = (
        P("section", None, "replica"),
        P(None, None, "replica"),
        P(),
        P(None, "replica"),
        P("section", "tensor", "replica"),
        P("section", "tensor", "replica"),
        P("section", "replica", "tensor"),
        P("section", "tensor", "replica"),
        P("section", None, "replica", None, "tensor", None),
        P("section", None, "replica", None, "tensor", None),
    )
    out_specs = (P("section", None, "replica"), P("section", None, "replica"))
    return jax.shard_map(
        on_device, mesh=mesh, in_specs=in_specs, out_specs=out_specs, check_vma=False
    )
```

```python
import jax
import jax.numpy as jnp
from jax import lax
from jax.experimental import pallas as pl
from jax.experimental.pallas import tpu as pltpu
from jax.sharding import PartitionSpec as P

HD = 128
NEAR = 2
BF = jnp.bfloat16
F32 = jnp.float32
VMEM = pl.BlockSpec(memory_space=pltpu.VMEM)
SMEM = pl.BlockSpec(memory_space=pltpu.SMEM)
HBM = pl.BlockSpec(memory_space=pltpu.HBM)
PARAMS = pltpu.CompilerParams(vmem_limit_bytes=12 * 1024 * 1024)


def in_hbm(x):
    return pltpu.with_memory_space_constraint(x, pltpu.HBM)


def shape(dims, dtype=BF):
    return jax.ShapeDtypeStruct(tuple(dims), dtype)


def cost(flops, size):
    return pl.CostEstimate(flops=flops, bytes_accessed=size, transcendentals=0)


def swapped(block, axis, bits):
    route = [(i, i ^ bits) for i in range(lax.axis_size(axis))]
    return lax.ppermute(block, axis, route)


def from_behind(block, bits):
    sections, tensors = lax.axis_size("section"), lax.axis_size("tensor")
    route = [
        (s * tensors + (t ^ bits), (s + 1) % sections * tensors + t)
        for s in range(sections)
        for t in range(tensors)
    ]
    return lax.ppermute(block, ("section", "tensor"), route)


def tree_sum(pieces):
    pieces = [piece.astype(F32) for piece in pieces]
    while len(pieces) > 1:
        pieces = [pieces[i] + pieces[i + 1] for i in range(0, len(pieces), 2)]
    return pieces[0]


def batch_at(tick, sections):
    return lax.rem(lax.axis_index("section") + (sections - tick), sections)


def pack_kernel(dims, *refs):
    sections, tensors, rows, heads_dev, group, kv_dev = dims
    sources, refs = refs[:8], refs[8:]
    packs, (h_ref, next_ref, lengths_ref) = refs[:tensors], refs[tensors : tensors + 3]
    ids, lengths, gains, biases, keys, values, sems = refs[tensors + 3 :]
    held = 2 * sections * kv_dev
    targets = (ids, lengths, keys, values, gains, biases, h_ref, next_ref)
    copies = [
        pltpu.make_async_copy(source, target, sems.at[i])
        for i, (source, target) in enumerate(zip(sources, targets))
    ]
    for copy in copies:
        copy.start()
    at = lax.axis_index("tensor")
    tenants = gains.shape[0]
    count = sections * rows
    spot = lax.broadcasted_iota(jnp.int32, (count, tenants), 0)
    line = lax.broadcasted_iota(jnp.int32, lengths_ref.shape, 0)
    wanted = jnp.zeros((count, tenants), jnp.int32)
    kept = jnp.zeros(lengths_ref.shape, jnp.int32)
    copies[0].wait()
    copies[1].wait()
    for tick in range(sections):
        batch = batch_at(tick, sections)
        kept = jnp.where(line == tick, lengths[batch], kept)
        for i in range(rows):
            wanted = jnp.where(spot == tick * rows + i, ids[batch, i], wanted)
    lengths_ref[...] = kept.astype(F32)
    wanted = wanted - at * tenants
    onehot = jnp.where(wanted == lax.broadcasted_iota(jnp.int32, (count, tenants), 1), 1.0, 0.0)
    onehot = onehot.astype(BF)
    copies[2].wait()
    copies[3].wait()
    pos, lanes = keys.shape[2:]
    width = gains.shape[1]
    per = pos // (2 * rows)
    blocks = width // lanes // per
    for d in range(tensors):
        start = lax.bitwise_xor(at, d) * heads_dev // group
        for which, cache in enumerate((keys, values)):
            for b in range(sections):
                for g in range(kv_dev):
                    to = (which * sections + b) * kv_dev + g
                    packs[d][to] = cache[b, start + g]
    copies[4].wait()
    gain_rows = jnp.dot(onehot, gains[...], preferred_element_type=F32)
    copies[5].wait()
    bias_rows = jnp.dot(onehot, biases[...], preferred_element_type=F32)
    for tick in range(sections):
        mine = slice(tick * rows, (tick + 1) * rows)
        both = jnp.concatenate([gain_rows[mine], bias_rows[mine]], 0)
        for j in range(blocks):
            block = jnp.concatenate(
                [both[:, (j * per + k) * lanes : (j * per + k + 1) * lanes] for k in range(per)], 0
            ).astype(BF)
            for d in range(tensors if tick == 0 else min(tensors, NEAR)):
                packs[d][held + tick * blocks + j] = block
    copies[6].wait()
    copies[7].wait()


def pack(dims, tenant, lengths, gain, bias, keys, values, h, following):
    sections, tensors, rows, heads_dev, group, kv_dev = dims
    pos = keys.shape[2]
    blocks = 2 * rows * gain.shape[1] // (pos * HD)
    held, later = 2 * sections * kv_dev, (sections - 1) * blocks
    out_shape = [
        shape((held + blocks + (later if d < NEAR else 0), pos, HD)) for d in range(tensors)
    ]
    out_shape += [shape(h.shape), shape(following.shape), shape((sections, HD), F32)]
    operands = (tenant, lengths, keys, values, gain, bias, h, following)
    return pl.pallas_call(
        lambda *refs: pack_kernel(dims, *refs),
        out_shape=out_shape,
        in_specs=[HBM] * len(operands),
        out_specs=[VMEM] * len(out_shape),
        scratch_shapes=[pltpu.SMEM(x.shape, jnp.int32) for x in (tenant, lengths)]
        + [pltpu.VMEM(x.shape, BF) for x in (gain, bias, keys, values)]
        + [pltpu.SemaphoreType.DMA((len(operands),))],
        compiler_params=PARAMS,
        cost_estimate=cost(0, 4 * gain.size),
    )(*[in_hbm(x) for x in operands])


def join_kernel(count, size, refs):
    out_ref = refs[-1]
    for i in range(count):
        out_ref[i] = refs[i][:size]


def join(pieces, size, after):
    count = len(pieces)
    dims = pieces[0].shape
    return pl.pallas_call(
        lambda *refs: join_kernel(count, size, refs),
        out_shape=shape((count, size) + dims[1:]),
        in_specs=[VMEM] * count + [pl.BlockSpec(memory_space=pl.ANY)] * len(after),
        out_specs=VMEM,
        compiler_params=PARAMS,
    )(*pieces, *after)


def hold_kernel(parts, columns, after_ref, *refs):
    count = len(columns)
    copies = []
    sems = refs[-1]
    for source, target, (first, size) in zip(refs[:count], refs[count:-1], columns):
        rows = source.shape[0] // parts
        for i in range(parts):
            at = pl.ds(i * rows, rows)
            copies.append(
                pltpu.make_async_copy(
                    source.at[at, pl.ds(first, size)], target.at[at], sems.at[len(copies)]
                )
            )
    for copy in copies:
        copy.start()
    for copy in copies:
        copy.wait()


def hold(weights, columns, after):
    parts = 8
    total = sum(w.shape[0] * size for w, (_, size) in zip(weights, columns))
    return pl.pallas_call(
        lambda *refs: hold_kernel(parts, columns, *refs),
        out_shape=[pltpu.VMEM((w.shape[0], size), BF) for w, (_, size) in zip(weights, columns)],
        in_specs=[pl.BlockSpec(memory_space=pl.ANY)] + [HBM] * len(weights),
        out_specs=[VMEM] * len(weights),
        scratch_shapes=[pltpu.SemaphoreType.DMA((len(weights) * parts,))],
        compiler_params=PARAMS,
        cost_estimate=cost(0, 2 * total),
    )(after, *[in_hbm(w) for w in weights])


def tiles(w_ref):
    width = min(512, w_ref.shape[1])
    return [slice(i, i + width) for i in range(0, w_ref.shape[1], width)]


def thirds(x):
    high = x.astype(BF).astype(F32)
    middle = (x - high).astype(BF).astype(F32)
    return [high, middle, x - high - middle]


def query_sums(first_blocks, length, h, pieces, w_ref, out_ref):
    rows, width = h.shape
    pos, lanes = pieces[0].shape[1:]
    per = pos // (2 * rows)
    cols = []
    for j in range(width // lanes // per):
        block = tree_sum([piece[first + j] for first, piece in zip(first_blocks, pieces)])
        cols += [block[k * 2 * rows : (k + 1) * 2 * rows] for k in range(per)]
    affine = jnp.concatenate(cols, 1)
    total = jnp.sum(h, axis=-1, keepdims=True)
    squares = jnp.sum(h * h, axis=-1, keepdims=True)
    centred = (h - total * (1.0 / width)) * affine[:rows]
    x = jnp.concatenate([centred, affine], 0).astype(BF)
    count = w_ref.shape[1]
    for at in tiles(w_ref):
        got = jnp.dot(x, w_ref[:, at], preferred_element_type=F32)
        for k in range(3):
            to = slice(k * count + at.start, k * count + at.stop)
            out_ref[:, to] = got[k * rows : (k + 1) * rows].astype(BF)
    lane = lax.broadcasted_iota(jnp.int32, (rows, HD), 1)
    tail = jnp.broadcast_to(length, (rows, HD))
    for i, term in enumerate(thirds(total) + thirds(squares)):
        tail = jnp.where(lane == i, term, tail)
    out_ref[:, 3 * count :] = tail.astype(BF)


def first_kernel(tensors, held, lengths_ref, h_ref, *refs):
    pieces, (w_ref, out_ref) = refs[:tensors], refs[tensors:]
    query_sums([held] * tensors, lengths_ref[0:1], h_ref[...].astype(F32), pieces, w_ref, out_ref)


def first_sums(held, lengths, h, pieces, w):
    tensors = len(pieces)
    return pl.pallas_call(
        lambda *refs: first_kernel(tensors, held, *refs),
        out_shape=shape((h.shape[0], 3 * w.shape[1] + HD)),
        in_specs=[VMEM] * (tensors + 3),
        out_specs=VMEM,
        compiler_params=PARAMS,
        cost_estimate=cost(24 * w.size, 2 * w.size),
    )(lengths, h, *pieces, w)


def arrive(arrivals, following, tick):
    sections, rows, width = following.shape
    rest = arrivals[0][:, width:].astype(F32)
    section = jnp.full((rows, width), lax.axis_index("section"))
    left, carried = rest[:, :width], jnp.zeros((rows, width), F32)
    if sections == 2 and tick > 0:
        left = jnp.where(section == 1, following[-tick % sections].astype(F32), rest)
        carried = rest
    elif tick > 0:
        carried = rest[:, width:]
    came = tree_sum([arrival[:, :width] for arrival in arrivals]) + left
    came = came.astype(BF).astype(F32)
    h = jnp.where(section == 0, following[-(tick + 1) % sections].astype(F32), came)
    return h, jnp.where(section == 0, came, carried)


def later_kernel(count, tick, lengths_ref, *refs):
    arrivals, next_ref = refs[:count], refs[count]
    pieces, (w_ref, out_ref, carry_ref) = refs[count + 1 : -3], refs[-3:]
    h, emitted = arrive(arrivals, next_ref, tick - 1)
    width = h.shape[1]
    if carry_ref.shape[1] == width:
        first = jnp.full(h.shape, lax.axis_index("section")) == 0
        carry_ref[...] = jnp.where(first, emitted, h).astype(BF)
    else:
        carry_ref[:, :width] = h.astype(BF)
        carry_ref[:, width:] = emitted.astype(BF)
    blocks = 2 * h.shape[0] * width // (pieces[0].shape[1] * HD)
    query_sums([(tick - 1) * blocks] * len(pieces), lengths_ref[tick : tick + 1], h, pieces, w_ref, out_ref)


def later_sums(tick, lengths, arrivals, following, pieces, w):
    rows, width = following.shape[1:]
    parts = 1 if following.shape[0] == 2 else 2
    return pl.pallas_call(
        lambda *refs: later_kernel(len(arrivals), tick, *refs),
        out_shape=[shape((rows, 3 * w.shape[1] + HD)), shape((rows, width * parts))],
        in_specs=[VMEM] * (len(arrivals) + len(pieces) + 3),
        out_specs=[VMEM] * 2,
        compiler_params=PARAMS,
        cost_estimate=cost(24 * w.size, 2 * w.size),
    )(lengths, *arrivals, following, *pieces, w)


def last_kernel(count, *refs):
    state_ref, emitted_ref = refs[-2:]
    h, emitted = arrive(refs[:count], refs[count], refs[count].shape[0] - 1)
    state_ref[0] = h.astype(BF)
    emitted_ref[0] = emitted.astype(BF)


def last(arrivals, following):
    return pl.pallas_call(
        lambda *refs: last_kernel(len(arrivals), *refs),
        out_shape=[shape((1,) + following.shape[1:])] * 2,
        in_specs=[VMEM] * (len(arrivals) + 1),
        out_specs=[VMEM] * 2,
        compiler_params=PARAMS,
    )(*arrivals, following)


def attend_kernel(dims, turns, tick, *refs):
    sections, tensors, rows, kv_dev = dims
    count = len(turns)
    pieces, (carry_ref, *w_refs), refs = refs[:count], refs[count : count + 3], refs[count + 3 :]
    caches, (out_ref, full_ref) = refs[:-2], refs[-2:]
    each = caches[0].shape[0] // tensors
    span = w_refs[0].shape[0]
    half = w_refs[0].shape[1]
    width = 2 * half
    batch = batch_at(tick, sections)

    tails = [piece[:, 3 * span :].astype(F32) for piece in pieces]
    totals = [tail[:, 0:1] + tail[:, 1:2] + tail[:, 2:3] for tail in tails]
    squares = [tail[:, 3:4] + tail[:, 4:5] + tail[:, 5:6] for tail in tails]
    scale = 1.0 / (width * count)
    mean = tree_sum(totals) * scale
    rstd = lax.rsqrt(tree_sum(squares) * scale - mean * mean + 1e-05)
    query = tree_sum(
        [
            piece[:, :span].astype(F32)
            + (total * (1.0 / width) - mean) * piece[:, span : 2 * span].astype(F32)
            for piece, total in zip(pieces, totals)
        ]
    )
    query = rstd * query + tree_sum([piece[:, 2 * span : 3 * span] for piece in pieces])
    query = query.astype(BF).astype(F32)

    pos = caches[0].shape[2]
    tensor_at, replica_at = lax.axis_index("tensor"), lax.axis_index("replica")
    cols = lax.broadcasted_iota(jnp.int32, (rows, tensors * pos), 1)
    row = lax.broadcasted_iota(jnp.int32, (rows, tensors * pos), 0)
    spots = jnp.bitwise_xor(cols // pos, tensor_at) * pos + cols % pos
    spots = spots.astype(F32)
    keep = []
    for turn in turns:
        valid = jnp.logical_and(row == jnp.bitwise_xor(replica_at, turn), spots < tails[turn][:, 6:7])
        keep.append(jnp.where(valid, 0.0, -1e30))
    per_kv = span // HD // kv_dev
    keep = jnp.concatenate([jnp.concatenate(keep, 1)] * per_kv, 0)

    att = []
    for g in range(kv_dev):
        mine = jnp.concatenate(
            [query[:, h * HD : (h + 1) * HD] for h in range(g * per_kv, (g + 1) * per_kv)], 0
        ).astype(BF)
        keys, values = (
            jnp.concatenate(
                [
                    cache[i, (which * sections + batch) * kv_dev + g]
                    for cache in caches
                    for i in range(each * tensors)
                ],
                0,
            )
            for which in range(2)
        )
        scores = lax.dot_general(mine, keys, (((1,), (1,)), ((), ())), preferred_element_type=F32)
        scores = scores * (HD**-0.5) + keep
        probs = jnp.exp(scores - jnp.max(scores, axis=-1, keepdims=True))
        total = jnp.sum(probs, axis=-1, keepdims=True)
        got = jnp.dot(probs.astype(BF), values, preferred_element_type=F32) / total
        att += [got[h * rows : (h + 1) * rows] for h in range(per_kv)]
    att = jnp.concatenate(att, 1).astype(BF)
    for i, w_ref in enumerate(w_refs):
        for at in tiles(w_ref):
            got = jnp.dot(att, w_ref[:, at], preferred_element_type=F32).astype(BF)
            to = slice(i * half + at.start, i * half + at.stop)
            out_ref[:, to] = got
            full_ref[:, to] = got
    full_ref[:, width:] = carry_ref[...]


def attend(dims, turns, tick, pieces, caches, carry, left, right):
    rows, width = carry.shape[0], left.shape[1] + right.shape[1]
    return pl.pallas_call(
        lambda *refs: attend_kernel(dims, turns, tick, *refs),
        out_shape=[shape((rows, width)), shape((rows, width + carry.shape[1]))],
        in_specs=[VMEM] * (len(pieces) + len(caches) + 3),
        out_specs=[VMEM] * 2,
        compiler_params=PARAMS,
        cost_estimate=cost(16 * left.size, 4 * left.size),
    )(*pieces, carry, left, right, *caches)


def on_device(state, next_embed, tenant, lengths, gain, bias, wq, wo, keys, values):
    sections = lax.axis_size("section")
    tensors = lax.axis_size("tensor")
    replicas = lax.axis_size("replica")
    rows, width = state.shape[1:]
    heads_dev = wq.shape[2] // HD
    group = heads_dev * tensors // keys.shape[3]
    kv_dev = max(1, heads_dev // group)
    dims = (sections, tensors, rows, heads_dev, group, kv_dev)

    *packs, carry, following, lengths = pack(
        dims,
        tenant,
        lengths.reshape(-1),
        gain[0],
        bias[0],
        keys[0, :, 0],
        values[0, :, 0],
        state[0],
        next_embed,
    )
    got = [packs[0]] + [swapped(packs[d], "tensor", d) for d in range(1, tensors)]
    half = width // 2
    wq_held, wo_left = hold([wq[0], wo[0]], [(0, wq.shape[2]), (0, half)], packs[0])

    held = 2 * sections * kv_dev
    kv = join(got, held, [wq_held, wo_left])

    later = [piece[held + 2 * rows * width // (keys.shape[4] * HD) :] for piece in got[:NEAR]]
    bit = NEAR
    while bit < tensors:
        later = [sum(later)]
        later = later + [swapped(later[0], "tensor", bit)]
        bit *= 2
    turns, bit = [0], replicas // 2
    caches, waiting = [kv], None
    if bit:
        waiting = swapped(kv, "replica", bit)
    arrivals = None
    for tick in range(sections):
        if tick == 0:
            sums = first_sums(held, lengths, carry, got, wq_held)
        else:
            sums, carry = later_sums(tick, lengths, arrivals, following, later, wq_held)
        pieces = [sums] + [swapped(sums, "replica", d) for d in range(1, replicas)]
        if tick == 0:
            (wo_right,) = hold([wo[0]], [(half, half)], sums)
            while bit:
                turns = turns + [turn ^ bit for turn in turns]
                caches, bit = [kv, waiting], bit // 2
                if bit:
                    both = join(caches, kv.shape[0], pieces[2:] + [wo_right])
                    kv = both.reshape((-1,) + both.shape[2:])
                    waiting = swapped(kv, "replica", bit)
        out, full = attend(
            (sections, tensors, rows, kv_dev), turns, tick, pieces, caches, carry, wo_left, wo_right
        )
        arrivals = [from_behind(full, 0)] + [from_behind(out, d) for d in range(1, tensors)]
    return tuple(last(arrivals, following))


def solution(mesh):
    in_specs = (
        P("section", None, "replica"),
        P(None, None, "replica"),
        P(),
        P(None, "replica"),
        P("section", "tensor", "replica"),
        P("section", "tensor", "replica"),
        P("section", "replica", "tensor"),
        P("section", "tensor", "replica"),
        P("section", None, "replica", None, "tensor", None),
        P("section", None, "replica", None, "tensor", None),
    )
    out_specs = (P("section", None, "replica"), P("section", None, "replica"))
    return jax.shard_map(
        on_device, mesh=mesh, in_specs=in_specs, out_specs=out_specs, check_vma=False
    )
```

```python
import jax
import jax.numpy as jnp
from jax import lax
from jax.experimental import pallas as pl
from jax.experimental.pallas import tpu as pltpu
from jax.sharding import PartitionSpec as P

HD = 128
NEAR = 2
BF = jnp.bfloat16
F32 = jnp.float32
VMEM = pl.BlockSpec(memory_space=pltpu.VMEM)
SMEM = pl.BlockSpec(memory_space=pltpu.SMEM)
HBM = pl.BlockSpec(memory_space=pltpu.HBM)
PARAMS = pltpu.CompilerParams(vmem_limit_bytes=12 * 1024 * 1024)


def in_hbm(x):
    return pltpu.with_memory_space_constraint(x, pltpu.HBM)


def shape(dims, dtype=BF):
    return jax.ShapeDtypeStruct(tuple(dims), dtype)


def cost(flops, size):
    return pl.CostEstimate(flops=flops, bytes_accessed=size, transcendentals=0)


def swapped(block, axis, bits):
    route = [(i, i ^ bits) for i in range(lax.axis_size(axis))]
    return lax.ppermute(block, axis, route)


def from_behind(block, bits):
    sections, tensors = lax.axis_size("section"), lax.axis_size("tensor")
    route = [
        (s * tensors + (t ^ bits), (s + 1) % sections * tensors + t)
        for s in range(sections)
        for t in range(tensors)
    ]
    return lax.ppermute(block, ("section", "tensor"), route)


def tree_sum(pieces):
    pieces = [piece.astype(F32) for piece in pieces]
    while len(pieces) > 1:
        pieces = [pieces[i] + pieces[i + 1] for i in range(0, len(pieces), 2)]
    return pieces[0]


def batch_at(tick, sections):
    return lax.rem(lax.axis_index("section") + (sections - tick), sections)


def pack_kernel(dims, *refs):
    sections, tensors, rows, heads_dev, group, kv_dev = dims
    sources, refs = refs[:8], refs[8:]
    packs, (h_ref, next_ref, facts_ref) = refs[:tensors], refs[tensors : tensors + 3]
    ids, lengths, gains, biases, keys, values, sems = refs[tensors + 3 :]
    held = 2 * sections * kv_dev
    targets = (ids, lengths, keys, values, gains, biases, h_ref, next_ref)
    copies = [
        pltpu.make_async_copy(source, target, sems.at[i])
        for i, (source, target) in enumerate(zip(sources, targets))
    ]
    for copy in copies:
        copy.start()
    at = lax.axis_index("tensor")
    tenants = gains.shape[0]
    count = sections * rows
    spot = lax.broadcasted_iota(jnp.int32, (count, tenants), 0)
    lane = lax.broadcasted_iota(jnp.int32, facts_ref.shape, 1)
    wanted = jnp.zeros((count, tenants), jnp.int32)
    facts = jnp.zeros(facts_ref.shape, jnp.int32)
    copies[0].wait()
    copies[1].wait()
    for tick in range(sections):
        batch = batch_at(tick, sections)
        facts = jnp.where(lane == tick + 2, lengths[batch], facts)
        for i in range(rows):
            wanted = jnp.where(spot == tick * rows + i, ids[batch, i], wanted)
    wanted = wanted - at * tenants
    onehot = jnp.where(wanted == lax.broadcasted_iota(jnp.int32, (count, tenants), 1), 1.0, 0.0)
    onehot = onehot.astype(BF)
    copies[2].wait()
    copies[3].wait()
    pos, lanes = keys.shape[2:]
    width = gains.shape[1]
    per = pos // (2 * rows)
    blocks = width // lanes // per
    for d in range(tensors):
        start = lax.bitwise_xor(at, d) * heads_dev // group
        for which, cache in enumerate((keys, values)):
            for b in range(sections):
                for g in range(kv_dev):
                    to = (which * sections + b) * kv_dev + g
                    packs[d][to] = cache[b, start + g]
    copies[4].wait()
    gain_rows = jnp.dot(onehot, gains[...], preferred_element_type=F32)
    copies[5].wait()
    bias_rows = jnp.dot(onehot, biases[...], preferred_element_type=F32)
    for tick in range(sections):
        mine = slice(tick * rows, (tick + 1) * rows)
        both = jnp.concatenate([gain_rows[mine], bias_rows[mine]], 0)
        for j in range(blocks):
            block = jnp.concatenate(
                [both[:, (j * per + k) * lanes : (j * per + k + 1) * lanes] for k in range(per)], 0
            ).astype(BF)
            for d in range(tensors if tick == 0 else min(tensors, NEAR)):
                packs[d][held + tick * blocks + j] = block
    copies[6].wait()
    h = h_ref[...].astype(F32)
    facts = jnp.where(lane == 0, jnp.sum(h, axis=-1, keepdims=True), facts.astype(F32))
    facts_ref[...] = jnp.where(lane == 1, jnp.sum(h * h, axis=-1, keepdims=True), facts)
    copies[7].wait()


def pack(dims, tenant, lengths, gain, bias, keys, values, h, following):
    sections, tensors, rows, heads_dev, group, kv_dev = dims
    pos = keys.shape[2]
    blocks = 2 * rows * gain.shape[1] // (pos * HD)
    held, later = 2 * sections * kv_dev, (sections - 1) * blocks
    out_shape = [
        shape((held + blocks + (later if d < NEAR else 0), pos, HD)) for d in range(tensors)
    ]
    out_shape += [shape(h.shape), shape(following.shape), shape((rows, HD), F32)]
    operands = (tenant, lengths, keys, values, gain, bias, h, following)
    return pl.pallas_call(
        lambda *refs: pack_kernel(dims, *refs),
        out_shape=out_shape,
        in_specs=[HBM] * len(operands),
        out_specs=[VMEM] * len(out_shape),
        scratch_shapes=[pltpu.SMEM(x.shape, jnp.int32) for x in (tenant, lengths)]
        + [pltpu.VMEM(x.shape, BF) for x in (gain, bias, keys, values)]
        + [pltpu.SemaphoreType.DMA((len(operands),))],
        compiler_params=PARAMS,
        cost_estimate=cost(0, 4 * gain.size),
    )(*[in_hbm(x) for x in operands])


def join_kernel(count, size, refs):
    out_ref = refs[-1]
    for i in range(count):
        out_ref[i] = refs[i][:size]


def join(pieces, size, after):
    count = len(pieces)
    dims = pieces[0].shape
    return pl.pallas_call(
        lambda *refs: join_kernel(count, size, refs),
        out_shape=shape((count, size) + dims[1:], pieces[0].dtype),
        in_specs=[VMEM] * count + [pl.BlockSpec(memory_space=pl.ANY)] * len(after),
        out_specs=VMEM,
        compiler_params=PARAMS,
    )(*pieces, *after)


def hold_kernel(parts, columns, after_ref, *refs):
    count = len(columns)
    copies = []
    sems = refs[-1]
    for source, target, (first, size) in zip(refs[:count], refs[count:-1], columns):
        rows = source.shape[0] // parts
        for i in range(parts):
            at = pl.ds(i * rows, rows)
            copies.append(
                pltpu.make_async_copy(
                    source.at[at, pl.ds(first, size)], target.at[at], sems.at[len(copies)]
                )
            )
    for copy in copies:
        copy.start()
    for copy in copies:
        copy.wait()


def hold(weights, columns, after):
    parts = 8
    total = sum(w.shape[0] * size for w, (_, size) in zip(weights, columns))
    return pl.pallas_call(
        lambda *refs: hold_kernel(parts, columns, *refs),
        out_shape=[pltpu.VMEM((w.shape[0], size), BF) for w, (_, size) in zip(weights, columns)],
        in_specs=[pl.BlockSpec(memory_space=pl.ANY)] + [HBM] * len(weights),
        out_specs=[VMEM] * len(weights),
        scratch_shapes=[pltpu.SemaphoreType.DMA((len(weights) * parts,))],
        compiler_params=PARAMS,
        cost_estimate=cost(0, 2 * total),
    )(after, *[in_hbm(w) for w in weights])


def tiles(w_ref):
    width = min(512, w_ref.shape[1])
    return [slice(i, i + width) for i in range(0, w_ref.shape[1], width)]


def thirds(x):
    high = x.astype(BF).astype(F32)
    middle = (x - high).astype(BF).astype(F32)
    return [high, middle, x - high - middle]


def affine_rows(first, rows, width, pieces):
    pos, lanes = pieces[0].shape[1:]
    per = pos // (2 * rows)
    cols = []
    for j in range(width // lanes // per):
        block = tree_sum([piece[first + j] for piece in pieces])
        cols += [block[k * 2 * rows : (k + 1) * 2 * rows] for k in range(per)]
    return jnp.concatenate(cols, 1)


def scales(total, squares, width):
    mean = total * (1.0 / width)
    return mean, lax.rsqrt(squares * (1.0 / width) - mean * mean + 1e-05)


def query_sums(first, h, pieces, w_ref, out_ref):
    rows, width = h.shape
    affine = affine_rows(first, rows, width, pieces)
    total = jnp.sum(h, axis=-1, keepdims=True)
    squares = jnp.sum(h * h, axis=-1, keepdims=True)
    centred = (h - total * (1.0 / width)) * affine[:rows]
    x = jnp.concatenate([centred, affine], 0).astype(BF)
    count = w_ref.shape[1]
    for at in tiles(w_ref):
        got = jnp.dot(x, w_ref[:, at], preferred_element_type=F32)
        for k in range(3):
            to = slice(k * count + at.start, k * count + at.stop)
            out_ref[:, to] = got[k * rows : (k + 1) * rows].astype(BF)
    lane = lax.broadcasted_iota(jnp.int32, (rows, HD), 1)
    tail = jnp.zeros((rows, HD), F32)
    for i, term in enumerate(thirds(total) + thirds(squares)):
        tail = jnp.where(lane == i, term, tail)
    out_ref[:, 3 * count :] = tail.astype(BF)


def first_kernel(tensors, held, h_ref, *refs):
    pieces, facts, (w_ref, out_ref) = refs[:tensors], refs[tensors:-2], refs[-2:]
    rows, width = h_ref.shape
    facts = [ref[i] for ref in facts for i in range(ref.shape[0])]
    facts = tree_sum(facts)
    replicas = lax.axis_size("replica")
    mean, rstd = scales(facts[:, 0:1], facts[:, 1:2], width * replicas)
    affine = affine_rows(held, rows, width, pieces)
    x = (h_ref[...].astype(F32) - mean) * rstd * affine[:rows] + affine[rows:]
    x = x.astype(BF)
    for at in tiles(w_ref):
        out_ref[:, at] = jnp.dot(x, w_ref[:, at], preferred_element_type=F32).astype(BF)


def first_sums(held, h, pieces, facts, w):
    tensors = len(pieces)
    return pl.pallas_call(
        lambda *refs: first_kernel(tensors, held, *refs),
        out_shape=shape((h.shape[0], w.shape[1])),
        in_specs=[VMEM] * (tensors + len(facts) + 2),
        out_specs=VMEM,
        compiler_params=PARAMS,
        cost_estimate=cost(24 * w.size, 2 * w.size),
    )(h, *pieces, *facts, w)


def arrive(arrivals, following, tick):
    sections, rows, width = following.shape
    rest = arrivals[0][:, width:].astype(F32)
    section = jnp.full((rows, width), lax.axis_index("section"))
    left, carried = rest[:, :width], jnp.zeros((rows, width), F32)
    if sections == 2 and tick > 0:
        left = jnp.where(section == 1, following[-tick % sections].astype(F32), rest)
        carried = rest
    elif tick > 0:
        carried = rest[:, width:]
    came = tree_sum([arrival[:, :width] for arrival in arrivals]) + left
    came = came.astype(BF).astype(F32)
    h = jnp.where(section == 0, following[-(tick + 1) % sections].astype(F32), came)
    return h, jnp.where(section == 0, came, carried)


def later_kernel(count, tick, *refs):
    arrivals, next_ref = refs[:count], refs[count]
    pieces, (w_ref, out_ref, carry_ref) = refs[count + 1 : -3], refs[-3:]
    h, emitted = arrive(arrivals, next_ref, tick - 1)
    width = h.shape[1]
    if carry_ref.shape[1] == width:
        first = jnp.full(h.shape, lax.axis_index("section")) == 0
        carry_ref[...] = jnp.where(first, emitted, h).astype(BF)
    else:
        carry_ref[:, :width] = h.astype(BF)
        carry_ref[:, width:] = emitted.astype(BF)
    blocks = 2 * h.shape[0] * width // (pieces[0].shape[1] * HD)
    query_sums((tick - 1) * blocks, h, pieces, w_ref, out_ref)


def later_sums(tick, arrivals, following, pieces, w):
    rows, width = following.shape[1:]
    parts = 1 if following.shape[0] == 2 else 2
    return pl.pallas_call(
        lambda *refs: later_kernel(len(arrivals), tick, *refs),
        out_shape=[shape((rows, 3 * w.shape[1] + HD)), shape((rows, width * parts))],
        in_specs=[VMEM] * (len(arrivals) + len(pieces) + 2),
        out_specs=[VMEM] * 2,
        compiler_params=PARAMS,
        cost_estimate=cost(24 * w.size, 2 * w.size),
    )(*arrivals, following, *pieces, w)


def last_kernel(count, *refs):
    state_ref, emitted_ref = refs[-2:]
    h, emitted = arrive(refs[:count], refs[count], refs[count].shape[0] - 1)
    state_ref[0] = h.astype(BF)
    emitted_ref[0] = emitted.astype(BF)


def last(arrivals, following):
    return pl.pallas_call(
        lambda *refs: last_kernel(len(arrivals), *refs),
        out_shape=[shape((1,) + following.shape[1:])] * 2,
        in_specs=[VMEM] * (len(arrivals) + 1),
        out_specs=[VMEM] * 2,
        compiler_params=PARAMS,
    )(*arrivals, following)


def attend_kernel(dims, turns, tick, *refs):
    sections, tensors, rows, kv_dev = dims
    count = len(turns)
    pieces, (carry_ref, *w_refs), refs = refs[:count], refs[count : count + 3], refs[count + 3 :]
    (out_ref, full_ref), refs = refs[-2:], refs[:-2]
    caches, facts = refs[: len(refs) // 2], refs[len(refs) // 2 :]
    each = caches[0].shape[0] // tensors
    facts = [ref[i] for ref in facts for i in range(ref.shape[0])]
    span = w_refs[0].shape[0]
    half = w_refs[0].shape[1]
    width = 2 * half
    batch = batch_at(tick, sections)

    if tick == 0:
        query = tree_sum([piece[...] for piece in pieces])
    else:
        tails = [piece[:, 3 * span :].astype(F32) for piece in pieces]
        totals = [tail[:, 0:1] + tail[:, 1:2] + tail[:, 2:3] for tail in tails]
        squares = [tail[:, 3:4] + tail[:, 4:5] + tail[:, 5:6] for tail in tails]
        mean, rstd = scales(tree_sum(totals), tree_sum(squares), width * count)
        query = tree_sum(
            [
                piece[:, :span].astype(F32)
                + (total * (1.0 / width) - mean) * piece[:, span : 2 * span].astype(F32)
                for piece, total in zip(pieces, totals)
            ]
        )
        query = rstd * query + tree_sum([piece[:, 2 * span : 3 * span] for piece in pieces])
    query = query.astype(BF).astype(F32)

    pos = caches[0].shape[2]
    tensor_at, replica_at = lax.axis_index("tensor"), lax.axis_index("replica")
    cols = lax.broadcasted_iota(jnp.int32, (rows, tensors * pos), 1)
    row = lax.broadcasted_iota(jnp.int32, (rows, tensors * pos), 0)
    spots = jnp.bitwise_xor(cols // pos, tensor_at) * pos + cols % pos
    spots = spots.astype(F32)
    keep = []
    for turn, fact in zip(turns, facts):
        length = fact[:, tick + 2 : tick + 3]
        valid = jnp.logical_and(row == jnp.bitwise_xor(replica_at, turn), spots < length)
        keep.append(jnp.where(valid, 0.0, -1e30))
    per_kv = span // HD // kv_dev
    keep = jnp.concatenate([jnp.concatenate(keep, 1)] * per_kv, 0)

    att = []
    for g in range(kv_dev):
        mine = jnp.concatenate(
            [query[:, h * HD : (h + 1) * HD] for h in range(g * per_kv, (g + 1) * per_kv)], 0
        ).astype(BF)
        keys, values = (
            jnp.concatenate(
                [
                    cache[i, (which * sections + batch) * kv_dev + g]
                    for cache in caches
                    for i in range(each * tensors)
                ],
                0,
            )
            for which in range(2)
        )
        scores = lax.dot_general(mine, keys, (((1,), (1,)), ((), ())), preferred_element_type=F32)
        scores = scores * (HD**-0.5) + keep
        probs = jnp.exp(scores - jnp.max(scores, axis=-1, keepdims=True))
        total = jnp.sum(probs, axis=-1, keepdims=True)
        got = jnp.dot(probs.astype(BF), values, preferred_element_type=F32) / total
        att += [got[h * rows : (h + 1) * rows] for h in range(per_kv)]
    att = jnp.concatenate(att, 1).astype(BF)
    for i, w_ref in enumerate(w_refs):
        for at in tiles(w_ref):
            got = jnp.dot(att, w_ref[:, at], preferred_element_type=F32).astype(BF)
            to = slice(i * half + at.start, i * half + at.stop)
            out_ref[:, to] = got
            full_ref[:, to] = got
    full_ref[:, width:] = carry_ref[...]


def attend(dims, turns, tick, pieces, caches, facts, carry, left, right):
    rows, width = carry.shape[0], left.shape[1] + right.shape[1]
    return pl.pallas_call(
        lambda *refs: attend_kernel(dims, turns, tick, *refs),
        out_shape=[shape((rows, width)), shape((rows, width + carry.shape[1]))],
        in_specs=[VMEM] * (len(pieces) + len(caches) + len(facts) + 3),
        out_specs=[VMEM] * 2,
        compiler_params=PARAMS,
        cost_estimate=cost(16 * left.size, 4 * left.size),
    )(*pieces, carry, left, right, *caches, *facts)


def on_device(state, next_embed, tenant, lengths, gain, bias, wq, wo, keys, values):
    sections = lax.axis_size("section")
    tensors = lax.axis_size("tensor")
    replicas = lax.axis_size("replica")
    rows, width = state.shape[1:]
    heads_dev = wq.shape[2] // HD
    group = heads_dev * tensors // keys.shape[3]
    kv_dev = max(1, heads_dev // group)
    dims = (sections, tensors, rows, heads_dev, group, kv_dev)

    *packs, carry, following, facts = pack(
        dims,
        tenant,
        lengths.reshape(-1),
        gain[0],
        bias[0],
        keys[0, :, 0],
        values[0, :, 0],
        state[0],
        next_embed,
    )
    got = [packs[0]] + [swapped(packs[d], "tensor", d) for d in range(1, tensors)]
    half = width // 2
    (wq_held,) = hold([wq[0]], [(0, wq.shape[2])], packs[0])

    facts = [facts[None]]
    bit = replicas // 2
    while bit:
        if len(facts) > 1:
            both = join(facts, facts[0].shape[0], [wq_held])
            facts = [both.reshape((-1,) + both.shape[2:])]
        facts = [facts[0], swapped(facts[0], "replica", bit)]
        bit //= 2
    (wo_left,) = hold([wo[0]], [(0, half)], facts[0])

    held = 2 * sections * kv_dev
    kv = join(got, held, [wo_left, facts[-1]])

    later = [piece[held + 2 * rows * width // (keys.shape[4] * HD) :] for piece in got[:NEAR]]
    bit = NEAR
    while bit < tensors:
        later = [sum(later)]
        later = later + [swapped(later[0], "tensor", bit)]
        bit *= 2
    turns, bit = [0], replicas // 2
    caches, waiting = [kv], None
    if bit:
        waiting = swapped(kv, "replica", bit)
    arrivals = None
    for tick in range(sections):
        if tick == 0:
            sums = first_sums(held, carry, got, facts, wq_held)
        else:
            sums, carry = later_sums(tick, arrivals, following, later, wq_held)
        pieces = [sums] + [swapped(sums, "replica", d) for d in range(1, replicas)]
        if tick == 0:
            (wo_right,) = hold([wo[0]], [(half, half)], sums)
            while bit:
                turns = turns + [turn ^ bit for turn in turns]
                caches, bit = [kv, waiting], bit // 2
                if bit:
                    both = join(caches, kv.shape[0], pieces[2:] + [wo_right])
                    kv = both.reshape((-1,) + both.shape[2:])
                    waiting = swapped(kv, "replica", bit)
        out, full = attend(
            (sections, tensors, rows, kv_dev), turns, tick, pieces, caches, facts, carry, wo_left, wo_right
        )
        arrivals = [from_behind(full, 0)] + [from_behind(out, d) for d in range(1, tensors)]
    return tuple(last(arrivals, following))


def solution(mesh):
    in_specs = (
        P("section", None, "replica"),
        P(None, None, "replica"),
        P(),
        P(None, "replica"),
        P("section", "tensor", "replica"),
        P("section", "tensor", "replica"),
        P("section", "replica", "tensor"),
        P("section", "tensor", "replica"),
        P("section", None, "replica", None, "tensor", None),
        P("section", None, "replica", None, "tensor", None),
    )
    out_specs = (P("section", None, "replica"), P("section", None, "replica"))
    return jax.shard_map(
        on_device, mesh=mesh, in_specs=in_specs, out_specs=out_specs, check_vma=False
    )
```

```python
import jax
import jax.numpy as jnp
from jax import lax
from jax.experimental import pallas as pl
from jax.experimental.pallas import tpu as pltpu
from jax.sharding import PartitionSpec as P

HD = 128
NEAR = 2
BF = jnp.bfloat16
F32 = jnp.float32
VMEM = pl.BlockSpec(memory_space=pltpu.VMEM)
SMEM = pl.BlockSpec(memory_space=pltpu.SMEM)
HBM = pl.BlockSpec(memory_space=pltpu.HBM)
PARAMS = pltpu.CompilerParams(vmem_limit_bytes=12 * 1024 * 1024)


def in_hbm(x):
    return pltpu.with_memory_space_constraint(x, pltpu.HBM)


def shape(dims, dtype=BF):
    return jax.ShapeDtypeStruct(tuple(dims), dtype)


def cost(flops, size):
    return pl.CostEstimate(flops=flops, bytes_accessed=size, transcendentals=0)


def swapped(block, axis, bits):
    route = [(i, i ^ bits) for i in range(lax.axis_size(axis))]
    return lax.ppermute(block, axis, route)


def from_behind(block, bits):
    sections, tensors = lax.axis_size("section"), lax.axis_size("tensor")
    route = [
        (s * tensors + (t ^ bits), (s + 1) % sections * tensors + t)
        for s in range(sections)
        for t in range(tensors)
    ]
    return lax.ppermute(block, ("section", "tensor"), route)


def tree_sum(pieces):
    pieces = [piece.astype(F32) for piece in pieces]
    while len(pieces) > 1:
        pieces = [pieces[i] + pieces[i + 1] for i in range(0, len(pieces), 2)]
    return pieces[0]


def batch_at(tick, sections):
    return lax.rem(lax.axis_index("section") + (sections - tick), sections)


def pack_kernel(dims, *refs):
    sections, tensors, rows, heads_dev, group, kv_dev = dims
    sources, refs = refs[:8], refs[8:]
    packs, (h_ref, next_ref, lengths_ref) = refs[:tensors], refs[tensors : tensors + 3]
    ids, lengths, gains, biases, keys, values, sems = refs[tensors + 3 :]
    held = 2 * sections * kv_dev
    targets = (ids, lengths, keys, values, gains, biases, h_ref, next_ref)
    copies = [
        pltpu.make_async_copy(source, target, sems.at[i])
        for i, (source, target) in enumerate(zip(sources, targets))
    ]
    for copy in copies:
        copy.start()
    at = lax.axis_index("tensor")
    tenants = gains.shape[0]
    count = sections * rows
    spot = lax.broadcasted_iota(jnp.int32, (count, tenants), 0)
    line = lax.broadcasted_iota(jnp.int32, lengths_ref.shape, 0)
    wanted = jnp.zeros((count, tenants), jnp.int32)
    kept = jnp.zeros(lengths_ref.shape, jnp.int32)
    copies[0].wait()
    copies[1].wait()
    for tick in range(sections):
        batch = batch_at(tick, sections)
        kept = jnp.where(line == tick, lengths[batch], kept)
        for i in range(rows):
            wanted = jnp.where(spot == tick * rows + i, ids[batch, i], wanted)
    lengths_ref[...] = kept.astype(F32)
    wanted = wanted - at * tenants
    onehot = jnp.where(wanted == lax.broadcasted_iota(jnp.int32, (count, tenants), 1), 1.0, 0.0)
    onehot = onehot.astype(BF)
    copies[2].wait()
    copies[3].wait()
    pos, lanes = keys.shape[2:]
    width = gains.shape[1]
    per = pos // (2 * rows)
    blocks = width // lanes // per
    for d in range(tensors):
        start = lax.bitwise_xor(at, d) * heads_dev // group
        for which, cache in enumerate((keys, values)):
            for b in range(sections):
                for g in range(kv_dev):
                    to = (which * sections + b) * kv_dev + g
                    packs[d][to] = cache[b, start + g]
    copies[4].wait()
    gain_rows = jnp.dot(onehot, gains[...], preferred_element_type=F32)
    copies[5].wait()
    bias_rows = jnp.dot(onehot, biases[...], preferred_element_type=F32)
    for tick in range(sections):
        mine = slice(tick * rows, (tick + 1) * rows)
        both = jnp.concatenate([gain_rows[mine], bias_rows[mine]], 0)
        for j in range(blocks):
            block = jnp.concatenate(
                [both[:, (j * per + k) * lanes : (j * per + k + 1) * lanes] for k in range(per)], 0
            ).astype(BF)
            for d in range(tensors if tick == 0 else min(tensors, NEAR)):
                packs[d][held + tick * blocks + j] = block
    copies[6].wait()
    copies[7].wait()


def pack(dims, tenant, lengths, gain, bias, keys, values, h, following):
    sections, tensors, rows, heads_dev, group, kv_dev = dims
    pos = keys.shape[2]
    blocks = 2 * rows * gain.shape[1] // (pos * HD)
    held, later = 2 * sections * kv_dev, (sections - 1) * blocks
    out_shape = [
        shape((held + blocks + (later if d < NEAR else 0), pos, HD)) for d in range(tensors)
    ]
    out_shape += [shape(h.shape), shape(following.shape), shape((sections, HD), F32)]
    operands = (tenant, lengths, keys, values, gain, bias, h, following)
    return pl.pallas_call(
        lambda *refs: pack_kernel(dims, *refs),
        out_shape=out_shape,
        in_specs=[HBM] * len(operands),
        out_specs=[VMEM] * len(out_shape),
        scratch_shapes=[pltpu.SMEM(x.shape, jnp.int32) for x in (tenant, lengths)]
        + [pltpu.VMEM(x.shape, BF) for x in (gain, bias, keys, values)]
        + [pltpu.SemaphoreType.DMA((len(operands),))],
        compiler_params=PARAMS,
        cost_estimate=cost(0, 4 * gain.size),
    )(*[in_hbm(x) for x in operands])


def join_kernel(count, size, refs):
    out_ref = refs[-1]
    for i in range(count):
        out_ref[i] = refs[i][:size]


def join(pieces, size, after):
    count = len(pieces)
    dims = pieces[0].shape
    return pl.pallas_call(
        lambda *refs: join_kernel(count, size, refs),
        out_shape=shape((count, size) + dims[1:]),
        in_specs=[VMEM] * count + [pl.BlockSpec(memory_space=pl.ANY)] * len(after),
        out_specs=VMEM,
        compiler_params=PARAMS,
    )(*pieces, *after)


def hold_kernel(parts, columns, after_ref, *refs):
    count = len(columns)
    copies = []
    sems = refs[-1]
    for source, target, (first, size) in zip(refs[:count], refs[count:-1], columns):
        rows = source.shape[0] // parts
        for i in range(parts):
            at = pl.ds(i * rows, rows)
            copies.append(
                pltpu.make_async_copy(
                    source.at[at, pl.ds(first, size)], target.at[at], sems.at[len(copies)]
                )
            )
    for copy in copies:
        copy.start()
    for copy in copies:
        copy.wait()


def hold(weights, columns, after):
    parts = 8
    total = sum(w.shape[0] * size for w, (_, size) in zip(weights, columns))
    return pl.pallas_call(
        lambda *refs: hold_kernel(parts, columns, *refs),
        out_shape=[pltpu.VMEM((w.shape[0], size), BF) for w, (_, size) in zip(weights, columns)],
        in_specs=[pl.BlockSpec(memory_space=pl.ANY)] + [HBM] * len(weights),
        out_specs=[VMEM] * len(weights),
        scratch_shapes=[pltpu.SemaphoreType.DMA((len(weights) * parts,))],
        compiler_params=PARAMS,
        cost_estimate=cost(0, 2 * total),
    )(after, *[in_hbm(w) for w in weights])


def tiles(w_ref):
    width = min(512, w_ref.shape[1])
    return [slice(i, i + width) for i in range(0, w_ref.shape[1], width)]


def thirds(x):
    high = x.astype(BF).astype(F32)
    middle = (x - high).astype(BF).astype(F32)
    return [high, middle, x - high - middle]


def query_sums(first_blocks, length, h, pieces, w_ref, out_ref):
    rows, width = h.shape
    pos, lanes = pieces[0].shape[1:]
    per = pos // (2 * rows)
    cols = []
    for j in range(width // lanes // per):
        block = tree_sum([piece[first + j] for first, piece in zip(first_blocks, pieces)])
        cols += [block[k * 2 * rows : (k + 1) * 2 * rows] for k in range(per)]
    affine = jnp.concatenate(cols, 1)
    total = jnp.sum(h, axis=-1, keepdims=True)
    squares = jnp.sum(h * h, axis=-1, keepdims=True)
    centred = (h - total * (1.0 / width)) * affine[:rows]
    x = jnp.concatenate([centred, affine], 0).astype(BF)
    count = w_ref.shape[1]
    for at in tiles(w_ref):
        got = jnp.dot(x, w_ref[:, at], preferred_element_type=F32)
        for k in range(3):
            to = slice(k * count + at.start, k * count + at.stop)
            out_ref[:, to] = got[k * rows : (k + 1) * rows].astype(BF)
    lane = lax.broadcasted_iota(jnp.int32, (rows, HD), 1)
    tail = jnp.broadcast_to(length, (rows, HD))
    for i, term in enumerate(thirds(total) + thirds(squares)):
        tail = jnp.where(lane == i, term, tail)
    out_ref[:, 3 * count :] = tail.astype(BF)


def first_kernel(tensors, held, lengths_ref, h_ref, *refs):
    pieces, (w_ref, out_ref) = refs[:tensors], refs[tensors:]
    query_sums([held] * tensors, lengths_ref[0:1], h_ref[...].astype(F32), pieces, w_ref, out_ref)


def first_sums(held, lengths, h, pieces, w):
    tensors = len(pieces)
    return pl.pallas_call(
        lambda *refs: first_kernel(tensors, held, *refs),
        out_shape=shape((h.shape[0], 3 * w.shape[1] + HD)),
        in_specs=[VMEM] * (tensors + 3),
        out_specs=VMEM,
        compiler_params=PARAMS,
        cost_estimate=cost(24 * w.size, 2 * w.size),
    )(lengths, h, *pieces, w)


def arrive(arrivals, following, tick):
    sections, rows, width = following.shape
    if arrivals[0].shape[1] == width:
        arrivals, rest = arrivals[:-1], arrivals[-1][...].astype(F32)
    else:
        rest = arrivals[0][:, width:].astype(F32)
    section = jnp.full((rows, width), lax.axis_index("section"))
    left, carried = rest[:, :width], jnp.zeros((rows, width), F32)
    if sections == 2 and tick > 0:
        left = jnp.where(section == 1, following[-tick % sections].astype(F32), rest)
        carried = rest
    elif tick > 0:
        carried = rest[:, width:]
    came = tree_sum([arrival[:, :width] for arrival in arrivals]) + left
    came = came.astype(BF).astype(F32)
    h = jnp.where(section == 0, following[-(tick + 1) % sections].astype(F32), came)
    return h, jnp.where(section == 0, came, carried)


def later_kernel(count, tick, lengths_ref, *refs):
    arrivals, next_ref = refs[:count], refs[count]
    pieces, (w_ref, out_ref, carry_ref) = refs[count + 1 : -3], refs[-3:]
    h, emitted = arrive(arrivals, next_ref, tick - 1)
    width = h.shape[1]
    if carry_ref.shape[1] == width:
        first = jnp.full(h.shape, lax.axis_index("section")) == 0
        carry_ref[...] = jnp.where(first, emitted, h).astype(BF)
    else:
        carry_ref[:, :width] = h.astype(BF)
        carry_ref[:, width:] = emitted.astype(BF)
    blocks = 2 * h.shape[0] * width // (pieces[0].shape[1] * HD)
    query_sums([(tick - 1) * blocks] * len(pieces), lengths_ref[tick : tick + 1], h, pieces, w_ref, out_ref)


def later_sums(tick, lengths, arrivals, following, pieces, w):
    rows, width = following.shape[1:]
    parts = 1 if following.shape[0] == 2 else 2
    return pl.pallas_call(
        lambda *refs: later_kernel(len(arrivals), tick, *refs),
        out_shape=[shape((rows, 3 * w.shape[1] + HD)), shape((rows, width * parts))],
        in_specs=[VMEM] * (len(arrivals) + len(pieces) + 3),
        out_specs=[VMEM] * 2,
        compiler_params=PARAMS,
        cost_estimate=cost(24 * w.size, 2 * w.size),
    )(lengths, *arrivals, following, *pieces, w)


def last_kernel(count, *refs):
    state_ref, emitted_ref = refs[-2:]
    h, emitted = arrive(refs[:count], refs[count], refs[count].shape[0] - 1)
    state_ref[0] = h.astype(BF)
    emitted_ref[0] = emitted.astype(BF)


def last(arrivals, following):
    return pl.pallas_call(
        lambda *refs: last_kernel(len(arrivals), *refs),
        out_shape=[shape((1,) + following.shape[1:])] * 2,
        in_specs=[VMEM] * (len(arrivals) + 1),
        out_specs=[VMEM] * 2,
        compiler_params=PARAMS,
    )(*arrivals, following)


def attend_kernel(dims, turns, tick, *refs):
    sections, tensors, rows, kv_dev = dims
    count = len(turns)
    pieces, (carry_ref, *w_refs), refs = refs[:count], refs[count : count + 3], refs[count + 3 :]
    caches, (out_ref, full_ref) = refs[:-2], refs[-2:]
    each = caches[0].shape[0] // tensors
    span = w_refs[0].shape[0]
    half = w_refs[0].shape[1]
    width = 2 * half
    batch = batch_at(tick, sections)

    tails = [piece[:, 3 * span :].astype(F32) for piece in pieces]
    totals = [tail[:, 0:1] + tail[:, 1:2] + tail[:, 2:3] for tail in tails]
    squares = [tail[:, 3:4] + tail[:, 4:5] + tail[:, 5:6] for tail in tails]
    scale = 1.0 / (width * count)
    mean = tree_sum(totals) * scale
    rstd = lax.rsqrt(tree_sum(squares) * scale - mean * mean + 1e-05)
    query = tree_sum(
        [
            piece[:, :span].astype(F32)
            + (total * (1.0 / width) - mean) * piece[:, span : 2 * span].astype(F32)
            for piece, total in zip(pieces, totals)
        ]
    )
    query = rstd * query + tree_sum([piece[:, 2 * span : 3 * span] for piece in pieces])
    query = query.astype(BF).astype(F32)

    pos = caches[0].shape[2]
    tensor_at, replica_at = lax.axis_index("tensor"), lax.axis_index("replica")
    cols = lax.broadcasted_iota(jnp.int32, (rows, tensors * pos), 1)
    row = lax.broadcasted_iota(jnp.int32, (rows, tensors * pos), 0)
    spots = jnp.bitwise_xor(cols // pos, tensor_at) * pos + cols % pos
    spots = spots.astype(F32)
    keep = []
    for turn in turns:
        valid = jnp.logical_and(row == jnp.bitwise_xor(replica_at, turn), spots < tails[turn][:, 6:7])
        keep.append(jnp.where(valid, 0.0, -1e30))
    per_kv = span // HD // kv_dev
    keep = jnp.concatenate([jnp.concatenate(keep, 1)] * per_kv, 0)

    att = []
    for g in range(kv_dev):
        mine = jnp.concatenate(
            [query[:, h * HD : (h + 1) * HD] for h in range(g * per_kv, (g + 1) * per_kv)], 0
        ).astype(BF)
        keys, values = (
            jnp.concatenate(
                [
                    cache[i, (which * sections + batch) * kv_dev + g]
                    for cache in caches
                    for i in range(each * tensors)
                ],
                0,
            )
            for which in range(2)
        )
        scores = lax.dot_general(mine, keys, (((1,), (1,)), ((), ())), preferred_element_type=F32)
        scores = scores * (HD**-0.5) + keep
        probs = jnp.exp(scores - jnp.max(scores, axis=-1, keepdims=True))
        total = jnp.sum(probs, axis=-1, keepdims=True)
        got = jnp.dot(probs.astype(BF), values, preferred_element_type=F32) / total
        att += [got[h * rows : (h + 1) * rows] for h in range(per_kv)]
    att = jnp.concatenate(att, 1).astype(BF)
    for i, w_ref in enumerate(w_refs):
        for at in tiles(w_ref):
            got = jnp.dot(att, w_ref[:, at], preferred_element_type=F32).astype(BF)
            to = slice(i * half + at.start, i * half + at.stop)
            out_ref[:, to] = got
            full_ref[:, to] = got
    full_ref[:, width:] = carry_ref[...]


def attend(dims, turns, tick, pieces, caches, carry, left, right):
    rows, width = carry.shape[0], left.shape[1] + right.shape[1]
    return pl.pallas_call(
        lambda *refs: attend_kernel(dims, turns, tick, *refs),
        out_shape=[shape((rows, width)), shape((rows, width + carry.shape[1]))],
        in_specs=[VMEM] * (len(pieces) + len(caches) + 3),
        out_specs=[VMEM] * 2,
        compiler_params=PARAMS,
        cost_estimate=cost(16 * left.size, 4 * left.size),
    )(*pieces, carry, left, right, *caches)


def on_device(state, next_embed, tenant, lengths, gain, bias, wq, wo, keys, values):
    sections = lax.axis_size("section")
    tensors = lax.axis_size("tensor")
    replicas = lax.axis_size("replica")
    rows, width = state.shape[1:]
    heads_dev = wq.shape[2] // HD
    group = heads_dev * tensors // keys.shape[3]
    kv_dev = max(1, heads_dev // group)
    dims = (sections, tensors, rows, heads_dev, group, kv_dev)

    *packs, carry, following, lengths = pack(
        dims,
        tenant,
        lengths.reshape(-1),
        gain[0],
        bias[0],
        keys[0, :, 0],
        values[0, :, 0],
        state[0],
        next_embed,
    )
    got = [packs[0]] + [swapped(packs[d], "tensor", d) for d in range(1, tensors)]
    half = width // 2
    wq_held, wo_left = hold([wq[0], wo[0]], [(0, wq.shape[2]), (0, half)], packs[0])

    held = 2 * sections * kv_dev
    kv = join(got, held, [wq_held, wo_left])

    later = [piece[held + 2 * rows * width // (keys.shape[4] * HD) :] for piece in got[:NEAR]]
    bit = NEAR
    while bit < tensors:
        later = [sum(later)]
        later = later + [swapped(later[0], "tensor", bit)]
        bit *= 2
    turns, bit = [0], replicas // 2
    caches, waiting = [kv], None
    if bit:
        waiting = swapped(kv, "replica", bit)
    arrivals = None
    for tick in range(sections):
        if tick == 0:
            sums = first_sums(held, lengths, carry, got, wq_held)
        else:
            sums, carry = later_sums(tick, lengths, arrivals, following, later, wq_held)
        pieces = [sums] + [swapped(sums, "replica", d) for d in range(1, replicas)]
        if tick == 0:
            behind = from_behind(carry, 0)
            (wo_right,) = hold([wo[0]], [(half, half)], sums)
            while bit:
                turns = turns + [turn ^ bit for turn in turns]
                caches, bit = [kv, waiting], bit // 2
                if bit:
                    both = join(caches, kv.shape[0], pieces[2:] + [wo_right, behind])
                    kv = both.reshape((-1,) + both.shape[2:])
                    waiting = swapped(kv, "replica", bit)
        out, full = attend(
            (sections, tensors, rows, kv_dev), turns, tick, pieces, caches, carry, wo_left, wo_right
        )
        arrivals = [from_behind(out if tick == 0 else full, 0)]
        arrivals += [from_behind(out, d) for d in range(1, tensors)]
        if tick == 0:
            arrivals += [behind]
    return tuple(last(arrivals, following))


def solution(mesh):
    in_specs = (
        P("section", None, "replica"),
        P(None, None, "replica"),
        P(),
        P(None, "replica"),
        P("section", "tensor", "replica"),
        P("section", "tensor", "replica"),
        P("section", "replica", "tensor"),
        P("section", "tensor", "replica"),
        P("section", None, "replica", None, "tensor", None),
        P("section", None, "replica", None, "tensor", None),
    )
    out_specs = (P("section", None, "replica"), P("section", None, "replica"))
    return jax.shard_map(
        on_device, mesh=mesh, in_specs=in_specs, out_specs=out_specs, check_vma=False
    )
```

```python
import jax
import jax.numpy as jnp
from jax import lax
from jax.experimental import pallas as pl
from jax.experimental.pallas import tpu as pltpu
from jax.sharding import PartitionSpec as P

HD = 128
NEAR = 2
BF = jnp.bfloat16
F32 = jnp.float32
VMEM = pl.BlockSpec(memory_space=pltpu.VMEM)
SMEM = pl.BlockSpec(memory_space=pltpu.SMEM)
HBM = pl.BlockSpec(memory_space=pltpu.HBM)
PARAMS = pltpu.CompilerParams(vmem_limit_bytes=12 * 1024 * 1024)


def in_hbm(x):
    return pltpu.with_memory_space_constraint(x, pltpu.HBM)


def shape(dims, dtype=BF):
    return jax.ShapeDtypeStruct(tuple(dims), dtype)


def cost(flops, size):
    return pl.CostEstimate(flops=flops, bytes_accessed=size, transcendentals=0)


def swapped(block, axis, bits):
    route = [(i, i ^ bits) for i in range(lax.axis_size(axis))]
    return lax.ppermute(block, axis, route)


def from_behind(block, bits):
    sections, tensors = lax.axis_size("section"), lax.axis_size("tensor")
    route = [
        (s * tensors + (t ^ bits), (s + 1) % sections * tensors + t)
        for s in range(sections)
        for t in range(tensors)
    ]
    return lax.ppermute(block, ("section", "tensor"), route)


def tree_sum(pieces):
    pieces = [piece.astype(F32) for piece in pieces]
    while len(pieces) > 1:
        pieces = [pieces[i] + pieces[i + 1] for i in range(0, len(pieces), 2)]
    return pieces[0]


def batch_at(tick, sections):
    return lax.rem(lax.axis_index("section") + (sections - tick), sections)


def pack_kernel(dims, *refs):
    sections, tensors, rows, heads_dev, group, kv_dev = dims
    sources, refs = refs[:8], refs[8:]
    packs, (h_ref, next_ref, lengths_ref) = refs[:tensors], refs[tensors : tensors + 3]
    ids, lengths, gains, biases, keys, values, sems = refs[tensors + 3 :]
    held = 2 * sections * kv_dev
    targets = (ids, lengths, keys, values, gains, biases, h_ref, next_ref)
    copies = [
        pltpu.make_async_copy(source, target, sems.at[i])
        for i, (source, target) in enumerate(zip(sources, targets))
    ]
    quarter = gains.shape[1] // 4
    tables = [
        [
            pltpu.make_async_copy(
                sources[which].at[:, pl.ds(i * quarter, quarter)],
                targets[which].at[:, pl.ds(i * quarter, quarter)],
                sems.at[4 * (which - 2) + i],
            )
            for i in range(4)
        ]
        for which in (4, 5)
    ]
    for copy in copies[:2] + tables[0] + tables[1] + copies[2:4] + copies[6:]:
        copy.start()
    at = lax.axis_index("tensor")
    tenants = gains.shape[0]
    count = sections * rows
    spot = lax.broadcasted_iota(jnp.int32, (count, tenants), 0)
    line = lax.broadcasted_iota(jnp.int32, lengths_ref.shape, 0)
    wanted = jnp.zeros((count, tenants), jnp.int32)
    kept = jnp.zeros(lengths_ref.shape, jnp.int32)
    copies[0].wait()
    copies[1].wait()
    for tick in range(sections):
        batch = batch_at(tick, sections)
        kept = jnp.where(line == tick, lengths[batch], kept)
        for i in range(rows):
            wanted = jnp.where(spot == tick * rows + i, ids[batch, i], wanted)
    lengths_ref[...] = kept.astype(F32)
    wanted = wanted - at * tenants
    onehot = jnp.where(wanted == lax.broadcasted_iota(jnp.int32, (count, tenants), 1), 1.0, 0.0)
    onehot = onehot.astype(BF)
    copies[2].wait()
    copies[3].wait()
    pos, lanes = keys.shape[2:]
    width = gains.shape[1]
    per = pos // (2 * rows)
    blocks = width // lanes // per
    for d in range(tensors):
        start = lax.bitwise_xor(at, d) * heads_dev // group
        for which, cache in enumerate((keys, values)):
            for b in range(sections):
                for g in range(kv_dev):
                    to = (which * sections + b) * kv_dev + g
                    packs[d][to] = cache[b, start + g]
    for copy in tables[0]:
        copy.wait()
    gain_rows = jnp.dot(onehot, gains[...], preferred_element_type=F32)
    for copy in tables[1]:
        copy.wait()
    bias_rows = jnp.dot(onehot, biases[...], preferred_element_type=F32)
    for tick in range(sections):
        mine = slice(tick * rows, (tick + 1) * rows)
        both = jnp.concatenate([gain_rows[mine], bias_rows[mine]], 0)
        for j in range(blocks):
            block = jnp.concatenate(
                [both[:, (j * per + k) * lanes : (j * per + k + 1) * lanes] for k in range(per)], 0
            ).astype(BF)
            for d in range(tensors if tick == 0 else min(tensors, NEAR)):
                packs[d][held + tick * blocks + j] = block
    copies[6].wait()
    copies[7].wait()


def pack(dims, tenant, lengths, gain, bias, keys, values, h, following):
    sections, tensors, rows, heads_dev, group, kv_dev = dims
    pos = keys.shape[2]
    blocks = 2 * rows * gain.shape[1] // (pos * HD)
    held, later = 2 * sections * kv_dev, (sections - 1) * blocks
    out_shape = [
        shape((held + blocks + (later if d < NEAR else 0), pos, HD)) for d in range(tensors)
    ]
    out_shape += [shape(h.shape), shape(following.shape), shape((sections, HD), F32)]
    operands = (tenant, lengths, keys, values, gain, bias, h, following)
    return pl.pallas_call(
        lambda *refs: pack_kernel(dims, *refs),
        out_shape=out_shape,
        in_specs=[HBM] * len(operands),
        out_specs=[VMEM] * len(out_shape),
        scratch_shapes=[pltpu.SMEM(x.shape, jnp.int32) for x in (tenant, lengths)]
        + [pltpu.VMEM(x.shape, BF) for x in (gain, bias, keys, values)]
        + [pltpu.SemaphoreType.DMA((16,))],
        compiler_params=PARAMS,
        cost_estimate=cost(0, 4 * gain.size),
    )(*[in_hbm(x) for x in operands])


def join_kernel(count, size, refs):
    out_ref = refs[-1]
    for i in range(count):
        out_ref[i] = refs[i][:size]


def join(pieces, size, after):
    count = len(pieces)
    dims = pieces[0].shape
    return pl.pallas_call(
        lambda *refs: join_kernel(count, size, refs),
        out_shape=shape((count, size) + dims[1:]),
        in_specs=[VMEM] * count + [pl.BlockSpec(memory_space=pl.ANY)] * len(after),
        out_specs=VMEM,
        compiler_params=PARAMS,
    )(*pieces, *after)


def hold_kernel(parts, columns, after_ref, *refs):
    count = len(columns)
    copies = []
    sems = refs[-1]
    for source, target, (first, size) in zip(refs[:count], refs[count:-1], columns):
        rows = source.shape[0] // parts
        for i in range(parts):
            at = pl.ds(i * rows, rows)
            copies.append(
                pltpu.make_async_copy(
                    source.at[at, pl.ds(first, size)], target.at[at], sems.at[len(copies)]
                )
            )
    for copy in copies:
        copy.start()
    for copy in copies:
        copy.wait()


def hold(weights, columns, after):
    parts = 8
    total = sum(w.shape[0] * size for w, (_, size) in zip(weights, columns))
    return pl.pallas_call(
        lambda *refs: hold_kernel(parts, columns, *refs),
        out_shape=[pltpu.VMEM((w.shape[0], size), BF) for w, (_, size) in zip(weights, columns)],
        in_specs=[pl.BlockSpec(memory_space=pl.ANY)] + [HBM] * len(weights),
        out_specs=[VMEM] * len(weights),
        scratch_shapes=[pltpu.SemaphoreType.DMA((len(weights) * parts,))],
        compiler_params=PARAMS,
        cost_estimate=cost(0, 2 * total),
    )(after, *[in_hbm(w) for w in weights])


def tiles(w_ref):
    width = min(512, w_ref.shape[1])
    return [slice(i, i + width) for i in range(0, w_ref.shape[1], width)]


def thirds(x):
    high = x.astype(BF).astype(F32)
    middle = (x - high).astype(BF).astype(F32)
    return [high, middle, x - high - middle]


def query_sums(first_blocks, length, h, pieces, w_ref, out_ref):
    rows, width = h.shape
    pos, lanes = pieces[0].shape[1:]
    per = pos // (2 * rows)
    cols = []
    for j in range(width // lanes // per):
        block = tree_sum([piece[first + j] for first, piece in zip(first_blocks, pieces)])
        cols += [block[k * 2 * rows : (k + 1) * 2 * rows] for k in range(per)]
    affine = jnp.concatenate(cols, 1)
    total = jnp.sum(h, axis=-1, keepdims=True)
    squares = jnp.sum(h * h, axis=-1, keepdims=True)
    centred = (h - total * (1.0 / width)) * affine[:rows]
    x = jnp.concatenate([centred, affine], 0).astype(BF)
    count = w_ref.shape[1]
    for at in tiles(w_ref):
        got = jnp.dot(x, w_ref[:, at], preferred_element_type=F32)
        for k in range(3):
            to = slice(k * count + at.start, k * count + at.stop)
            out_ref[:, to] = got[k * rows : (k + 1) * rows].astype(BF)
    lane = lax.broadcasted_iota(jnp.int32, (rows, HD), 1)
    tail = jnp.broadcast_to(length, (rows, HD))
    for i, term in enumerate(thirds(total) + thirds(squares)):
        tail = jnp.where(lane == i, term, tail)
    out_ref[:, 3 * count :] = tail.astype(BF)


def first_kernel(tensors, held, lengths_ref, h_ref, *refs):
    pieces, (w_ref, out_ref) = refs[:tensors], refs[tensors:]
    query_sums([held] * tensors, lengths_ref[0:1], h_ref[...].astype(F32), pieces, w_ref, out_ref)


def first_sums(held, lengths, h, pieces, w):
    tensors = len(pieces)
    return pl.pallas_call(
        lambda *refs: first_kernel(tensors, held, *refs),
        out_shape=shape((h.shape[0], 3 * w.shape[1] + HD)),
        in_specs=[VMEM] * (tensors + 3),
        out_specs=VMEM,
        compiler_params=PARAMS,
        cost_estimate=cost(24 * w.size, 2 * w.size),
    )(lengths, h, *pieces, w)


def arrive(arrivals, following, tick):
    sections, rows, width = following.shape
    rest = arrivals[0][:, width:].astype(F32)
    section = jnp.full((rows, width), lax.axis_index("section"))
    left, carried = rest[:, :width], jnp.zeros((rows, width), F32)
    if sections == 2 and tick > 0:
        left = jnp.where(section == 1, following[-tick % sections].astype(F32), rest)
        carried = rest
    elif tick > 0:
        carried = rest[:, width:]
    came = tree_sum([arrival[:, :width] for arrival in arrivals]) + left
    came = came.astype(BF).astype(F32)
    h = jnp.where(section == 0, following[-(tick + 1) % sections].astype(F32), came)
    return h, jnp.where(section == 0, came, carried)


def later_kernel(count, tick, lengths_ref, *refs):
    arrivals, next_ref = refs[:count], refs[count]
    pieces, (w_ref, out_ref, carry_ref) = refs[count + 1 : -3], refs[-3:]
    h, emitted = arrive(arrivals, next_ref, tick - 1)
    width = h.shape[1]
    if carry_ref.shape[1] == width:
        first = jnp.full(h.shape, lax.axis_index("section")) == 0
        carry_ref[...] = jnp.where(first, emitted, h).astype(BF)
    else:
        carry_ref[:, :width] = h.astype(BF)
        carry_ref[:, width:] = emitted.astype(BF)
    blocks = 2 * h.shape[0] * width // (pieces[0].shape[1] * HD)
    query_sums([(tick - 1) * blocks] * len(pieces), lengths_ref[tick : tick + 1], h, pieces, w_ref, out_ref)


def later_sums(tick, lengths, arrivals, following, pieces, w):
    rows, width = following.shape[1:]
    parts = 1 if following.shape[0] == 2 else 2
    return pl.pallas_call(
        lambda *refs: later_kernel(len(arrivals), tick, *refs),
        out_shape=[shape((rows, 3 * w.shape[1] + HD)), shape((rows, width * parts))],
        in_specs=[VMEM] * (len(arrivals) + len(pieces) + 3),
        out_specs=[VMEM] * 2,
        compiler_params=PARAMS,
        cost_estimate=cost(24 * w.size, 2 * w.size),
    )(lengths, *arrivals, following, *pieces, w)


def last_kernel(count, *refs):
    state_ref, emitted_ref = refs[-2:]
    h, emitted = arrive(refs[:count], refs[count], refs[count].shape[0] - 1)
    state_ref[0] = h.astype(BF)
    emitted_ref[0] = emitted.astype(BF)


def last(arrivals, following):
    return pl.pallas_call(
        lambda *refs: last_kernel(len(arrivals), *refs),
        out_shape=[shape((1,) + following.shape[1:])] * 2,
        in_specs=[VMEM] * (len(arrivals) + 1),
        out_specs=[VMEM] * 2,
        compiler_params=PARAMS,
    )(*arrivals, following)


def attend_kernel(dims, turns, tick, *refs):
    sections, tensors, rows, kv_dev = dims
    count = len(turns)
    pieces, (carry_ref, *w_refs), refs = refs[:count], refs[count : count + 3], refs[count + 3 :]
    caches, (out_ref, full_ref) = refs[:-2], refs[-2:]
    each = caches[0].shape[0] // tensors
    span = w_refs[0].shape[0]
    half = w_refs[0].shape[1]
    width = 2 * half
    batch = batch_at(tick, sections)

    tails = [piece[:, 3 * span :].astype(F32) for piece in pieces]
    totals = [tail[:, 0:1] + tail[:, 1:2] + tail[:, 2:3] for tail in tails]
    squares = [tail[:, 3:4] + tail[:, 4:5] + tail[:, 5:6] for tail in tails]
    scale = 1.0 / (width * count)
    mean = tree_sum(totals) * scale
    rstd = lax.rsqrt(tree_sum(squares) * scale - mean * mean + 1e-05)
    query = tree_sum(
        [
            piece[:, :span].astype(F32)
            + (total * (1.0 / width) - mean) * piece[:, span : 2 * span].astype(F32)
            for piece, total in zip(pieces, totals)
        ]
    )
    query = rstd * query + tree_sum([piece[:, 2 * span : 3 * span] for piece in pieces])
    query = query.astype(BF).astype(F32)

    pos = caches[0].shape[2]
    tensor_at, replica_at = lax.axis_index("tensor"), lax.axis_index("replica")
    cols = lax.broadcasted_iota(jnp.int32, (rows, tensors * pos), 1)
    row = lax.broadcasted_iota(jnp.int32, (rows, tensors * pos), 0)
    spots = jnp.bitwise_xor(cols // pos, tensor_at) * pos + cols % pos
    spots = spots.astype(F32)
    keep = []
    for turn in turns:
        valid = jnp.logical_and(row == jnp.bitwise_xor(replica_at, turn), spots < tails[turn][:, 6:7])
        keep.append(jnp.where(valid, 0.0, -1e30))
    per_kv = span // HD // kv_dev
    keep = jnp.concatenate([jnp.concatenate(keep, 1)] * per_kv, 0)

    att = []
    for g in range(kv_dev):
        mine = jnp.concatenate(
            [query[:, h * HD : (h + 1) * HD] for h in range(g * per_kv, (g + 1) * per_kv)], 0
        ).astype(BF)
        keys, values = (
            jnp.concatenate(
                [
                    cache[i, (which * sections + batch) * kv_dev + g]
                    for cache in caches
                    for i in range(each * tensors)
                ],
                0,
            )
            for which in range(2)
        )
        scores = lax.dot_general(mine, keys, (((1,), (1,)), ((), ())), preferred_element_type=F32)
        scores = scores * (HD**-0.5) + keep
        probs = jnp.exp(scores - jnp.max(scores, axis=-1, keepdims=True))
        total = jnp.sum(probs, axis=-1, keepdims=True)
        got = jnp.dot(probs.astype(BF), values, preferred_element_type=F32) / total
        att += [got[h * rows : (h + 1) * rows] for h in range(per_kv)]
    att = jnp.concatenate(att, 1).astype(BF)
    for i, w_ref in enumerate(w_refs):
        for at in tiles(w_ref):
            got = jnp.dot(att, w_ref[:, at], preferred_element_type=F32).astype(BF)
            to = slice(i * half + at.start, i * half + at.stop)
            out_ref[:, to] = got
            full_ref[:, to] = got
    full_ref[:, width:] = carry_ref[...]


def attend(dims, turns, tick, pieces, caches, carry, left, right):
    rows, width = carry.shape[0], left.shape[1] + right.shape[1]
    return pl.pallas_call(
        lambda *refs: attend_kernel(dims, turns, tick, *refs),
        out_shape=[shape((rows, width)), shape((rows, width + carry.shape[1]))],
        in_specs=[VMEM] * (len(pieces) + len(caches) + 3),
        out_specs=[VMEM] * 2,
        compiler_params=PARAMS,
        cost_estimate=cost(16 * left.size, 4 * left.size),
    )(*pieces, carry, left, right, *caches)


def on_device(state, next_embed, tenant, lengths, gain, bias, wq, wo, keys, values):
    sections = lax.axis_size("section")
    tensors = lax.axis_size("tensor")
    replicas = lax.axis_size("replica")
    rows, width = state.shape[1:]
    heads_dev = wq.shape[2] // HD
    group = heads_dev * tensors // keys.shape[3]
    kv_dev = max(1, heads_dev // group)
    dims = (sections, tensors, rows, heads_dev, group, kv_dev)

    *packs, carry, following, lengths = pack(
        dims,
        tenant,
        lengths.reshape(-1),
        gain[0],
        bias[0],
        keys[0, :, 0],
        values[0, :, 0],
        state[0],
        next_embed,
    )
    got = [packs[0]] + [swapped(packs[d], "tensor", d) for d in range(1, tensors)]
    half = width // 2
    wq_held, wo_left = hold([wq[0], wo[0]], [(0, wq.shape[2]), (0, half)], packs[0])

    held = 2 * sections * kv_dev
    kv = join(got, held, [wq_held, wo_left])

    later = [piece[held + 2 * rows * width // (keys.shape[4] * HD) :] for piece in got[:NEAR]]
    bit = NEAR
    while bit < tensors:
        later = [sum(later)]
        later = later + [swapped(later[0], "tensor", bit)]
        bit *= 2
    turns, bit = [0], replicas // 2
    caches, waiting = [kv], None
    if bit:
        waiting = swapped(kv, "replica", bit)
    arrivals = None
    for tick in range(sections):
        if tick == 0:
            sums = first_sums(held, lengths, carry, got, wq_held)
        else:
            sums, carry = later_sums(tick, lengths, arrivals, following, later, wq_held)
        pieces = [sums] + [swapped(sums, "replica", d) for d in range(1, replicas)]
        if tick == 0:
            (wo_right,) = hold([wo[0]], [(half, half)], sums)
            while bit:
                turns = turns + [turn ^ bit for turn in turns]
                caches, bit = [kv, waiting], bit // 2
                if bit:
                    both = join(caches, kv.shape[0], pieces[2:] + [wo_right])
                    kv = both.reshape((-1,) + both.shape[2:])
                    waiting = swapped(kv, "replica", bit)
        out, full = attend(
            (sections, tensors, rows, kv_dev), turns, tick, pieces, caches, carry, wo_left, wo_right
        )
        arrivals = [from_behind(full, 0)] + [from_behind(out, d) for d in range(1, tensors)]
    return tuple(last(arrivals, following))


def solution(mesh):
    in_specs = (
        P("section", None, "replica"),
        P(None, None, "replica"),
        P(),
        P(None, "replica"),
        P("section", "tensor", "replica"),
        P("section", "tensor", "replica"),
        P("section", "replica", "tensor"),
        P("section", "tensor", "replica"),
        P("section", None, "replica", None, "tensor", None),
        P("section", None, "replica", None, "tensor", None),
    )
    out_specs = (P("section", None, "replica"), P("section", None, "replica"))
    return jax.shard_map(
        on_device, mesh=mesh, in_specs=in_specs, out_specs=out_specs, check_vma=False
    )
```

```python
import jax
import jax.numpy as jnp
from jax import lax
from jax.experimental import pallas as pl
from jax.experimental.pallas import tpu as pltpu
from jax.sharding import PartitionSpec as P

HD = 128
NEAR = 2
BF = jnp.bfloat16
F32 = jnp.float32
VMEM = pl.BlockSpec(memory_space=pltpu.VMEM)
SMEM = pl.BlockSpec(memory_space=pltpu.SMEM)
HBM = pl.BlockSpec(memory_space=pltpu.HBM)
PARAMS = pltpu.CompilerParams(vmem_limit_bytes=12 * 1024 * 1024)


def in_hbm(x):
    return pltpu.with_memory_space_constraint(x, pltpu.HBM)


def shape(dims, dtype=BF):
    return jax.ShapeDtypeStruct(tuple(dims), dtype)


def cost(flops, size):
    return pl.CostEstimate(flops=flops, bytes_accessed=size, transcendentals=0)


def swapped(block, axis, bits):
    route = [(i, i ^ bits) for i in range(lax.axis_size(axis))]
    return lax.ppermute(block, axis, route)


def from_behind(block, bits):
    sections, tensors = lax.axis_size("section"), lax.axis_size("tensor")
    route = [
        (s * tensors + (t ^ bits), (s + 1) % sections * tensors + t)
        for s in range(sections)
        for t in range(tensors)
    ]
    return lax.ppermute(block, ("section", "tensor"), route)


def tree_sum(pieces):
    pieces = [piece.astype(F32) for piece in pieces]
    while len(pieces) > 1:
        pieces = [pieces[i] + pieces[i + 1] for i in range(0, len(pieces), 2)]
    return pieces[0]


def batch_at(tick, sections):
    return lax.rem(lax.axis_index("section") + (sections - tick), sections)


def pack_kernel(dims, *refs):
    sections, tensors, rows, heads_dev, group, kv_dev = dims
    sources, refs = refs[:8], refs[8:]
    packs, (h_ref, next_ref, lengths_ref) = refs[:tensors], refs[tensors : tensors + 3]
    ids, lengths, gains, biases, keys, values, sems = refs[tensors + 3 :]
    held = 2 * sections * kv_dev
    targets = (ids, lengths, keys, values, gains, biases, h_ref, next_ref)
    copies = [
        pltpu.make_async_copy(source, target, sems.at[i])
        for i, (source, target) in enumerate(zip(sources, targets))
    ]
    for copy in copies:
        copy.start()
    at = lax.axis_index("tensor")
    tenants = gains.shape[0]
    count = sections * rows
    spot = lax.broadcasted_iota(jnp.int32, (count, tenants), 0)
    line = lax.broadcasted_iota(jnp.int32, lengths_ref.shape, 0)
    wanted = jnp.zeros((count, tenants), jnp.int32)
    kept = jnp.zeros(lengths_ref.shape, jnp.int32)
    copies[0].wait()
    copies[1].wait()
    for tick in range(sections):
        batch = batch_at(tick, sections)
        kept = jnp.where(line == tick, lengths[batch], kept)
        for i in range(rows):
            wanted = jnp.where(spot == tick * rows + i, ids[batch, i], wanted)
    lengths_ref[...] = kept.astype(F32)
    wanted = wanted - at * tenants
    onehot = jnp.where(wanted == lax.broadcasted_iota(jnp.int32, (count, tenants), 1), 1.0, 0.0)
    onehot = onehot.astype(BF)
    copies[2].wait()
    copies[3].wait()
    pos, lanes = keys.shape[2:]
    width = gains.shape[1]
    per = pos // (2 * rows)
    blocks = width // lanes // per
    for d in range(tensors):
        start = lax.bitwise_xor(at, d) * heads_dev // group
        for which, cache in enumerate((keys, values)):
            for b in range(sections):
                for g in range(kv_dev):
                    to = (which * sections + b) * kv_dev + g
                    packs[d][to] = cache[b, start + g]
    copies[4].wait()
    gain_rows = jnp.dot(onehot, gains[...], preferred_element_type=F32)
    copies[5].wait()
    bias_rows = jnp.dot(onehot, biases[...], preferred_element_type=F32)
    for tick in range(sections):
        mine = slice(tick * rows, (tick + 1) * rows)
        both = jnp.concatenate([gain_rows[mine], bias_rows[mine]], 0)
        for j in range(blocks):
            block = jnp.concatenate(
                [both[:, (j * per + k) * lanes : (j * per + k + 1) * lanes] for k in range(per)], 0
            ).astype(BF)
            for d in range(tensors if tick == 0 else min(tensors, NEAR)):
                packs[d][held + tick * blocks + j] = block
    copies[6].wait()
    copies[7].wait()


def pack(dims, tenant, lengths, gain, bias, keys, values, h, following):
    sections, tensors, rows, heads_dev, group, kv_dev = dims
    pos = keys.shape[2]
    blocks = 2 * rows * gain.shape[1] // (pos * HD)
    held, later = 2 * sections * kv_dev, (sections - 1) * blocks
    out_shape = [
        shape((held + blocks + (later if d < NEAR else 0), pos, HD)) for d in range(tensors)
    ]
    out_shape += [shape(h.shape), shape(following.shape), shape((sections, HD), F32)]
    operands = (tenant, lengths, keys, values, gain, bias, h, following)
    return pl.pallas_call(
        lambda *refs: pack_kernel(dims, *refs),
        out_shape=out_shape,
        in_specs=[HBM] * len(operands),
        out_specs=[VMEM] * len(out_shape),
        scratch_shapes=[pltpu.SMEM(x.shape, jnp.int32) for x in (tenant, lengths)]
        + [pltpu.VMEM(x.shape, BF) for x in (gain, bias, keys, values)]
        + [pltpu.SemaphoreType.DMA((len(operands),))],
        compiler_params=PARAMS,
        cost_estimate=cost(0, 4 * gain.size),
    )(*[in_hbm(x) for x in operands])


def join_kernel(count, size, refs):
    out_ref = refs[-1]
    for i in range(count):
        out_ref[i] = refs[i][:size]


def join(pieces, size, after):
    count = len(pieces)
    dims = pieces[0].shape
    return pl.pallas_call(
        lambda *refs: join_kernel(count, size, refs),
        out_shape=shape((count, size) + dims[1:]),
        in_specs=[VMEM] * count + [pl.BlockSpec(memory_space=pl.ANY)] * len(after),
        out_specs=VMEM,
        compiler_params=PARAMS,
    )(*pieces, *after)


def hold_kernel(parts, columns, after_ref, *refs):
    count = len(columns)
    copies = []
    sems = refs[-1]
    for source, target, (first, size) in zip(refs[:count], refs[count:-1], columns):
        rows = source.shape[0] // parts
        for i in range(parts):
            at = pl.ds(i * rows, rows)
            copies.append(
                pltpu.make_async_copy(
                    source.at[at, pl.ds(first, size)], target.at[at], sems.at[len(copies)]
                )
            )
    for copy in copies:
        copy.start()
    for copy in copies:
        copy.wait()


def hold(weights, columns, after):
    parts = 8
    total = sum(w.shape[0] * size for w, (_, size) in zip(weights, columns))
    return pl.pallas_call(
        lambda *refs: hold_kernel(parts, columns, *refs),
        out_shape=[pltpu.VMEM((w.shape[0], size), BF) for w, (_, size) in zip(weights, columns)],
        in_specs=[pl.BlockSpec(memory_space=pl.ANY)] + [HBM] * len(weights),
        out_specs=[VMEM] * len(weights),
        scratch_shapes=[pltpu.SemaphoreType.DMA((len(weights) * parts,))],
        compiler_params=PARAMS,
        cost_estimate=cost(0, 2 * total),
    )(after, *[in_hbm(w) for w in weights])


def tiles(w_ref):
    width = min(512, w_ref.shape[1])
    return [slice(i, i + width) for i in range(0, w_ref.shape[1], width)]


def thirds(x):
    high = x.astype(BF).astype(F32)
    middle = (x - high).astype(BF).astype(F32)
    return [high, middle, x - high - middle]


def query_sums(first_blocks, length, h, pieces, w_ref, out_ref):
    rows, width = h.shape
    pos, lanes = pieces[0].shape[1:]
    per = pos // (2 * rows)
    cols = []
    for j in range(width // lanes // per):
        block = tree_sum([piece[first + j] for first, piece in zip(first_blocks, pieces)])
        cols += [block[k * 2 * rows : (k + 1) * 2 * rows] for k in range(per)]
    affine = jnp.concatenate(cols, 1)
    total = jnp.sum(h, axis=-1, keepdims=True)
    squares = jnp.sum(h * h, axis=-1, keepdims=True)
    centred = (h - total * (1.0 / width)) * affine[:rows]
    x = jnp.concatenate([centred, affine], 0).astype(BF)
    count = w_ref.shape[1]
    for at in tiles(w_ref):
        got = jnp.dot(x, w_ref[:, at], preferred_element_type=F32)
        for k in range(3):
            to = slice(k * count + at.start, k * count + at.stop)
            out_ref[:, to] = got[k * rows : (k + 1) * rows].astype(BF)
    lane = lax.broadcasted_iota(jnp.int32, (rows, HD), 1)
    tail = jnp.broadcast_to(length, (rows, HD))
    for i, term in enumerate(thirds(total) + thirds(squares)):
        tail = jnp.where(lane == i, term, tail)
    out_ref[:, 3 * count :] = tail.astype(BF)


def first_kernel(tensors, held, lengths_ref, h_ref, *refs):
    pieces, (w_ref, out_ref) = refs[:tensors], refs[tensors:]
    query_sums([held] * tensors, lengths_ref[0:1], h_ref[...].astype(F32), pieces, w_ref, out_ref)


def first_sums(held, lengths, h, pieces, w):
    tensors = len(pieces)
    return pl.pallas_call(
        lambda *refs: first_kernel(tensors, held, *refs),
        out_shape=shape((h.shape[0], 3 * w.shape[1] + HD)),
        in_specs=[VMEM] * (tensors + 3),
        out_specs=VMEM,
        compiler_params=PARAMS,
        cost_estimate=cost(24 * w.size, 2 * w.size),
    )(lengths, h, *pieces, w)


def arrive(arrivals, following, tick):
    sections, rows, width = following.shape
    rest = arrivals[0][:, width:].astype(F32)
    section = jnp.full((rows, width), lax.axis_index("section"))
    left, carried = rest[:, :width], jnp.zeros((rows, width), F32)
    if sections == 2 and tick > 0:
        left = jnp.where(section == 1, following[-tick % sections].astype(F32), rest)
        carried = rest
    elif tick > 0:
        carried = rest[:, width:]
    came = tree_sum([arrival[:, :width] for arrival in arrivals]) + left
    came = came.astype(BF).astype(F32)
    h = jnp.where(section == 0, following[-(tick + 1) % sections].astype(F32), came)
    return h, jnp.where(section == 0, came, carried)


def later_kernel(count, tick, lengths_ref, *refs):
    arrivals, next_ref = refs[:count], refs[count]
    pieces, (w_ref, out_ref, carry_ref) = refs[count + 1 : -3], refs[-3:]
    h, emitted = arrive(arrivals, next_ref, tick - 1)
    width = h.shape[1]
    if carry_ref.shape[1] == width:
        first = jnp.full(h.shape, lax.axis_index("section")) == 0
        carry_ref[...] = jnp.where(first, emitted, h).astype(BF)
    else:
        carry_ref[:, :width] = h.astype(BF)
        carry_ref[:, width:] = emitted.astype(BF)
    blocks = 2 * h.shape[0] * width // (pieces[0].shape[1] * HD)
    query_sums([(tick - 1) * blocks] * len(pieces), lengths_ref[tick : tick + 1], h, pieces, w_ref, out_ref)


def later_sums(tick, lengths, arrivals, following, pieces, w):
    rows, width = following.shape[1:]
    parts = 1 if following.shape[0] == 2 else 2
    return pl.pallas_call(
        lambda *refs: later_kernel(len(arrivals), tick, *refs),
        out_shape=[shape((rows, 3 * w.shape[1] + HD)), shape((rows, width * parts))],
        in_specs=[VMEM] * (len(arrivals) + len(pieces) + 3),
        out_specs=[VMEM] * 2,
        compiler_params=PARAMS,
        cost_estimate=cost(24 * w.size, 2 * w.size),
    )(lengths, *arrivals, following, *pieces, w)


def last_kernel(count, *refs):
    state_ref, emitted_ref = refs[-2:]
    h, emitted = arrive(refs[:count], refs[count], refs[count].shape[0] - 1)
    state_ref[0] = h.astype(BF)
    emitted_ref[0] = emitted.astype(BF)


def last(arrivals, following):
    return pl.pallas_call(
        lambda *refs: last_kernel(len(arrivals), *refs),
        out_shape=[shape((1,) + following.shape[1:])] * 2,
        in_specs=[VMEM] * (len(arrivals) + 1),
        out_specs=[VMEM] * 2,
        compiler_params=PARAMS,
    )(*arrivals, following)


def attend_kernel(dims, turns, tick, *refs):
    sections, tensors, rows, kv_dev = dims
    count = len(turns)
    pieces, (carry_ref, *w_refs), refs = refs[:count], refs[count : count + 3], refs[count + 3 :]
    caches, (out_ref, full_ref) = refs[:-2], refs[-2:]
    each = caches[0].shape[0] // tensors
    span = w_refs[0].shape[0]
    half = w_refs[0].shape[1]
    width = 2 * half
    batch = batch_at(tick, sections)

    tails = [piece[:, 3 * span :].astype(F32) for piece in pieces]
    totals = [tail[:, 0:1] + tail[:, 1:2] + tail[:, 2:3] for tail in tails]
    squares = [tail[:, 3:4] + tail[:, 4:5] + tail[:, 5:6] for tail in tails]
    scale = 1.0 / (width * count)
    mean = tree_sum(totals) * scale
    rstd = lax.rsqrt(tree_sum(squares) * scale - mean * mean + 1e-05)
    query = tree_sum(
        [
            piece[:, :span].astype(F32)
            + (total * (1.0 / width) - mean) * piece[:, span : 2 * span].astype(F32)
            for piece, total in zip(pieces, totals)
        ]
    )
    query = rstd * query + tree_sum([piece[:, 2 * span : 3 * span] for piece in pieces])
    query = query.astype(BF).astype(F32)

    pos = caches[0].shape[2]
    tensor_at, replica_at = lax.axis_index("tensor"), lax.axis_index("replica")
    cols = lax.broadcasted_iota(jnp.int32, (rows, tensors * pos), 1)
    row = lax.broadcasted_iota(jnp.int32, (rows, tensors * pos), 0)
    spots = jnp.bitwise_xor(cols // pos, tensor_at) * pos + cols % pos
    spots = spots.astype(F32)
    keep = []
    for turn in turns:
        valid = jnp.logical_and(row == jnp.bitwise_xor(replica_at, turn), spots < tails[turn][:, 6:7])
        keep.append(jnp.where(valid, 0.0, -1e30))
    per_kv = span // HD // kv_dev
    keep = jnp.concatenate([jnp.concatenate(keep, 1)] * per_kv, 0)

    att = []
    for g in range(kv_dev):
        mine = jnp.concatenate(
            [query[:, h * HD : (h + 1) * HD] for h in range(g * per_kv, (g + 1) * per_kv)], 0
        ).astype(BF)
        keys, values = (
            jnp.concatenate(
                [
                    cache[i, (which * sections + batch) * kv_dev + g]
                    for cache in caches
                    for i in range(each * tensors)
                ],
                0,
            )
            for which in range(2)
        )
        scores = lax.dot_general(mine, keys, (((1,), (1,)), ((), ())), preferred_element_type=F32)
        scores = scores * (HD**-0.5) + keep
        probs = jnp.exp(scores - jnp.max(scores, axis=-1, keepdims=True))
        total = jnp.sum(probs, axis=-1, keepdims=True)
        got = jnp.dot(probs.astype(BF), values, preferred_element_type=F32) / total
        att += [got[h * rows : (h + 1) * rows] for h in range(per_kv)]
    att = jnp.concatenate(att, 1).astype(BF)
    for i, w_ref in enumerate(w_refs):
        for at in tiles(w_ref):
            got = jnp.dot(att, w_ref[:, at], preferred_element_type=F32).astype(BF)
            to = slice(i * half + at.start, i * half + at.stop)
            out_ref[:, to] = got
            full_ref[:, to] = got
    full_ref[:, width:] = carry_ref[...]


def attend(dims, turns, tick, pieces, caches, carry, left, right):
    rows, width = carry.shape[0], left.shape[1] + right.shape[1]
    return pl.pallas_call(
        lambda *refs: attend_kernel(dims, turns, tick, *refs),
        out_shape=[shape((rows, width)), shape((rows, width + carry.shape[1]))],
        in_specs=[VMEM] * (len(pieces) + len(caches) + 3),
        out_specs=[VMEM] * 2,
        compiler_params=PARAMS,
        cost_estimate=cost(16 * left.size, 4 * left.size),
    )(*pieces, carry, left, right, *caches)


def on_device(state, next_embed, tenant, lengths, gain, bias, wq, wo, keys, values):
    sections = lax.axis_size("section")
    tensors = lax.axis_size("tensor")
    replicas = lax.axis_size("replica")
    rows, width = state.shape[1:]
    heads_dev = wq.shape[2] // HD
    group = heads_dev * tensors // keys.shape[3]
    kv_dev = max(1, heads_dev // group)
    dims = (sections, tensors, rows, heads_dev, group, kv_dev)

    *packs, carry, following, lengths = pack(
        dims,
        tenant,
        lengths.reshape(-1),
        gain[0],
        bias[0],
        keys[0, :, 0],
        values[0, :, 0],
        state[0],
        next_embed,
    )
    got = [packs[0]] + [swapped(packs[d], "tensor", d) for d in range(1, tensors)]
    half = width // 2
    wq_held, wo_left = hold([wq[0], wo[0]], [(0, wq.shape[2]), (0, half)], packs[0])

    held = 2 * sections * kv_dev
    kv = join(got, held, [wq_held, wo_left])

    later = [piece[held + 2 * rows * width // (keys.shape[4] * HD) :] for piece in got[:NEAR]]
    bit = NEAR
    while bit < tensors:
        later = [sum(later)]
        later = later + [swapped(later[0], "tensor", bit)]
        bit *= 2
    turns, bit = [0], replicas // 2
    caches, waiting = [kv], None
    if bit:
        waiting = swapped(kv, "replica", bit)
    arrivals = None
    for tick in range(sections):
        if tick == 0:
            sums = first_sums(held, lengths, carry, got, wq_held)
        else:
            sums, carry = later_sums(tick, lengths, arrivals, following, later, wq_held)
        pieces = [sums] + [swapped(sums, "replica", d) for d in range(1, replicas)]
        if tick == 0:
            (wo_right,) = hold([wo[0]], [(half, half)], sums)
            while bit:
                turns = turns + [turn ^ bit for turn in turns]
                caches, bit = [kv, waiting], bit // 2
                if bit:
                    both = join(caches, kv.shape[0], pieces[1:] + [wo_right])
                    kv = both.reshape((-1,) + both.shape[2:])
                    waiting = swapped(kv, "replica", bit)
        out, full = attend(
            (sections, tensors, rows, kv_dev), turns, tick, pieces, caches, carry, wo_left, wo_right
        )
        arrivals = [from_behind(full, 0)] + [from_behind(out, d) for d in range(1, tensors)]
    return tuple(last(arrivals, following))


def solution(mesh):
    in_specs = (
        P("section", None, "replica"),
        P(None, None, "replica"),
        P(),
        P(None, "replica"),
        P("section", "tensor", "replica"),
        P("section", "tensor", "replica"),
        P("section", "replica", "tensor"),
        P("section", "tensor", "replica"),
        P("section", None, "replica", None, "tensor", None),
        P("section", None, "replica", None, "tensor", None),
    )
    out_specs = (P("section", None, "replica"), P("section", None, "replica"))
    return jax.shard_map(
        on_device, mesh=mesh, in_specs=in_specs, out_specs=out_specs, check_vma=False
    )
```
